256 devices in a mesh: seq: 64 (over z, y_lo, x), head: 4 (over y_hi, core).
Axes of the slice: x: 4, y: 4 (y_hi: 2, y_lo: 2; y = y_hi * 2 + y_lo), z: 8, core: 2. Of those that a mesh axis runs over, the one named last changes fastest.
Arguments:
- tokens: bfloat16 [32768, 1152], P('seq', 'head'), may hold values from -6 to 6
- cotangent: bfloat16 [32768, 1152], P('seq', 'head'), may hold values from -6 to 6
- qkv_weight: bfloat16 [2, 1152, 3, 1152], P(None, None, None, 'head'), may hold values from -0.14583333 to 0.14583333
- out_weight: bfloat16 [2, 1152, 1152], P(None, 'head'), may hold values from -0.1875 to 0.1875
- modulation: float32 [2, 3, 1152], replicated, may hold values from -3 to 3
- head_gains: float32 [2, 2, 72], replicated, may hold values from 1.2 to 2.2
Outputs:
- mixed: bfloat16 [32768, 1152], P('seq', 'head')
- grad_tokens: bfloat16 [32768, 1152], P('seq', 'head')
The draws below stay inside these ranges and needn't reach their ends.
All inputs are finite; a program needn't handle non-finite values.
Results may differ from the reference program's by a relative error of at most 0.025.
Values may be sent and summed in bfloat16 or wider, within the bound.
No kernel may reach another device: no remote copies, remote signals or barrier semaphores. Data moves between devices by JAX's collectives and lax.ppermute only.
A program may use at most 128 MiB of HBM per device.

```python
import jax
import jax.numpy as jnp
from jax import lax

HEADS = 16
HEAD_DIM = 72
D = 1152
P_SIZE = 512
FRAMES = 64
TOKENS = 32768
N_HEAD = 4


def draw_qkv_weight(key, part):
    key = jax.random.fold_in(key, 11)
    key_rows, key_cols = jax.random.split(key)
    noise = jnp.clip(jax.random.normal(key_rows, (2, D, 3, D), jnp.float32), -4.0, 4.0)
    common = jnp.clip(jax.random.normal(key_cols, (2, 1, 3, D), jnp.float32), -3.0, 3.0)
    return ((noise + common) / jnp.sqrt(2.0 * D)).astype(jnp.bfloat16)


def draw_modulation(key, part):
    key = jax.random.fold_in(key, 23)
    key_shift, key_scale, key_gate = jax.random.split(key, 3)
    place = jnp.arange(D, dtype=jnp.float32) / (D - 1)
    ramp = 0.5 + place
    factor = jnp.exp(jax.random.uniform(key_scale, (2, D), jnp.float32, jnp.log(0.7), jnp.log(1.4)))
    scale_part = ramp[None, :] * factor - 1.0
    shift_part = jnp.clip(0.8 * jax.random.normal(key_shift, (2, D), jnp.float32), -3.0, 3.0)
    gate_part = jnp.clip(0.8 * jax.random.normal(key_gate, (2, D), jnp.float32), -3.0, 3.0)
    return jnp.stack([shift_part, scale_part, gate_part], axis=1)


def block_levels(rng, dims, shards, smallest, high):
    def one(axis_at, shards_of):
        steps = jax.random.uniform(jax.random.fold_in(jax.random.fold_in(rng, 6), axis_at), (shards_of,), jnp.float32, smallest / len(shards), high / len(shards))
        return jnp.repeat(jnp.exp(steps), dims[axis_at] // shards_of).reshape((-1,) + (1,) * (len(dims) - axis_at - 1))

    loudness = one(*shards[0])
    for cut in shards[1:]:
        loudness = loudness * one(*cut)
    return loudness


def gaussian(rng, extent, width, most, cuts=(), kind=jnp.bfloat16):
    drawn = width * jax.random.normal(rng, extent, jnp.float32)
    if cuts:
        drawn = drawn * block_levels(rng, extent, cuts, -0.22, 0.18)
    return jnp.clip(drawn, -most, most).astype(kind)


def setup_inputs(seed: int = 0) -> dict:
    seeds = jax.random.split(jax.random.key(seed), 7)
    tokens = gaussian(seeds[0], (TOKENS, D), 1.0, 6.0, ((0, 64), (1, 4)))
    cotangent = gaussian(seeds[1], (TOKENS, D), 1.0, 6.0, ((0, 64), (1, 4)))
    qkv_weight = draw_qkv_weight(jax.random.fold_in(seeds[6], 71), 0)
    out_weight = gaussian(seeds[3], (2, D, D), D ** -0.5, 0.1875, ((1, 4),))
    modulation = draw_modulation(jax.random.fold_in(seeds[6], 71), 0)
    head_gains = jnp.clip(jax.random.uniform(seeds[5], (2, 2, HEAD_DIM), jnp.float32, 1.2, 2.2), 1.2, 2.2)
    return dict(tokens=tokens, cotangent=cotangent, qkv_weight=qkv_weight, out_weight=out_weight, modulation=modulation, head_gains=head_gains)


EPS = 1e-06

def round_sum(running, addend):
    rounded = lax.optimization_barrier(addend.astype(jnp.bfloat16))
    return running + rounded.astype(jnp.float32)

def head_norm(values, gains):
    inverse = lax.rsqrt(lax.optimization_barrier(jnp.mean(values * values, axis=-1, keepdims=True)) + EPS)
    return ((values * inverse * gains).astype(jnp.bfloat16), inverse)

def head_back(incoming, normed, inverse, gains):
    grad_f = incoming.astype(jnp.float32)
    norm_f = normed.astype(jnp.float32)
    inner = lax.optimization_barrier(jnp.mean(norm_f * grad_f, axis=-1, keepdims=True))
    return (inverse * (gains * grad_f - norm_f / gains * inner)).astype(jnp.bfloat16)

def scores_of(queries, keys):
    scaling = queries.shape[-1] ** (-0.5)
    return jnp.einsum('lhc,mhc->hlm', queries.astype(jnp.float32), keys.astype(jnp.float32)) * scaling

def attend_group(operands):
    queries, keys, values = operands
    unnormed = jnp.exp(scores_of(queries, keys))
    weights = (unnormed / lax.optimization_barrier(jnp.sum(unnormed, axis=-1, keepdims=True))).astype(jnp.bfloat16)
    return jnp.einsum('hlm,mhc->lhc', weights.astype(jnp.float32), values.astype(jnp.float32)).astype(jnp.bfloat16)

def attend_back_group(operands):
    queries, keys, values, incoming = operands
    scaling = queries.shape[-1] ** (-0.5)
    unnormed = jnp.exp(scores_of(queries, keys))
    probs = unnormed / lax.optimization_barrier(jnp.sum(unnormed, axis=-1, keepdims=True))
    weights = probs.astype(jnp.bfloat16)
    grad_in = incoming.astype(jnp.float32)
    grad_probs = jnp.einsum('lhc,mhc->hlm', grad_in, values.astype(jnp.float32))
    grad_values = jnp.einsum('hlm,lhc->mhc', weights.astype(jnp.float32), grad_in).astype(jnp.bfloat16)
    grad_scores = (probs * (grad_probs - lax.optimization_barrier(jnp.sum(grad_probs * probs, axis=-1, keepdims=True)))).astype(jnp.bfloat16)
    grad_queries = (scaling * jnp.einsum('hlm,mhc->lhc', grad_scores.astype(jnp.float32), keys.astype(jnp.float32))).astype(jnp.bfloat16)
    grad_keys = (scaling * jnp.einsum('hlm,lhc->mhc', grad_scores.astype(jnp.float32), queries.astype(jnp.float32))).astype(jnp.bfloat16)
    return (grad_queries, grad_keys, grad_values)

def arrange(values, spatial):
    grouped = values.reshape(FRAMES, P_SIZE, HEADS, HEAD_DIM)
    return grouped if spatial else jnp.swapaxes(grouped, 0, 1)

def restore(values, spatial):
    ordered = values if spatial else jnp.swapaxes(values, 0, 1)
    return ordered.reshape(FRAMES * P_SIZE, HEADS, HEAD_DIM)

def forward(stream, weights_in, weights_out, modulation, gains, spatial):
    stream_f = stream.astype(jnp.float32)
    row_mean = lax.optimization_barrier(jnp.mean(stream_f, axis=-1, keepdims=True))
    centred = stream_f - row_mean
    inverse = lax.rsqrt(lax.optimization_barrier(jnp.mean(centred * centred, axis=-1, keepdims=True)) + EPS)
    normed = (centred * inverse * (1.0 + modulation[1]) + modulation[0]).astype(jnp.bfloat16)
    projected = jnp.dot(normed, weights_in.reshape(D, 3 * D), preferred_element_type=jnp.float32)
    projected = projected.reshape(-1, 3, HEADS, HEAD_DIM)
    queries, query_inv = head_norm(projected[:, 0], gains[0])
    keys, key_inv = head_norm(projected[:, 1], gains[1])
    values = projected[:, 2].astype(jnp.bfloat16)
    grouped = lax.map(attend_group, (arrange(queries, spatial), arrange(keys, spatial), arrange(values, spatial)))
    attended = restore(grouped, spatial).reshape(-1, D)
    group_width = D // N_HEAD
    branch = jnp.zeros(stream.shape, jnp.float32)
    for head_group in range(N_HEAD):
        lower = head_group * group_width
        addend = jnp.dot(attended[:, lower:lower + group_width], weights_out[lower:lower + group_width], preferred_element_type=jnp.float32)
        branch = round_sum(branch, addend)
    output = (stream_f + modulation[2] * branch).astype(jnp.bfloat16)
    return (output, (row_mean, inverse, queries, keys, values, query_inv, key_inv))

def backward(incoming, stream, weights_in, weights_out, modulation, gains, stored, spatial):
    row_mean, inverse, queries, keys, values, query_inv, key_inv = stored
    grad_branch = (modulation[2] * incoming.astype(jnp.float32)).astype(jnp.bfloat16)
    grad_att = jnp.dot(grad_branch, weights_out.T, preferred_element_type=jnp.float32).astype(jnp.bfloat16)
    grad_att = grad_att.reshape(-1, HEADS, HEAD_DIM)
    grad_q, grad_k, grad_v = lax.map(attend_back_group, (arrange(queries, spatial), arrange(keys, spatial), arrange(values, spatial), arrange(grad_att, spatial)))
    grad_q = restore(grad_q, spatial)
    grad_k = restore(grad_k, spatial)
    grad_v = restore(grad_v, spatial)
    query_grad = head_back(grad_q, queries, query_inv, gains[0])
    key_grad = head_back(grad_k, keys, key_inv, gains[1])
    count = stream.shape[0]
    stacked = jnp.stack([query_grad.reshape(count, D), key_grad.reshape(count, D), grad_v.reshape(count, D)], axis=1)
    group_width = D // N_HEAD
    grad_normed = jnp.zeros(stream.shape, jnp.float32)
    for head_group in range(N_HEAD):
        lower = head_group * group_width
        left = stacked[:, :, lower:lower + group_width].reshape(count, 3 * group_width)
        right = weights_in[:, :, lower:lower + group_width].reshape(D, 3 * group_width)
        grad_normed = round_sum(grad_normed, jnp.dot(left, right.T, preferred_element_type=jnp.float32))
    scaled = grad_normed * (1.0 + modulation[1])
    centred = (stream.astype(jnp.float32) - row_mean) * inverse
    first = lax.optimization_barrier(jnp.mean(scaled, axis=-1, keepdims=True))
    second = lax.optimization_barrier(jnp.mean(scaled * centred, axis=-1, keepdims=True))
    return (incoming.astype(jnp.float32) + inverse * (scaled - first - centred * second)).astype(jnp.bfloat16)

def reference(tokens, cotangent, qkv_weight, out_weight, modulation, head_gains):
    middle, stored_s = forward(tokens, qkv_weight[0], out_weight[0], modulation[0], head_gains[0], True)
    mixed, stored_t = forward(middle, qkv_weight[1], out_weight[1], modulation[1], head_gains[1], False)
    grad_middle = backward(cotangent, middle, qkv_weight[1], out_weight[1], modulation[1], head_gains[1], stored_t, False)
    grad_tokens = backward(grad_middle, tokens, qkv_weight[0], out_weight[0], modulation[0], head_gains[0], stored_s, True)
    return (mixed, grad_tokens)
```

```python
import jax
import jax.numpy as jnp
from jax import lax
from jax.experimental import pallas as pl
from jax.experimental.pallas import tpu as pltpu
from jax.sharding import PartitionSpec as P

EPS = 1e-06
HEAD = 72
PER = 4
WIDE = 1152
PART = 288
ROWS = 512
OWN = 128
LOG2E = 1.4426950408889634
SCALE = HEAD**-0.5
F32 = jnp.float32
BF16 = jnp.bfloat16
VMEM_LIMIT = 56 * 1024 * 1024


def dot(a, b, over):
    return lax.dot_general(a, b, (((over[0],), (over[1],)), ((), ())), preferred_element_type=F32)


def call(body, outs, operands, scratch=(), flops=0, smem=0):
    size = sum(o.size * o.dtype.itemsize for o in (*outs, *operands))
    specs = [
        pl.BlockSpec(memory_space=pltpu.SMEM) if i < smem else pl.BlockSpec(memory_space=pltpu.VMEM)
        for i in range(len(operands))
    ]
    return pl.pallas_call(
        body,
        out_shape=list(outs),
        in_specs=specs,
        out_specs=[pl.BlockSpec(memory_space=pltpu.VMEM)] * len(outs),
        scratch_shapes=list(scratch),
        compiler_params=pltpu.CompilerParams(vmem_limit_bytes=VMEM_LIMIT),
        cost_estimate=pl.CostEstimate(flops=flops, bytes_accessed=size, transcendentals=0),
    )(*operands)


def out(shape, dtype=BF16):
    return jax.ShapeDtypeStruct(shape, dtype)


def head_norm_t(part, gains):
    n = part.shape[1]
    cube = part.reshape(PER, HEAD, n)
    inverse = lax.rsqrt(jnp.sum(cube * cube, axis=1, keepdims=True) * (1.0 / HEAD) + EPS)
    return (cube * inverse * gains.reshape(PER, HEAD, 1)).reshape(PART, n).astype(BF16), inverse


def head_back_t(incoming, normed, inverse, gains):
    n = incoming.shape[1]
    grad = incoming.astype(F32).reshape(PER, HEAD, n)
    norm = normed.astype(F32).reshape(PER, HEAD, n)
    gain = gains.reshape(PER, HEAD, 1)
    inner = jnp.sum(norm * grad, axis=1, keepdims=True) * (1.0 / HEAD)
    return (inverse * (gain * grad - norm * (1.0 / gain) * inner)).reshape(PART, n).astype(BF16)


def spatial_forward(
    me_ref, x0, x1, x2, x3, modc, gains, wt, wo, q_o, k_o, v_o, st_o, p0, p1, p2, p3, xrow, xs
):
    me = me_ref[0]
    for d, x in enumerate((x0, x1, x2, x3)):
        xs[pl.ds(pl.multiple_of((me ^ d) * PART, 32), PART), :] = x[...]
    stream = xs[...].astype(F32)
    mean = jnp.sum(stream, axis=0, keepdims=True) * (1.0 / WIDE)
    centred = stream - mean
    inverse = lax.rsqrt(jnp.sum(centred * centred, axis=0, keepdims=True) * (1.0 / WIDE) + EPS)
    normed = (centred * inverse * (1.0 + modc[:, 1:2]) + modc[:, 0:1]).astype(BF16)
    projected = dot(wt[...].reshape(3 * PART, WIDE), normed, (1, 0))
    query, inv_q = head_norm_t(projected[:PART], gains[:, 0:1])
    key, inv_k = head_norm_t(projected[PART : 2 * PART], gains[:, 1:2])
    q_o[...] = query
    k_o[...] = key
    v_o[...] = projected[2 * PART :].astype(BF16)
    st_o[0:4, :] = inv_q.reshape(PER, ROWS)
    st_o[4:8, :] = inv_k.reshape(PER, ROWS)
    st_o[8:9, :] = mean
    st_o[9:10, :] = inverse
    for d, partial in ((3, p3), (2, p2), (1, p1), (0, p0)):
        columns = pl.ds(pl.multiple_of((me ^ d) * OWN, OWN), OWN)
        queries = q_o[:, columns]
        pieces = []
        for h in range(PER):
            rows = slice(h * HEAD, (h + 1) * HEAD)
            scores = dot(k_o[rows, :], queries[rows], (0, 0))
            unnormed = jnp.exp2(scores * (SCALE * LOG2E))
            total = jnp.sum(unnormed, axis=0, keepdims=True)
            pieces.append(dot(v_o[rows, :], unnormed.astype(BF16), (1, 0)) * (1.0 / total))
        attended = jnp.concatenate(pieces, axis=0).astype(BF16)
        partial[...] = dot(attended, wo[...], (0, 0)).astype(BF16)
    own = xs[:, pl.ds(pl.multiple_of(me * OWN, OWN), OWN)].astype(F32)
    xrow[...] = own.T.astype(BF16)


def temporal(
    x0, x1, c0, c1, modr, gains, wt_a, wo_a, wt_b, wo_b, gn0, gn1, op0, op1
):
    stream = jnp.concatenate([x0[...], x1[...]], axis=0).astype(F32)
    incoming = jnp.concatenate([c0[...], c1[...]], axis=0).astype(F32)
    mean = jnp.sum(stream, axis=1, keepdims=True) * (1.0 / WIDE)
    centred = stream - mean
    inverse = lax.rsqrt(jnp.sum(centred * centred, axis=1, keepdims=True) * (1.0 / WIDE) + EPS)
    normed = (centred * inverse * (1.0 + modr[1:2, :]) + modr[0:1, :]).astype(BF16)
    gated = (modr[2:3, :] * incoming).astype(BF16)
    n = stream.shape[0]
    left = lax.broadcasted_iota(jnp.int32, (n, n), 0)
    right = lax.broadcasted_iota(jnp.int32, (n, n), 1)
    mask = ((left & 1) == (right & 1)) & ((left // OWN) == (right // OWN))
    branch = None
    grad_normed = None
    for wt, wo in ((wt_a, wo_a), (wt_b, wo_b)):
        weights = wt[...].reshape(3 * PART, WIDE)
        projected = dot(weights, normed, (1, 1))
        query, inv_q = head_norm_t(projected[:PART], gains[:, 0:1])
        key, inv_k = head_norm_t(projected[PART : 2 * PART], gains[:, 1:2])
        value = projected[2 * PART :].astype(BF16)
        grad_att = dot(wo[...], gated, (1, 1)).astype(BF16)
        attended, gq, gk, gv = [], [], [], []
        for h in range(PER):
            rows = slice(h * HEAD, (h + 1) * HEAD)
            q, k, v, da = query[rows], key[rows], value[rows], grad_att[rows]
            scores = dot(k, q, (0, 0))
            unnormed = jnp.where(mask, jnp.exp2(scores * (SCALE * LOG2E)), 0.0)
            probs = unnormed * (1.0 / jnp.sum(unnormed, axis=0, keepdims=True))
            rounded = probs.astype(BF16)
            attended.append(dot(v, rounded, (1, 0)))
            grad_probs = dot(v, da, (0, 0))
            inner = jnp.sum(grad_probs * probs, axis=0, keepdims=True)
            grad_scores = (probs * (grad_probs - inner)).astype(BF16)
            gv.append(dot(da, rounded, (1, 1)))
            gq.append(dot(k, grad_scores, (1, 0)) * SCALE)
            gk.append(dot(q, grad_scores, (1, 1)) * SCALE)
        attended = jnp.concatenate(attended, axis=0).astype(BF16)
        gq = jnp.concatenate(gq, axis=0).astype(BF16)
        gk = jnp.concatenate(gk, axis=0).astype(BF16)
        gv = jnp.concatenate(gv, axis=0).astype(BF16)
        dq = head_back_t(gq, query, inv_q, gains[:, 0:1])
        dk = head_back_t(gk, key, inv_k, gains[:, 1:2])
        stacked = jnp.concatenate([dq, dk, gv], axis=0)
        term = dot(stacked, weights, (0, 0))
        grad_normed = term if grad_normed is None else grad_normed + term
        term = dot(attended, wo[...], (0, 0))
        branch = term if branch is None else branch + term
    gn0[...] = grad_normed[:OWN]
    gn1[...] = grad_normed[OWN:].astype(BF16)
    op0[...] = branch[:OWN]
    op1[...] = branch[OWN:].astype(BF16)


def temporal_finish(x0, c0, gn0, gn1, op0, op1, modr, gm_o, mixed_o):
    stream = x0[...].astype(F32)
    mean = jnp.sum(stream, axis=1, keepdims=True) * (1.0 / WIDE)
    shifted = stream - mean
    inverse = lax.rsqrt(jnp.sum(shifted * shifted, axis=1, keepdims=True) * (1.0 / WIDE) + EPS)
    centred = shifted * inverse
    scaled = (gn0[...] + gn1[...].astype(F32)) * (1.0 + modr[1:2, :])
    first = jnp.sum(scaled, axis=1, keepdims=True) * (1.0 / WIDE)
    second = jnp.sum(scaled * centred, axis=1, keepdims=True) * (1.0 / WIDE)
    gm_o[...] = (c0[...].astype(F32) + inverse * (scaled - first - centred * second)).astype(BF16)
    mixed_o[...] = (stream + modr[2:3, :] * (op0[...] + op1[...].astype(F32))).astype(BF16)


def spatial_backward(
    me_ref, g0, g1, g2, g3, x0, x1, x2, x3, q_r, k_r, v_r, st, modr, modc, gains, wo, wn,
    p0, p1, p2, p3, rs_o, gown, da_s, gq_s,
):
    me = me_ref[0]
    gk = [None] * PER
    gv = [None] * PER
    for d, g in enumerate((g0, g1, g2, g3)):
        columns = pl.ds(pl.multiple_of((me ^ d) * OWN, OWN), OWN)
        gated = (modr[2:3, :] * g[...].astype(F32)).astype(BF16)
        grad_att = dot(wo[...], gated, (1, 1)).astype(BF16)
        queries = q_r[:, columns]
        for h in range(PER):
            rows = slice(h * HEAD, (h + 1) * HEAD)
            q, k, v, da = queries[rows], k_r[rows, :], v_r[rows, :], grad_att[rows]
            scores = dot(k, q, (0, 0))
            unnormed = jnp.exp2(scores * (SCALE * LOG2E))
            probs = unnormed * (1.0 / jnp.sum(unnormed, axis=0, keepdims=True))
            rounded = probs.astype(BF16)
            grad_probs = dot(v, da, (0, 0))
            inner = jnp.sum(grad_probs * probs, axis=0, keepdims=True)
            grad_scores = (probs * (grad_probs - inner)).astype(BF16)
            gv_t = dot(da, rounded, (1, 1))
            gk_t = dot(q, grad_scores, (1, 1))
            gv[h] = gv_t if gv[h] is None else gv[h] + gv_t
            gk[h] = gk_t if gk[h] is None else gk[h] + gk_t
            gq_s[rows, columns] = dot(k, grad_scores, (1, 0)) * SCALE
    inv_q = st[0:4, :].reshape(PER, 1, ROWS)
    inv_k = st[4:8, :].reshape(PER, 1, ROWS)
    gk = (jnp.concatenate(gk, axis=0) * SCALE).astype(BF16)
    gv = jnp.concatenate(gv, axis=0).astype(BF16)
    dq = head_back_t(gq_s[...].astype(BF16), q_r[...], inv_q, gains[:, 0:1])
    dk = head_back_t(gk, k_r[...], inv_k, gains[:, 1:2])
    stacked = jnp.concatenate([dq, dk, gv], axis=0)
    first = jnp.zeros((1, ROWS), F32)
    second = jnp.zeros((1, ROWS), F32)
    for d, x, partial in ((3, x3, p3), (1, x1, p1), (2, x2, p2), (0, x0, p0)):
        block = pl.ds(pl.multiple_of((me ^ d) * PART, 32), PART)
        term = dot(wn[block, :], stacked, (1, 0))
        partial[...] = term.astype(BF16)
        scaled = term * (1.0 + modc[block, 1:2])
        centred = (x[...].astype(F32) - st[8:9, :]) * st[9:10, :]
        first += jnp.sum(scaled, axis=0, keepdims=True)
        second += jnp.sum(scaled * centred, axis=0, keepdims=True)
    rs_o[...] = jnp.zeros_like(rs_o)
    rs_o[0:1, :] = first
    rs_o[1:2, :] = second
    for d, g in enumerate((g0, g1, g2, g3)):
        columns = pl.ds(pl.multiple_of((me ^ d) * OWN, OWN), OWN)
        da_s[...] = g[...].astype(F32).T
        gown[:, columns] = da_s[pl.ds(pl.multiple_of(me * PART, 32), PART), :].astype(BF16)


def spatial_finish(me_ref, p0, m1, o2, rs, st, x0, gown, modc, out_o):
    block = pl.ds(pl.multiple_of(me_ref[0] * PART, 32), PART)
    grad = p0[...].astype(F32) + m1[...].astype(F32) + o2[...].astype(F32)
    inverse = st[9:10, :]
    scaled = grad * (1.0 + modc[block, 1:2])
    centred = (x0[...].astype(F32) - st[8:9, :]) * inverse
    first = rs[0:1, :] * (1.0 / WIDE)
    second = rs[1:2, :] * (1.0 / WIDE)
    out_o[...] = (gown[...].astype(F32) + inverse * (scaled - first - centred * second)).astype(BF16)


def gather_rows(me_ref, c0, c1, c2, c3, rows_o, cs):
    me = me_ref[0]
    for d, c in enumerate((c0, c1, c2, c3)):
        cs[pl.ds(pl.multiple_of((me ^ d) * PART, 32), PART), :] = c[...].astype(F32)
    rows_o[...] = cs[...].T.astype(BF16)


def split_rows(me_ref, rows, c0, c1, c2, c3, cs):
    me = me_ref[0]
    cs[...] = rows[...].astype(F32).T
    for d, c in enumerate((c0, c1, c2, c3)):
        c[...] = cs[pl.ds(pl.multiple_of((me ^ d) * PART, 32), PART), :].astype(BF16)


def place_columns(me_ref, c0, c1, c2, c3, out_o):
    me = me_ref[0]
    for d, c in enumerate((c0, c1, c2, c3)):
        out_o[:, pl.ds(pl.multiple_of((me ^ d) * OWN, OWN), OWN)] = c[...]


def swap(values, d):
    return lax.ppermute(values, "head", [(i, i ^ d) for i in range(4)])


def across_seq(rows):
    moved = lax.all_to_all(
        rows.reshape(64, 2, WIDE), "seq", split_axis=0, concat_axis=0, tiled=True
    )
    return moved.reshape(OWN, WIDE)


def on_device(tokens, cotangent, qkv_weight, out_weight, modulation, head_gains):
    me = lax.axis_index("head")
    mine = me.astype(jnp.int32).reshape(1)
    wt = jnp.transpose(qkv_weight, (0, 2, 3, 1))
    modc = jnp.pad(modulation.transpose(2, 0, 1).reshape(WIDE, 6), ((0, 0), (0, 2)))
    gains = jnp.tile(head_gains.reshape(4, HEAD).T, (PER, 1))
    gains = jnp.pad(gains, ((0, 0), (0, 4)), constant_values=1.0)
    modc_s, gains_s, gains_t = modc, gains[:, 0:2], gains[:, 2:4]

    x0 = tokens.T
    x2 = swap(x0, 2)
    x1 = swap(x0, 1)
    x3 = swap(x2, 1)

    wt_t, wo_t = wt[1], out_weight[1]
    wt_far, wo_far = swap(wt_t, 2), swap(wo_t, 2)

    cot = cotangent.T
    parts = [
        lax.dynamic_slice_in_dim(cot, (me ^ d) * OWN, OWN, axis=1) for d in range(4)
    ]
    parts = [parts[0]] + [swap(parts[d], d) for d in (1, 2, 3)]
    (cot_rows,) = call(
        gather_rows, [out((OWN, WIDE))], [mine, *parts],
        [pltpu.VMEM((WIDE, OWN), F32)], smem=1,
    )
    cot0 = across_seq(cot_rows)
    cot1 = swap(cot0, 1)

    query, key, value, stats, p0, p1, p2, p3, xrow = call(
        spatial_forward,
        [out((PART, ROWS))] * 3 + [out((16, ROWS), F32)] + [out((OWN, WIDE))] * 5,
        [mine, x0, x1, x2, x3, modc_s, gains_s, wt[0], out_weight[0]],
        [pltpu.VMEM((WIDE, ROWS), BF16)],
        flops=2 * 10**9, smem=1,
    )
    m1, m3 = swap(p1, 1), swap(p3, 1)
    far = swap((p2.astype(F32) + m3.astype(F32)).astype(BF16), 2)
    branch = p0.astype(F32) + m1.astype(F32) + far.astype(F32)
    middle = (xrow.astype(F32) + modulation[0, 2][None] * branch).astype(BF16)

    t0 = across_seq(middle)
    t1 = swap(t0, 1)
    gn0, gn1, op0, op1 = call(
        temporal,
        [out((OWN, WIDE), F32), out((OWN, WIDE)), out((OWN, WIDE), F32), out((OWN, WIDE))],
        [t0, t1, cot0, cot1, modulation[1], gains_t, wt_t, wo_t, wt_far, wo_far],
        flops=3 * 10**9,
    )
    gn1, op1 = swap(gn1, 1), swap(op1, 1)
    grad_middle, mixed_rows = call(
        temporal_finish, [out((OWN, WIDE))] * 2, [t0, cot0, gn0, gn1, op0, op1, modulation[1]]
    )

    g0 = across_seq(grad_middle)
    g2 = swap(g0, 2)
    g1 = swap(g0, 1)
    g3 = swap(g2, 1)

    mixed_rows = across_seq(mixed_rows)
    parts = call(
        split_rows, [out((PART, OWN))] * 4, [mine, mixed_rows],
        [pltpu.VMEM((WIDE, OWN), F32)], smem=1,
    )
    parts = [parts[0]] + [swap(parts[d], d) for d in (1, 2, 3)]
    (mixed,) = call(place_columns, [out((PART, ROWS))], [mine, *parts], smem=1)

    wn = jnp.transpose(qkv_weight[0].reshape(WIDE, 3 * PART), (0, 1))
    p0, p1, p2, p3, sums, gown = call(
        spatial_backward,
        [out((PART, ROWS))] * 4 + [out((8, ROWS), F32), out((PART, ROWS))],
        [mine, g0, g1, g2, g3, x0, x1, x2, x3, query, key, value, stats, modulation[0], modc_s,
         gains_s, out_weight[0], wn],
        [pltpu.VMEM((WIDE, OWN), F32), pltpu.VMEM((PART, ROWS), F32)],
        flops=3 * 10**9, smem=1,
    )
    m1, m3 = swap(p1, 1), swap(p3, 1)
    sums = sums + swap(sums, 1)
    far = swap((p2.astype(F32) + m3.astype(F32)).astype(BF16), 2)
    sums = sums + swap(sums, 2)
    (grad,) = call(
        spatial_finish, [out((PART, ROWS))],
        [mine, p0, m1, far, sums, stats, x0, gown, modc_s], smem=1,
    )
    return (mixed.T, grad.T)


def solution(mesh):
    in_specs = (
        P("seq", "head"),
        P("seq", "head"),
        P(None, None, None, "head"),
        P(None, "head", None),
        P(),
        P(),
    )
    out_specs = (P("seq", "head"), P("seq", "head"))
    return jax.shard_map(
        on_device, mesh=mesh, in_specs=in_specs, out_specs=out_specs, check_vma=False
    )
```

```python
import jax
import jax.numpy as jnp
from jax import lax
from jax.experimental import pallas as pl
from jax.experimental.pallas import tpu as pltpu
from jax.sharding import PartitionSpec as P

EPS = 1e-06
HEAD = 72
PER = 4
WIDE = 1152
PART = 288
ROWS = 512
OWN = 128
LOG2E = 1.4426950408889634
SCALE = HEAD**-0.5
F32 = jnp.float32
BF16 = jnp.bfloat16
VMEM_LIMIT = 56 * 1024 * 1024


def dot(a, b, over):
    return lax.dot_general(a, b, (((over[0],), (over[1],)), ((), ())), preferred_element_type=F32)


def call(body, outs, operands, scratch=(), flops=0, smem=0):
    size = sum(o.size * o.dtype.itemsize for o in (*outs, *operands))
    specs = [
        pl.BlockSpec(memory_space=pltpu.SMEM) if i < smem else pl.BlockSpec(memory_space=pltpu.VMEM)
        for i in range(len(operands))
    ]
    return pl.pallas_call(
        body,
        out_shape=list(outs),
        in_specs=specs,
        out_specs=[pl.BlockSpec(memory_space=pltpu.VMEM)] * len(outs),
        scratch_shapes=list(scratch),
        compiler_params=pltpu.CompilerParams(vmem_limit_bytes=VMEM_LIMIT),
        cost_estimate=pl.CostEstimate(flops=flops, bytes_accessed=size, transcendentals=0),
    )(*operands)


def out(shape, dtype=BF16):
    return jax.ShapeDtypeStruct(shape, dtype)


def head_norm_t(part, gains):
    n = part.shape[1]
    cube = part.reshape(PER, HEAD, n)
    inverse = lax.rsqrt(jnp.sum(cube * cube, axis=1, keepdims=True) * (1.0 / HEAD) + EPS)
    return (cube * inverse * gains.reshape(PER, HEAD, 1)).reshape(PART, n).astype(BF16), inverse


def head_back_t(incoming, normed, inverse, gains):
    n = incoming.shape[1]
    grad = incoming.astype(F32).reshape(PER, HEAD, n)
    norm = normed.astype(F32).reshape(PER, HEAD, n)
    gain = gains.reshape(PER, HEAD, 1)
    inner = jnp.sum(norm * grad, axis=1, keepdims=True) * (1.0 / HEAD)
    return (inverse * (gain * grad - norm * (1.0 / gain) * inner)).reshape(PART, n).astype(BF16)


def softmax_pieces(query, key, value):
    pieces = []
    for h in range(PER):
        rows = slice(h * HEAD, (h + 1) * HEAD)
        scores = dot(key[rows], query[rows], (0, 0))
        unnormed = jnp.exp2(scores * (SCALE * LOG2E))
        total = jnp.sum(unnormed, axis=0, keepdims=True)
        pieces.append(dot(value[rows], unnormed.astype(BF16), (1, 0)) * (1.0 / total))
    return jnp.concatenate(pieces, axis=0).astype(BF16)


def half_of(me, other):
    return pl.ds(pl.multiple_of(((me // 2) ^ other) * 2 * OWN, 2 * OWN), 2 * OWN)


def core_of(me, d):
    return pl.ds(pl.multiple_of(((me ^ d) & 1) * OWN, OWN), OWN)


def part_of(me, d):
    return pl.ds(pl.multiple_of((me ^ d) * PART, 32), PART)


def own_of(me, d):
    return pl.ds(pl.multiple_of((me ^ d) * OWN, OWN), OWN)


def spatial_forward(
    me_ref, x0, x1, x2, x3, modc, gains, wt, wo, q_o, k_o, v_o, st_o, p2, p3, xs, att
):
    me = me_ref[0]
    for d, x in enumerate((x0, x1, x2, x3)):
        xs[part_of(me, d), :] = x[...]
    stream = xs[...].astype(F32)
    mean = jnp.sum(stream, axis=0, keepdims=True) * (1.0 / WIDE)
    centred = stream - mean
    inverse = lax.rsqrt(jnp.sum(centred * centred, axis=0, keepdims=True) * (1.0 / WIDE) + EPS)
    normed = (centred * inverse * (1.0 + modc[:, 1:2]) + modc[:, 0:1]).astype(BF16)
    projected = dot(wt[...].reshape(3 * PART, WIDE), normed, (1, 0))
    query, inv_q = head_norm_t(projected[:PART], gains[:, 0:1])
    key, inv_k = head_norm_t(projected[PART : 2 * PART], gains[:, 1:2])
    q_o[...] = query
    k_o[...] = key
    v_o[...] = projected[2 * PART :].astype(BF16)
    st_o[0:4, :] = inv_q.reshape(PER, ROWS)
    st_o[4:8, :] = inv_k.reshape(PER, ROWS)
    st_o[8:9, :] = mean
    st_o[9:10, :] = inverse
    att[...] = softmax_pieces(q_o[:, half_of(me, 1)], k_o[...], v_o[...])
    for d, partial in ((3, p3), (2, p2)):
        partial[...] = dot(att[:, core_of(me, d)], wo[...], (0, 0)).astype(BF16)


def spatial_forward_own(me_ref, x0, x1, x2, x3, q_r, k_r, v_r, wo, p0, p1, xrow, xs, att):
    me = me_ref[0]
    att[...] = softmax_pieces(q_r[:, half_of(me, 0)], k_r[...], v_r[...])
    for d, partial in ((1, p1), (0, p0)):
        partial[...] = dot(att[:, core_of(me, d)], wo[...], (0, 0)).astype(BF16)
    for d, x in enumerate((x0, x1, x2, x3)):
        xs[part_of(me, d), :] = x[:, own_of(me, 0)].astype(F32)
    xrow[...] = xs[...].T.astype(BF16)


def temporal_group(normed, gated, gains, weights, wo):
    n = normed.shape[0]
    left = lax.broadcasted_iota(jnp.int32, (n, n), 0)
    right = lax.broadcasted_iota(jnp.int32, (n, n), 1)
    mask = ((left & 1) == (right & 1)) & ((left // OWN) == (right // OWN))
    projected = dot(weights, normed, (1, 1))
    query, inv_q = head_norm_t(projected[:PART], gains[:, 0:1])
    key, inv_k = head_norm_t(projected[PART : 2 * PART], gains[:, 1:2])
    value = projected[2 * PART :].astype(BF16)
    grad_att = dot(wo, gated, (1, 1)).astype(BF16)
    attended, gq, gk, gv = [], [], [], []
    for h in range(PER):
        rows = slice(h * HEAD, (h + 1) * HEAD)
        q, k, v, da = query[rows], key[rows], value[rows], grad_att[rows]
        scores = dot(k, q, (0, 0))
        unnormed = jnp.where(mask, jnp.exp2(scores * (SCALE * LOG2E)), 0.0)
        probs = unnormed * (1.0 / jnp.sum(unnormed, axis=0, keepdims=True))
        rounded = probs.astype(BF16)
        attended.append(dot(v, rounded, (1, 0)))
        grad_probs = dot(v, da, (0, 0))
        inner = jnp.sum(grad_probs * probs, axis=0, keepdims=True)
        grad_scores = (probs * (grad_probs - inner)).astype(BF16)
        gv.append(dot(da, rounded, (1, 1)))
        gq.append(dot(k, grad_scores, (1, 0)) * SCALE)
        gk.append(dot(q, grad_scores, (1, 1)) * SCALE)
    attended = jnp.concatenate(attended, axis=0).astype(BF16)
    gq = jnp.concatenate(gq, axis=0).astype(BF16)
    gk = jnp.concatenate(gk, axis=0).astype(BF16)
    gv = jnp.concatenate(gv, axis=0).astype(BF16)
    dq = head_back_t(gq, query, inv_q, gains[:, 0:1])
    dk = head_back_t(gk, key, inv_k, gains[:, 1:2])
    stacked = jnp.concatenate([dq, dk, gv], axis=0)
    return dot(stacked, weights, (0, 0)), dot(attended, wo, (0, 0))


def temporal_own(x0, x1, c0, c1, modr, gains, wt, wo, gn_o, br_o, normed_o, gated_o):
    stream = jnp.concatenate([x0[...], x1[...]], axis=0).astype(F32)
    incoming = jnp.concatenate([c0[...], c1[...]], axis=0).astype(F32)
    mean = jnp.sum(stream, axis=1, keepdims=True) * (1.0 / WIDE)
    centred = stream - mean
    inverse = lax.rsqrt(jnp.sum(centred * centred, axis=1, keepdims=True) * (1.0 / WIDE) + EPS)
    normed = (centred * inverse * (1.0 + modr[1:2, :]) + modr[0:1, :]).astype(BF16)
    gated = (modr[2:3, :] * incoming).astype(BF16)
    normed_o[...] = normed
    gated_o[...] = gated
    term, branch = temporal_group(
        normed, gated, gains[...], wt[...].reshape(3 * PART, WIDE), wo[...]
    )
    gn_o[...] = term.astype(BF16)
    br_o[...] = branch.astype(BF16)


def temporal_far(
    normed, gated, gn_r, br_r, gains, wq, wk, wv, wo, gn0, gn1, op0, op1
):
    weights = jnp.concatenate([wq[...], wk[...], wv[...]], axis=0)
    term, branch = temporal_group(normed[...], gated[...], gains[...], weights, wo[...])
    term = term + gn_r[...].astype(F32)
    branch = branch + br_r[...].astype(F32)
    gn0[...] = term[:OWN]
    gn1[...] = term[OWN:].astype(BF16)
    op0[...] = branch[:OWN]
    op1[...] = branch[OWN:].astype(BF16)


def temporal_finish(x0, c0, gn0, gn1, op0, op1, modr, gm_o, mixed_o):
    stream = x0[...].astype(F32)
    mean = jnp.sum(stream, axis=1, keepdims=True) * (1.0 / WIDE)
    shifted = stream - mean
    inverse = lax.rsqrt(jnp.sum(shifted * shifted, axis=1, keepdims=True) * (1.0 / WIDE) + EPS)
    centred = shifted * inverse
    scaled = (gn0[...] + gn1[...].astype(F32)) * (1.0 + modr[1:2, :])
    first = jnp.sum(scaled, axis=1, keepdims=True) * (1.0 / WIDE)
    second = jnp.sum(scaled * centred, axis=1, keepdims=True) * (1.0 / WIDE)
    gm_o[...] = (c0[...].astype(F32) + inverse * (scaled - first - centred * second)).astype(BF16)
    mixed_o[...] = (stream + modr[2:3, :] * (op0[...] + op1[...].astype(F32))).astype(BF16)


def backward_half(queries, grad_att, k_r, v_r):
    gq, gk, gv = [], [], []
    for h in range(PER):
        rows = slice(h * HEAD, (h + 1) * HEAD)
        q, k, v, da = queries[rows], k_r[rows, :], v_r[rows, :], grad_att[rows]
        scores = dot(k, q, (0, 0))
        unnormed = jnp.exp2(scores * (SCALE * LOG2E))
        probs = unnormed * (1.0 / jnp.sum(unnormed, axis=0, keepdims=True))
        rounded = probs.astype(BF16)
        grad_probs = dot(v, da, (0, 0))
        inner = jnp.sum(grad_probs * probs, axis=0, keepdims=True)
        grad_scores = (probs * (grad_probs - inner)).astype(BF16)
        gv.append(dot(da, rounded, (1, 1)))
        gk.append(dot(q, grad_scores, (1, 1)))
        gq.append(dot(k, grad_scores, (1, 0)) * SCALE)
    return [jnp.concatenate(g, axis=0) for g in (gq, gk, gv)]


def gated_half(me, d, ga, gb, modr, rows):
    rows[core_of(me, d), :] = (modr[2:3, :] * ga[...].astype(F32)).astype(BF16)
    rows[core_of(me, d ^ 1), :] = (modr[2:3, :] * gb[...].astype(F32)).astype(BF16)
    return rows[...]


def spatial_backward_own(me_ref, g0, g1, q_r, k_r, v_r, modr, wo, gq_o, gk_o, gv_o, rows):
    me = me_ref[0]
    gated = gated_half(me, 0, g0, g1, modr, rows)
    grad_att = dot(wo[...], gated, (1, 1)).astype(BF16)
    gq, gk, gv = backward_half(q_r[:, half_of(me, 0)], grad_att, k_r, v_r)
    gq_o[...] = gq.astype(BF16)
    gk_o[...] = gk
    gv_o[...] = gv


def block_back(me, d, stacked, x, st, modc, wn, partial):
    term = dot(wn[part_of(me, d), :], stacked, (1, 0))
    partial[...] = term.astype(BF16)
    scaled = term * (1.0 + modc[part_of(me, d), 1:2])
    centred = (x[...].astype(F32) - st[8:9, :]) * st[9:10, :]
    return (
        jnp.sum(scaled, axis=0, keepdims=True),
        jnp.sum(scaled * centred, axis=0, keepdims=True),
    )


def spatial_backward_far(
    me_ref, g2, g3, x2, x3, q_r, k_r, v_r, st, gq_r, gk_r, gv_r, modr, modc, gains, wo, wn,
    p2, p3, stacked_o, rs_o, rows, gq_s,
):
    me = me_ref[0]
    gated = gated_half(me, 2, g2, g3, modr, rows)
    grad_att = dot(wo[...], gated, (1, 1)).astype(BF16)
    gq, gk, gv = backward_half(q_r[:, half_of(me, 1)], grad_att, k_r, v_r)
    gq_s[:, half_of(me, 0)] = gq_r[...]
    gq_s[:, half_of(me, 1)] = gq.astype(BF16)
    gk = ((gk + gk_r[...]) * SCALE).astype(BF16)
    inv_q = st[0:4, :].reshape(PER, 1, ROWS)
    inv_k = st[4:8, :].reshape(PER, 1, ROWS)
    stacked_o[:PART, :] = head_back_t(gq_s[...], q_r[...], inv_q, gains[:, 0:1])
    stacked_o[PART : 2 * PART, :] = head_back_t(gk, k_r[...], inv_k, gains[:, 1:2])
    stacked_o[2 * PART :, :] = (gv + gv_r[...]).astype(BF16)
    stacked = stacked_o[...]
    first, second = block_back(me, 3, stacked, x3, st, modc, wn, p3)
    more, again = block_back(me, 2, stacked, x2, st, modc, wn, p2)
    rs_o[...] = jnp.zeros_like(rs_o)
    rs_o[0:1, :] = first + more
    rs_o[1:2, :] = second + again


def spatial_backward_last(
    me_ref, stacked_r, x0, x1, st, rs_r, modc, wn, g0, g1, g2, g3, p0, p1, rs_o, gown, rows
):
    me = me_ref[0]
    stacked = stacked_r[...]
    first, second = block_back(me, 1, stacked, x1, st, modc, wn, p1)
    more, again = block_back(me, 0, stacked, x0, st, modc, wn, p0)
    rs_o[...] = jnp.zeros_like(rs_o)
    rs_o[0:1, :] = rs_r[0:1, :] + first + more
    rs_o[1:2, :] = rs_r[1:2, :] + second + again
    for d, g in enumerate((g0, g1, g2, g3)):
        rows[...] = g[...].astype(F32).T
        gown[:, own_of(me, d)] = rows[part_of(me, 0), :].astype(BF16)


def spatial_finish(me_ref, p0, m1, o2, rs, st, x0, gown, modc, out_o):
    grad = p0[...].astype(F32) + m1[...].astype(F32) + o2[...].astype(F32)
    inverse = st[9:10, :]
    scaled = grad * (1.0 + modc[part_of(me_ref[0], 0), 1:2])
    centred = (x0[...].astype(F32) - st[8:9, :]) * inverse
    first = rs[0:1, :] * (1.0 / WIDE)
    second = rs[1:2, :] * (1.0 / WIDE)
    out_o[...] = (gown[...].astype(F32) + inverse * (scaled - first - centred * second)).astype(BF16)


def moves(swapped):
    a = lax.broadcasted_iota(jnp.int32, (ROWS, ROWS), 0)
    b = lax.broadcasted_iota(jnp.int32, (ROWS, ROWS), 1)
    if swapped:
        a, b = b, a
    target = ((a >> 1) & 3) * OWN + (a >> 3) * 2 + (a & 1)
    return jnp.where(target == b, 1.0, 0.0).astype(BF16)


def pack_columns(columns, rows_o):
    rows_o[...] = dot(moves(False), columns[...], (1, 1)).astype(BF16)


def unpack_rows(rows, columns_o):
    columns_o[...] = dot(rows[...], moves(False), (0, 0)).astype(BF16)


def unpack_parts(me_ref, rows, c0, c1, c2, c3, cs):
    me = me_ref[0]
    cs[...] = dot(rows[...], moves(False), (0, 0)).astype(BF16)
    for d, c in enumerate((c0, c1, c2, c3)):
        c[...] = cs[:, own_of(me, d)]


def gather_rows(me_ref, c0, c1, c2, c3, rows_o, cs):
    me = me_ref[0]
    for d, c in enumerate((c0, c1, c2, c3)):
        cs[part_of(me, d), :] = c[...].astype(F32)
    rows_o[...] = cs[...].T.astype(BF16)


def split_rows(me_ref, rows, c0, c1, c2, c3, cs):
    me = me_ref[0]
    cs[...] = rows[...].astype(F32).T
    for d, c in enumerate((c0, c1, c2, c3)):
        c[...] = cs[part_of(me, d), :].astype(BF16)


def pack_parts(me_ref, c0, c1, c2, c3, rows_o, cs):
    me = me_ref[0]
    for d, c in enumerate((c0, c1, c2, c3)):
        cs[:, own_of(me, d)] = c[...]
    rows_o[...] = dot(moves(False), cs[...], (1, 1)).astype(BF16)


def swap(values, d):
    return lax.ppermute(values, "head", [(i, i ^ d) for i in range(4)])


def after(values, *others):
    return lax.optimization_barrier((values, *others))[0]


def across_seq(rows, lines, width):
    moved = lax.all_to_all(
        rows.reshape(64, lines, width), "seq", split_axis=0, concat_axis=0, tiled=True
    )
    return moved.reshape(64 * lines, width)


def on_device(tokens, cotangent, qkv_weight, out_weight, modulation, head_gains):
    me = lax.axis_index("head")
    mine = me.astype(jnp.int32).reshape(1)
    wt = jnp.transpose(qkv_weight, (0, 2, 3, 1))
    modc = jnp.pad(modulation.transpose(2, 0, 1).reshape(WIDE, 6), ((0, 0), (0, 2)))
    gains = jnp.tile(head_gains.reshape(4, HEAD).T, (PER, 1))
    gains = jnp.pad(gains, ((0, 0), (0, 4)), constant_values=1.0)
    gains_s, gains_t = gains[:, 0:2], gains[:, 2:4]
    row = out((OWN, WIDE))
    col = out((PART, ROWS))
    piece = out((PART, OWN))

    x0 = tokens.T
    x2 = swap(x0, 2)
    x1 = swap(x0, 1)
    x3 = swap(x2, 1)

    (cot_rows,) = call(pack_columns, [out((ROWS, PART))], [cotangent.T], flops=10**8)
    cot_moved = across_seq(cot_rows, 8, PART)

    w0 = swap(after(wt[1, 0], x2), 2)
    query, key, value, stats, p2, p3 = call(
        spatial_forward,
        [col] * 3 + [out((16, ROWS), F32)] + [row] * 2,
        [mine, x0, x1, x2, x3, modc, gains_s, wt[0], out_weight[0]],
        [pltpu.VMEM((WIDE, ROWS), BF16), pltpu.VMEM((PART, 2 * OWN), BF16)],
        flops=2 * 10**9, smem=1,
    )
    m3 = swap(p3, 1)
    chip = (p2.astype(F32) + m3.astype(F32)).astype(BF16)
    far = swap(chip, 2)
    p0, p1, xrow = call(
        spatial_forward_own, [row] * 3,
        [mine, x0, x1, x2, x3, query, key, value, out_weight[0]],
        [pltpu.VMEM((WIDE, OWN), F32), pltpu.VMEM((PART, 2 * OWN), BF16)],
        flops=10**9, smem=1,
    )
    m1 = swap(p1, 1)
    parts = call(
        unpack_parts, [piece] * 4, [mine, after(cot_moved, chip)],
        [pltpu.VMEM((PART, ROWS), BF16)], flops=10**8, smem=1,
    )
    parts = [parts[0]] + [swap(parts[d], d) for d in (1, 2, 3)]
    (cot0,) = call(
        gather_rows, [row], [mine, *parts], [pltpu.VMEM((WIDE, OWN), F32)], smem=1
    )
    cot1 = swap(cot0, 1)
    w1, w2, w3 = (swap(after(w, far), 2) for w in (wt[1, 1], wt[1, 2], out_weight[1]))

    branch = p0.astype(F32) + m1.astype(F32) + far.astype(F32)
    middle = (xrow.astype(F32) + modulation[0, 2][None] * branch).astype(BF16)

    t0 = across_seq(middle, 2, WIDE)
    t1 = swap(t0, 1)
    gn, br, normed, gated = call(
        temporal_own, [out((2 * OWN, WIDE))] * 4,
        [t0, t1, cot0, cot1, modulation[1], gains_t, wt[1], out_weight[1]],
        flops=2 * 10**9,
    )
    gn0, gn1, op0, op1 = call(
        temporal_far,
        [out((OWN, WIDE), F32), row, out((OWN, WIDE), F32), row],
        [normed, gated, gn, br, gains_t, w0, w1, w2, w3],
        flops=2 * 10**9,
    )
    gn1, op1 = swap(gn1, 1), swap(op1, 1)
    grad_middle, mixed_rows = call(
        temporal_finish, [row] * 2, [t0, cot0, gn0, gn1, op0, op1, modulation[1]]
    )

    g0 = across_seq(grad_middle, 2, WIDE)
    g2 = swap(g0, 2)
    g1 = swap(g0, 1)
    g3 = swap(g2, 1)

    parts = call(
        split_rows, [piece] * 4, [mine, mixed_rows], [pltpu.VMEM((WIDE, OWN), F32)], smem=1
    )
    parts = [parts[0]] + [swap(parts[d], d) for d in (1, 2, 3)]
    (mixed_rows,) = call(
        pack_parts, [out((ROWS, PART))], [mine, *parts],
        [pltpu.VMEM((PART, ROWS), BF16)], flops=10**8, smem=1,
    )
    mixed_rows = across_seq(after(mixed_rows, g0), 8, PART)
    (mixed,) = call(unpack_rows, [col], [mixed_rows], flops=10**8)

    wn = qkv_weight[0].reshape(WIDE, 3 * PART)
    gq, gk, gv = call(
        spatial_backward_own,
        [out((PART, 2 * OWN)), out((PART, ROWS), F32), out((PART, ROWS), F32)],
        [mine, g0, g1, query, key, value, modulation[0], out_weight[0]],
        [pltpu.VMEM((2 * OWN, WIDE), BF16)],
        flops=2 * 10**9, smem=1,
    )
    p2, p3, stacked, sums = call(
        spatial_backward_far,
        [col, col, out((3 * PART, ROWS)), out((8, ROWS), F32)],
        [mine, g2, g3, x2, x3, query, key, value, stats, gq, gk, gv, modulation[0], modc,
         gains_s, out_weight[0], wn],
        [pltpu.VMEM((2 * OWN, WIDE), BF16), pltpu.VMEM((PART, ROWS), BF16)],
        flops=3 * 10**9, smem=1,
    )
    m3 = swap(p3, 1)
    far = swap((p2.astype(F32) + m3.astype(F32)).astype(BF16), 2)
    p0, p1, sums, gown = call(
        spatial_backward_last,
        [col, col, out((8, ROWS), F32), col],
        [mine, stacked, x0, x1, stats, sums, modc, wn, g0, g1, g2, g3],
        [pltpu.VMEM((WIDE, OWN), F32)],
        flops=10**9, smem=1,
    )
    m1 = swap(p1, 1)
    sums = sums + swap(sums, 1)
    sums = sums + swap(sums, 2)
    (grad,) = call(
        spatial_finish, [col], [mine, p0, m1, far, sums, stats, x0, gown, modc], smem=1
    )
    return (mixed.T, grad.T)


def solution(mesh):
    in_specs = (
        P("seq", "head"),
        P("seq", "head"),
        P(None, None, None, "head"),
        P(None, "head", None),
        P(),
        P(),
    )
    out_specs = (P("seq", "head"), P("seq", "head"))
    return jax.shard_map(
        on_device, mesh=mesh, in_specs=in_specs, out_specs=out_specs, check_vma=False
    )
```

```python
import jax
import jax.numpy as jnp
from jax import lax
from jax.experimental import pallas as pl
from jax.experimental.pallas import tpu as pltpu
from jax.sharding import PartitionSpec as P

EPS = 1e-06
HEAD = 72
PER = 4
WIDE = 1152
PART = 288
ROWS = 512
OWN = 128
LOG2E = 1.4426950408889634
SCALE = HEAD**-0.5
F32 = jnp.float32
BF16 = jnp.bfloat16
VMEM_LIMIT = 56 * 1024 * 1024


def dot(a, b, over):
    return lax.dot_general(a, b, (((over[0],), (over[1],)), ((), ())), preferred_element_type=F32)


def call(body, outs, operands, scratch=(), flops=0, smem=0):
    size = sum(o.size * o.dtype.itemsize for o in (*outs, *operands))
    specs = [
        pl.BlockSpec(memory_space=pltpu.SMEM) if i < smem else pl.BlockSpec(memory_space=pltpu.VMEM)
        for i in range(len(operands))
    ]
    return pl.pallas_call(
        body,
        out_shape=list(outs),
        in_specs=specs,
        out_specs=[pl.BlockSpec(memory_space=pltpu.VMEM)] * len(outs),
        scratch_shapes=list(scratch),
        compiler_params=pltpu.CompilerParams(vmem_limit_bytes=VMEM_LIMIT),
        cost_estimate=pl.CostEstimate(flops=flops, bytes_accessed=size, transcendentals=0),
    )(*operands)


def out(shape, dtype=BF16):
    return jax.ShapeDtypeStruct(shape, dtype)


def head_norm_t(part, gains):
    n = part.shape[1]
    cube = part.reshape(PER, HEAD, n)
    inverse = lax.rsqrt(jnp.sum(cube * cube, axis=1, keepdims=True) * (1.0 / HEAD) + EPS)
    return (cube * inverse * gains.reshape(PER, HEAD, 1)).reshape(PART, n).astype(BF16), inverse


def head_back_t(incoming, normed, inverse, gains):
    n = incoming.shape[1]
    grad = incoming.astype(F32).reshape(PER, HEAD, n)
    norm = normed.astype(F32).reshape(PER, HEAD, n)
    gain = gains.reshape(PER, HEAD, 1)
    inner = jnp.sum(norm * grad, axis=1, keepdims=True) * (1.0 / HEAD)
    return (inverse * (gain * grad - norm * (1.0 / gain) * inner)).reshape(PART, n).astype(BF16)


def softmax_pieces(query, key, value):
    pieces = []
    for h in range(PER):
        rows = slice(h * HEAD, (h + 1) * HEAD)
        scores = dot(key[rows], query[rows], (0, 0))
        unnormed = jnp.exp2(scores * (SCALE * LOG2E))
        total = jnp.sum(unnormed, axis=0, keepdims=True)
        pieces.append(dot(value[rows], unnormed.astype(BF16), (1, 0)) * (1.0 / total))
    return jnp.concatenate(pieces, axis=0).astype(BF16)


def half_of(me, other):
    return pl.ds(pl.multiple_of(((me // 2) ^ other) * 2 * OWN, 2 * OWN), 2 * OWN)


def core_of(me, d):
    return pl.ds(pl.multiple_of(((me ^ d) & 1) * OWN, OWN), OWN)


def part_of(me, d):
    return pl.ds(pl.multiple_of((me ^ d) * PART, 32), PART)


def own_of(me, d):
    return pl.ds(pl.multiple_of((me ^ d) * OWN, OWN), OWN)


def spatial_forward(
    me_ref, x0, x1, x2, x3, modc, gains, wt, wo, q_o, k_o, v_o, st_o, p2, p3, xs, att
):
    me = me_ref[0]
    for d, x in enumerate((x0, x1, x2, x3)):
        xs[part_of(me, d), :] = x[...]
    stream = xs[...].astype(F32)
    mean = jnp.sum(stream, axis=0, keepdims=True) * (1.0 / WIDE)
    centred = stream - mean
    inverse = lax.rsqrt(jnp.sum(centred * centred, axis=0, keepdims=True) * (1.0 / WIDE) + EPS)
    normed = (centred * inverse * (1.0 + modc[:, 1:2]) + modc[:, 0:1]).astype(BF16)
    projected = dot(wt[...].reshape(3 * PART, WIDE), normed, (1, 0))
    query, inv_q = head_norm_t(projected[:PART], gains[:, 0:1])
    key, inv_k = head_norm_t(projected[PART : 2 * PART], gains[:, 1:2])
    q_o[...] = query
    k_o[...] = key
    v_o[...] = projected[2 * PART :].astype(BF16)
    st_o[0:4, :] = inv_q.reshape(PER, ROWS)
    st_o[4:8, :] = inv_k.reshape(PER, ROWS)
    st_o[8:9, :] = mean
    st_o[9:10, :] = inverse
    att[...] = softmax_pieces(q_o[:, half_of(me, 1)], k_o[...], v_o[...])
    for d, partial in ((3, p3), (2, p2)):
        partial[...] = dot(att[:, core_of(me, d)], wo[...], (0, 0)).astype(BF16)


def spatial_forward_own(me_ref, x0, x1, x2, x3, q_r, k_r, v_r, wo, p0, p1, xrow, xs, att):
    me = me_ref[0]
    att[...] = softmax_pieces(q_r[:, half_of(me, 0)], k_r[...], v_r[...])
    for d, partial in ((1, p1), (0, p0)):
        partial[...] = dot(att[:, core_of(me, d)], wo[...], (0, 0)).astype(BF16)
    for d, x in enumerate((x0, x1, x2, x3)):
        xs[part_of(me, d), :] = x[:, own_of(me, 0)].astype(F32)
    xrow[...] = xs[...].T.astype(BF16)


def temporal_group(normed, gated, gains, weights, wo):
    n = normed.shape[0]
    left = lax.broadcasted_iota(jnp.int32, (n, n), 0)
    right = lax.broadcasted_iota(jnp.int32, (n, n), 1)
    mask = ((left & 1) == (right & 1)) & ((left // OWN) == (right // OWN))
    projected = dot(weights, normed, (1, 1))
    query, inv_q = head_norm_t(projected[:PART], gains[:, 0:1])
    key, inv_k = head_norm_t(projected[PART : 2 * PART], gains[:, 1:2])
    value = projected[2 * PART :].astype(BF16)
    grad_att = dot(wo, gated, (1, 1)).astype(BF16)
    attended, gq, gk, gv = [], [], [], []
    for h in range(PER):
        rows = slice(h * HEAD, (h + 1) * HEAD)
        q, k, v, da = query[rows], key[rows], value[rows], grad_att[rows]
        scores = dot(k, q, (0, 0))
        unnormed = jnp.where(mask, jnp.exp2(scores * (SCALE * LOG2E)), 0.0)
        probs = unnormed * (1.0 / jnp.sum(unnormed, axis=0, keepdims=True))
        rounded = probs.astype(BF16)
        attended.append(dot(v, rounded, (1, 0)))
        grad_probs = dot(v, da, (0, 0))
        inner = jnp.sum(grad_probs * probs, axis=0, keepdims=True)
        grad_scores = (probs * (grad_probs - inner)).astype(BF16)
        gv.append(dot(da, rounded, (1, 1)))
        gq.append(dot(k, grad_scores, (1, 0)) * SCALE)
        gk.append(dot(q, grad_scores, (1, 1)) * SCALE)
    attended = jnp.concatenate(attended, axis=0).astype(BF16)
    gq = jnp.concatenate(gq, axis=0).astype(BF16)
    gk = jnp.concatenate(gk, axis=0).astype(BF16)
    gv = jnp.concatenate(gv, axis=0).astype(BF16)
    dq = head_back_t(gq, query, inv_q, gains[:, 0:1])
    dk = head_back_t(gk, key, inv_k, gains[:, 1:2])
    stacked = jnp.concatenate([dq, dk, gv], axis=0)
    return dot(stacked, weights, (0, 0)), dot(attended, wo, (0, 0))


def temporal_own(x0, x1, c0, c1, modr, gains, wt, wo, gn_o, br_o, normed_o, gated_o):
    stream = jnp.concatenate([x0[...], x1[...]], axis=0).astype(F32)
    incoming = jnp.concatenate([c0[...], c1[...]], axis=0).astype(F32)
    mean = jnp.sum(stream, axis=1, keepdims=True) * (1.0 / WIDE)
    centred = stream - mean
    inverse = lax.rsqrt(jnp.sum(centred * centred, axis=1, keepdims=True) * (1.0 / WIDE) + EPS)
    normed = (centred * inverse * (1.0 + modr[1:2, :]) + modr[0:1, :]).astype(BF16)
    gated = (modr[2:3, :] * incoming).astype(BF16)
    normed_o[...] = normed
    gated_o[...] = gated
    term, branch = temporal_group(
        normed, gated, gains[...], wt[...].reshape(3 * PART, WIDE), wo[...]
    )
    gn_o[...] = term.astype(BF16)
    br_o[...] = branch.astype(BF16)


def temporal_far(
    at_ref, normed, gated, gn_r, br_r, gains, w0, w1, w2, w3, gn0, gn1, op0, op1, ws
):
    for d, w in enumerate((w0, w1, w2, w3)):
        ws[pl.ds(pl.multiple_of(((at_ref[0] + d) & 3) * PART, 32), PART), :] = w[...]
    term, branch = temporal_group(
        normed[...], gated[...], gains[...], ws[: 3 * PART, :], ws[3 * PART :, :]
    )
    term = term + gn_r[...].astype(F32)
    branch = branch + br_r[...].astype(F32)
    gn0[...] = term[:OWN]
    gn1[...] = term[OWN:].astype(BF16)
    op0[...] = branch[:OWN]
    op1[...] = branch[OWN:].astype(BF16)


def temporal_finish(x0, c0, gn0, gn1, op0, op1, modr, gm_o, mixed_o):
    stream = x0[...].astype(F32)
    mean = jnp.sum(stream, axis=1, keepdims=True) * (1.0 / WIDE)
    shifted = stream - mean
    inverse = lax.rsqrt(jnp.sum(shifted * shifted, axis=1, keepdims=True) * (1.0 / WIDE) + EPS)
    centred = shifted * inverse
    scaled = (gn0[...] + gn1[...].astype(F32)) * (1.0 + modr[1:2, :])
    first = jnp.sum(scaled, axis=1, keepdims=True) * (1.0 / WIDE)
    second = jnp.sum(scaled * centred, axis=1, keepdims=True) * (1.0 / WIDE)
    gm_o[...] = (c0[...].astype(F32) + inverse * (scaled - first - centred * second)).astype(BF16)
    mixed_o[...] = (stream + modr[2:3, :] * (op0[...] + op1[...].astype(F32))).astype(BF16)


def backward_half(queries, grad_att, k_r, v_r):
    gq, gk, gv = [], [], []
    for h in range(PER):
        rows = slice(h * HEAD, (h + 1) * HEAD)
        q, k, v, da = queries[rows], k_r[rows, :], v_r[rows, :], grad_att[rows]
        scores = dot(k, q, (0, 0))
        unnormed = jnp.exp2(scores * (SCALE * LOG2E))
        probs = unnormed * (1.0 / jnp.sum(unnormed, axis=0, keepdims=True))
        rounded = probs.astype(BF16)
        grad_probs = dot(v, da, (0, 0))
        inner = jnp.sum(grad_probs * probs, axis=0, keepdims=True)
        grad_scores = (probs * (grad_probs - inner)).astype(BF16)
        gv.append(dot(da, rounded, (1, 1)))
        gk.append(dot(q, grad_scores, (1, 1)))
        gq.append(dot(k, grad_scores, (1, 0)) * SCALE)
    return [jnp.concatenate(g, axis=0) for g in (gq, gk, gv)]


def gated_half(me, d, ga, gb, modr, rows):
    rows[core_of(me, d), :] = (modr[2:3, :] * ga[...].astype(F32)).astype(BF16)
    rows[core_of(me, d ^ 1), :] = (modr[2:3, :] * gb[...].astype(F32)).astype(BF16)
    return rows[...]


def spatial_backward_own(me_ref, g0, g1, q_r, k_r, v_r, modr, wo, gq_o, gk_o, gv_o, rows):
    me = me_ref[0]
    gated = gated_half(me, 0, g0, g1, modr, rows)
    grad_att = dot(wo[...], gated, (1, 1)).astype(BF16)
    gq, gk, gv = backward_half(q_r[:, half_of(me, 0)], grad_att, k_r, v_r)
    gq_o[...] = gq.astype(BF16)
    gk_o[...] = gk
    gv_o[...] = gv


def block_back(me, d, stacked, x, st, modc, wn, partial):
    term = dot(wn[part_of(me, d), :], stacked, (1, 0))
    partial[...] = term.astype(BF16)
    scaled = term * (1.0 + modc[part_of(me, d), 1:2])
    centred = (x[...].astype(F32) - st[8:9, :]) * st[9:10, :]
    return (
        jnp.sum(scaled, axis=0, keepdims=True),
        jnp.sum(scaled * centred, axis=0, keepdims=True),
    )


def spatial_backward_far(
    me_ref, g2, g3, x2, x3, q_r, k_r, v_r, st, gq_r, gk_r, gv_r, modr, modc, gains, wo, wn,
    p2, p3, stacked_o, rs_o, rows, gq_s,
):
    me = me_ref[0]
    gated = gated_half(me, 2, g2, g3, modr, rows)
    grad_att = dot(wo[...], gated, (1, 1)).astype(BF16)
    gq, gk, gv = backward_half(q_r[:, half_of(me, 1)], grad_att, k_r, v_r)
    gq_s[:, half_of(me, 0)] = gq_r[...]
    gq_s[:, half_of(me, 1)] = gq.astype(BF16)
    gk = ((gk + gk_r[...]) * SCALE).astype(BF16)
    inv_q = st[0:4, :].reshape(PER, 1, ROWS)
    inv_k = st[4:8, :].reshape(PER, 1, ROWS)
    stacked_o[:PART, :] = head_back_t(gq_s[...], q_r[...], inv_q, gains[:, 0:1])
    stacked_o[PART : 2 * PART, :] = head_back_t(gk, k_r[...], inv_k, gains[:, 1:2])
    stacked_o[2 * PART :, :] = (gv + gv_r[...]).astype(BF16)
    stacked = stacked_o[...]
    first, second = block_back(me, 3, stacked, x3, st, modc, wn, p3)
    more, again = block_back(me, 2, stacked, x2, st, modc, wn, p2)
    rs_o[...] = jnp.zeros_like(rs_o)
    rs_o[0:1, :] = first + more
    rs_o[1:2, :] = second + again


def spatial_backward_last(
    me_ref, stacked_r, x0, x1, st, rs_r, modc, wn, g0, g1, g2, g3, p0, p1, rs_o, gown, rows
):
    me = me_ref[0]
    stacked = stacked_r[...]
    first, second = block_back(me, 1, stacked, x1, st, modc, wn, p1)
    more, again = block_back(me, 0, stacked, x0, st, modc, wn, p0)
    rs_o[...] = jnp.zeros_like(rs_o)
    rs_o[0:1, :] = rs_r[0:1, :] + first + more
    rs_o[1:2, :] = rs_r[1:2, :] + second + again
    for d, g in enumerate((g0, g1, g2, g3)):
        rows[...] = g[...].astype(F32).T
        gown[:, own_of(me, d)] = rows[part_of(me, 0), :].astype(BF16)


def spatial_finish(me_ref, p0, m1, o2, rs, st, x0, gown, modc, out_o):
    grad = p0[...].astype(F32) + m1[...].astype(F32) + o2[...].astype(F32)
    inverse = st[9:10, :]
    scaled = grad * (1.0 + modc[part_of(me_ref[0], 0), 1:2])
    centred = (x0[...].astype(F32) - st[8:9, :]) * inverse
    first = rs[0:1, :] * (1.0 / WIDE)
    second = rs[1:2, :] * (1.0 / WIDE)
    out_o[...] = (gown[...].astype(F32) + inverse * (scaled - first - centred * second)).astype(BF16)


def gather_rows(me_ref, c0, c1, c2, c3, rows_o, cs):
    me = me_ref[0]
    for d, c in enumerate((c0, c1, c2, c3)):
        cs[part_of(me, d), :] = c[...].astype(F32)
    rows_o[...] = cs[...].T.astype(BF16)


def split_rows(me_ref, rows, c0, c1, c2, c3, cs):
    me = me_ref[0]
    cs[...] = rows[...].astype(F32).T
    for d, c in enumerate((c0, c1, c2, c3)):
        c[...] = cs[part_of(me, d), :].astype(BF16)


def place_columns(me_ref, c0, c1, c2, c3, out_o):
    me = me_ref[0]
    for d, c in enumerate((c0, c1, c2, c3)):
        out_o[:, own_of(me, d)] = c[...]


def swap(values, d):
    return lax.ppermute(values, "head", [(i, i ^ d) for i in range(4)])


def after(values, *others):
    return lax.optimization_barrier((values, *others))[0]


def across_seq(one, two):
    rows = jnp.concatenate([v.reshape(64, 2, WIDE) for v in (one, two)], axis=1)
    moved = lax.all_to_all(rows, "seq", split_axis=0, concat_axis=0, tiled=True)
    return moved[:, :2].reshape(OWN, WIDE), moved[:, 2:].reshape(OWN, WIDE)


def weights_of_other(chunks, at):
    mine = lax.dynamic_index_in_dim(chunks, at, 0, keepdims=False)
    index = [(s, h) for s in range(64) for h in range(4)]
    near = [(s * 4 + h, (s ^ 4) * 4 + (h ^ 2)) for s, h in index]
    mine = lax.ppermute(mine, ("seq", "head"), near)
    ring = [mine]
    for d in (1, 2, 3):
        pairs = [((s // 4 * 4 + (s + d) % 4), s) for s in range(64)]
        ring.append(lax.ppermute(mine, "seq", pairs))
    return ring


def on_device(tokens, cotangent, qkv_weight, out_weight, modulation, head_gains):
    me = lax.axis_index("head")
    mine = me.astype(jnp.int32).reshape(1)
    at = (lax.axis_index("seq") & 3).astype(jnp.int32)
    wt = jnp.transpose(qkv_weight, (0, 2, 3, 1))
    modc = jnp.pad(modulation.transpose(2, 0, 1).reshape(WIDE, 6), ((0, 0), (0, 2)))
    gains = jnp.tile(head_gains.reshape(4, HEAD).T, (PER, 1))
    gains = jnp.pad(gains, ((0, 0), (0, 4)), constant_values=1.0)
    gains_s, gains_t = gains[:, 0:2], gains[:, 2:4]
    row = out((OWN, WIDE))
    col = out((PART, ROWS))
    piece = out((PART, OWN))

    x0 = tokens.T
    x2 = swap(x0, 2)
    x1 = swap(x0, 1)
    x3 = swap(x2, 1)

    cot = after(cotangent.T, x2)
    parts = [lax.dynamic_slice_in_dim(cot, (me ^ d) * OWN, OWN, axis=1) for d in range(4)]
    parts = [parts[0]] + [swap(parts[d], d) for d in (1, 2, 3)]
    chunks = jnp.concatenate([wt[1], out_weight[1:2]], axis=0)
    others = weights_of_other(after(chunks, x2), at)

    query, key, value, stats, p2, p3 = call(
        spatial_forward,
        [col] * 3 + [out((16, ROWS), F32)] + [row] * 2,
        [mine, x0, x1, x2, x3, modc, gains_s, wt[0], out_weight[0]],
        [pltpu.VMEM((WIDE, ROWS), BF16), pltpu.VMEM((PART, 2 * OWN), BF16)],
        flops=2 * 10**9, smem=1,
    )
    m3 = swap(p3, 1)
    chip = (p2.astype(F32) + m3.astype(F32)).astype(BF16)
    far = swap(chip, 2)
    p0, p1, xrow = call(
        spatial_forward_own, [row] * 3,
        [mine, x0, x1, x2, x3, after(query, chip), key, value, out_weight[0]],
        [pltpu.VMEM((WIDE, OWN), F32), pltpu.VMEM((PART, 2 * OWN), BF16)],
        flops=10**9, smem=1,
    )
    m1 = swap(p1, 1)
    parts[0] = after(parts[0], p1)
    (cot0,) = call(
        gather_rows, [row], [mine, *parts], [pltpu.VMEM((WIDE, OWN), F32)], smem=1
    )

    branch = p0.astype(F32) + m1.astype(F32) + far.astype(F32)
    middle = (xrow.astype(F32) + modulation[0, 2][None] * branch).astype(BF16)

    t0, cot0 = across_seq(middle, cot0)
    t1, cot1 = swap(t0, 1), swap(cot0, 1)
    gn, br, normed, gated = call(
        temporal_own, [out((2 * OWN, WIDE))] * 4,
        [t0, t1, cot0, cot1, modulation[1], gains_t, wt[1], out_weight[1]],
        flops=2 * 10**9,
    )
    gn0, gn1, op0, op1 = call(
        temporal_far,
        [out((OWN, WIDE), F32), row, out((OWN, WIDE), F32), row],
        [at.reshape(1), normed, gated, gn, br, gains_t, *others],
        [pltpu.VMEM((4 * PART, WIDE), BF16)],
        flops=2 * 10**9, smem=1,
    )
    gn1, op1 = swap(gn1, 1), swap(op1, 1)
    grad_middle, mixed_rows = call(
        temporal_finish, [row] * 2, [t0, cot0, gn0, gn1, op0, op1, modulation[1]]
    )

    g0, mixed_rows = across_seq(grad_middle, mixed_rows)
    g2 = swap(g0, 2)
    g1 = swap(g0, 1)
    g3 = swap(g2, 1)

    wn = qkv_weight[0].reshape(WIDE, 3 * PART)
    gq, gk, gv = call(
        spatial_backward_own,
        [out((PART, 2 * OWN)), out((PART, ROWS), F32), out((PART, ROWS), F32)],
        [mine, g0, g1, query, key, value, modulation[0], out_weight[0]],
        [pltpu.VMEM((2 * OWN, WIDE), BF16)],
        flops=2 * 10**9, smem=1,
    )
    p2, p3, stacked, sums = call(
        spatial_backward_far,
        [col, col, out((3 * PART, ROWS)), out((8, ROWS), F32)],
        [mine, g2, g3, x2, x3, query, key, value, stats, gq, gk, gv, modulation[0], modc,
         gains_s, out_weight[0], wn],
        [pltpu.VMEM((2 * OWN, WIDE), BF16), pltpu.VMEM((PART, ROWS), BF16)],
        flops=3 * 10**9, smem=1,
    )
    m3 = swap(p3, 1)
    chip = (p2.astype(F32) + m3.astype(F32)).astype(BF16)
    far = swap(chip, 2)
    p0, p1, sums, gown = call(
        spatial_backward_last,
        [col, col, out((8, ROWS), F32), col],
        [mine, after(stacked, chip), x0, x1, stats, sums, modc, wn, g0, g1, g2, g3],
        [pltpu.VMEM((WIDE, OWN), F32)],
        flops=10**9, smem=1,
    )
    m1 = swap(p1, 1)
    sums = sums + swap(sums, 1)
    sums = sums + swap(sums, 2)

    parts = call(
        split_rows, [piece] * 4, [mine, mixed_rows], [pltpu.VMEM((WIDE, OWN), F32)], smem=1
    )
    parts = [parts[0]] + [swap(parts[d], d) for d in (1, 2, 3)]
    (mixed,) = call(place_columns, [col], [mine, *parts], smem=1)

    (grad,) = call(
        spatial_finish, [col], [mine, p0, m1, far, sums, stats, x0, gown, modc], smem=1
    )
    return (mixed.T, grad.T)


def solution(mesh):
    in_specs = (
        P("seq", "head"),
        P("seq", "head"),
        P(None, None, None, "head"),
        P(None, "head", None),
        P(),
        P(),
    )
    out_specs = (P("seq", "head"), P("seq", "head"))
    return jax.shard_map(
        on_device, mesh=mesh, in_specs=in_specs, out_specs=out_specs, check_vma=False
    )
```

```python
import jax
import jax.numpy as jnp
from jax import lax
from jax.experimental import pallas as pl
from jax.experimental.pallas import tpu as pltpu
from jax.sharding import PartitionSpec as P

EPS = 1e-06
HEAD = 72
PER = 4
WIDE = 1152
PART = 288
ROWS = 512
OWN = 128
LOG2E = 1.4426950408889634
SCALE = HEAD**-0.5
F32 = jnp.float32
BF16 = jnp.bfloat16
VMEM_LIMIT = 56 * 1024 * 1024


def dot(a, b, over):
    return lax.dot_general(a, b, (((over[0],), (over[1],)), ((), ())), preferred_element_type=F32)


def call(body, outs, operands, scratch=(), smem=0, behind=()):
    n, skip = len(operands), len(behind)
    specs = [
        pl.BlockSpec(memory_space=pltpu.SMEM) if i < smem else pl.BlockSpec(memory_space=pltpu.VMEM)
        for i in range(n)
    ]
    specs += [pl.BlockSpec(memory_space=pl.ANY)] * skip

    def run(*refs):
        body(*refs[:n], *refs[n + skip :])

    return pl.pallas_call(
        run,
        out_shape=list(outs),
        in_specs=specs,
        out_specs=[pl.BlockSpec(memory_space=pltpu.VMEM)] * len(outs),
        scratch_shapes=list(scratch),
        compiler_params=pltpu.CompilerParams(vmem_limit_bytes=VMEM_LIMIT),
        cost_estimate=pl.CostEstimate(flops=1, bytes_accessed=1, transcendentals=0),
    )(*operands, *behind)


def out(shape, dtype=BF16):
    return jax.ShapeDtypeStruct(shape, dtype)


def head_norm_t(part, gains):
    n = part.shape[1]
    cube = part.reshape(PER, HEAD, n)
    inverse = lax.rsqrt(jnp.sum(cube * cube, axis=1, keepdims=True) * (1.0 / HEAD) + EPS)
    return (cube * inverse * gains.reshape(PER, HEAD, 1)).reshape(PART, n).astype(BF16), inverse


def head_back_t(incoming, normed, inverse, gains):
    n = incoming.shape[1]
    grad = incoming.astype(F32).reshape(PER, HEAD, n)
    norm = normed.astype(F32).reshape(PER, HEAD, n)
    gain = gains.reshape(PER, HEAD, 1)
    inner = jnp.sum(norm * grad, axis=1, keepdims=True) * (1.0 / HEAD)
    return (inverse * (gain * grad - norm * (1.0 / gain) * inner)).reshape(PART, n).astype(BF16)


def gain_columns(gains, block, square):
    square[...] = jnp.zeros_like(square)
    square[0:2, 0:HEAD] = gains[block]
    turned = square[...].T
    return [jnp.concatenate([turned[:HEAD, i : i + 1]] * PER, axis=0) for i in range(2)]


def softmax_pieces(query, key, value):
    pieces = []
    for h in range(PER):
        rows = slice(h * HEAD, (h + 1) * HEAD)
        scores = dot(key[rows], query[rows], (0, 0))
        unnormed = jnp.exp2(scores * (SCALE * LOG2E))
        total = jnp.sum(unnormed, axis=0, keepdims=True)
        pieces.append(dot(value[rows], unnormed.astype(BF16), (1, 0)) * (1.0 / total))
    return jnp.concatenate(pieces, axis=0).astype(BF16)


def half_of(me, other):
    return pl.ds(pl.multiple_of(((me // 2) ^ other) * 2 * OWN, 2 * OWN), 2 * OWN)


def core_of(me, d):
    return pl.ds(pl.multiple_of(((me ^ d) & 1) * OWN, OWN), OWN)


def part_of(me, d):
    return pl.ds(pl.multiple_of((me ^ d) * PART, 32), PART)


def own_of(me, d):
    return pl.ds(pl.multiple_of((me ^ d) * OWN, OWN), OWN)


def spatial_forward(
    me_ref, x0, x1, x2, x3, mod, gains, wt, wo, q_o, k_o, v_o, st_o, p2, p3, modc, xs, att, lines,
    square,
):
    me = me_ref[0]
    gain_q, gain_k = gain_columns(gains, 0, square)
    lines[...] = jnp.zeros_like(lines)
    for i in range(3):
        lines[i : i + 1, :] = mod[i, 0:1, :]
    modc[...] = lines[...].T
    for d, x in enumerate((x0, x1, x2, x3)):
        xs[part_of(me, d), :] = x[...]
    stream = xs[...].astype(F32)
    mean = jnp.sum(stream, axis=0, keepdims=True) * (1.0 / WIDE)
    centred = stream - mean
    inverse = lax.rsqrt(jnp.sum(centred * centred, axis=0, keepdims=True) * (1.0 / WIDE) + EPS)
    normed = (centred * inverse * (1.0 + modc[:, 1:2]) + modc[:, 0:1]).astype(BF16)
    projected = dot(wt[...].reshape(3 * PART, WIDE), normed, (1, 0))
    query, inv_q = head_norm_t(projected[:PART], gain_q)
    key, inv_k = head_norm_t(projected[PART : 2 * PART], gain_k)
    q_o[...] = query
    k_o[...] = key
    v_o[...] = projected[2 * PART :].astype(BF16)
    st_o[0:4, :] = inv_q.reshape(PER, ROWS)
    st_o[4:8, :] = inv_k.reshape(PER, ROWS)
    st_o[8:9, :] = mean
    st_o[9:10, :] = inverse
    att[...] = softmax_pieces(q_o[:, half_of(me, 1)], k_o[...], v_o[...])
    for d, partial in ((3, p3), (2, p2)):
        partial[...] = dot(att[:, core_of(me, d)], wo[...], (0, 0)).astype(BF16)


def spatial_forward_own(
    me_ref, x0, x1, x2, x3, q_r, k_r, v_r, wo, wt, p0, p1, xrow, wn_o, xs, att
):
    me = me_ref[0]
    att[...] = softmax_pieces(q_r[:, half_of(me, 0)], k_r[...], v_r[...])
    for d, partial in ((1, p1), (0, p0)):
        partial[...] = dot(att[:, core_of(me, d)], wo[...], (0, 0)).astype(BF16)
    for d, x in enumerate((x0, x1, x2, x3)):
        xs[part_of(me, d), :] = x[:, own_of(me, 0)].astype(F32)
    xrow[...] = xs[...].T.astype(BF16)
    wn_o[...] = wt[...].reshape(3 * PART, WIDE).T


def temporal_group(normed, gated, gain_q, gain_k, weights, wo):
    n = normed.shape[0]
    left = lax.broadcasted_iota(jnp.int32, (n, n), 0)
    right = lax.broadcasted_iota(jnp.int32, (n, n), 1)
    mask = ((left & 1) == (right & 1)) & ((left // OWN) == (right // OWN))
    projected = dot(weights, normed, (1, 1))
    query, inv_q = head_norm_t(projected[:PART], gain_q)
    key, inv_k = head_norm_t(projected[PART : 2 * PART], gain_k)
    value = projected[2 * PART :].astype(BF16)
    grad_att = dot(wo, gated, (1, 1)).astype(BF16)
    attended, gq, gk, gv = [], [], [], []
    for h in range(PER):
        rows = slice(h * HEAD, (h + 1) * HEAD)
        q, k, v, da = query[rows], key[rows], value[rows], grad_att[rows]
        scores = dot(k, q, (0, 0))
        unnormed = jnp.where(mask, jnp.exp2(scores * (SCALE * LOG2E)), 0.0)
        probs = unnormed * (1.0 / jnp.sum(unnormed, axis=0, keepdims=True))
        rounded = probs.astype(BF16)
        attended.append(dot(v, rounded, (1, 0)))
        grad_probs = dot(v, da, (0, 0))
        inner = jnp.sum(grad_probs * probs, axis=0, keepdims=True)
        grad_scores = (probs * (grad_probs - inner)).astype(BF16)
        gv.append(dot(da, rounded, (1, 1)))
        gq.append(dot(k, grad_scores, (1, 0)) * SCALE)
        gk.append(dot(q, grad_scores, (1, 1)) * SCALE)
    attended = jnp.concatenate(attended, axis=0).astype(BF16)
    gq = jnp.concatenate(gq, axis=0).astype(BF16)
    gk = jnp.concatenate(gk, axis=0).astype(BF16)
    gv = jnp.concatenate(gv, axis=0).astype(BF16)
    dq = head_back_t(gq, query, inv_q, gain_q)
    dk = head_back_t(gk, key, inv_k, gain_k)
    stacked = jnp.concatenate([dq, dk, gv], axis=0)
    return dot(stacked, weights, (0, 0)), dot(attended, wo, (0, 0))


def temporal_own(x0, x1, c0, c1, mod, gains, wt, wo, gn_o, br_o, normed_o, gated_o, square):
    stream = jnp.concatenate([x0[...], x1[...]], axis=0).astype(F32)
    incoming = jnp.concatenate([c0[...], c1[...]], axis=0).astype(F32)
    mean = jnp.sum(stream, axis=1, keepdims=True) * (1.0 / WIDE)
    centred = stream - mean
    inverse = lax.rsqrt(jnp.sum(centred * centred, axis=1, keepdims=True) * (1.0 / WIDE) + EPS)
    normed = (centred * inverse * (1.0 + mod[1, 1:2, :]) + mod[0, 1:2, :]).astype(BF16)
    gated = (mod[2, 1:2, :] * incoming).astype(BF16)
    normed_o[...] = normed
    gated_o[...] = gated
    term, branch = temporal_group(
        normed, gated, *gain_columns(gains, 1, square), wt[...].reshape(3 * PART, WIDE), wo[...]
    )
    gn_o[...] = term.astype(BF16)
    br_o[...] = branch.astype(BF16)


def temporal_far(
    at_ref, normed, gated, gn_r, br_r, gains, w0, w1, w2, w3, gn0, gn1, op0, op1, ws, square
):
    for d, w in enumerate((w0, w1, w2, w3)):
        ws[pl.ds(pl.multiple_of(((at_ref[0] + d) & 3) * PART, 32), PART), :] = w[...]
    term, branch = temporal_group(
        normed[...],
        gated[...],
        *gain_columns(gains, 1, square),
        ws[: 3 * PART, :],
        ws[3 * PART :, :],
    )
    term = term + gn_r[...].astype(F32)
    branch = branch + br_r[...].astype(F32)
    gn0[...] = term[:OWN]
    gn1[...] = term[OWN:].astype(BF16)
    op0[...] = branch[:OWN]
    op1[...] = branch[OWN:].astype(BF16)


def temporal_finish(x0, c0, gn0, gn1, op0, op1, mod, gm_o, mixed_o):
    stream = x0[...].astype(F32)
    mean = jnp.sum(stream, axis=1, keepdims=True) * (1.0 / WIDE)
    shifted = stream - mean
    inverse = lax.rsqrt(jnp.sum(shifted * shifted, axis=1, keepdims=True) * (1.0 / WIDE) + EPS)
    centred = shifted * inverse
    scaled = (gn0[...] + gn1[...].astype(F32)) * (1.0 + mod[1, 1:2, :])
    first = jnp.sum(scaled, axis=1, keepdims=True) * (1.0 / WIDE)
    second = jnp.sum(scaled * centred, axis=1, keepdims=True) * (1.0 / WIDE)
    gm_o[...] = (c0[...].astype(F32) + inverse * (scaled - first - centred * second)).astype(BF16)
    mixed_o[...] = (stream + mod[2, 1:2, :] * (op0[...] + op1[...].astype(F32))).astype(BF16)


def backward_half(queries, grad_att, k_r, v_r):
    gq, gk, gv = [], [], []
    for h in range(PER):
        rows = slice(h * HEAD, (h + 1) * HEAD)
        q, k, v, da = queries[rows], k_r[rows, :], v_r[rows, :], grad_att[rows]
        scores = dot(k, q, (0, 0))
        unnormed = jnp.exp2(scores * (SCALE * LOG2E))
        probs = unnormed * (1.0 / jnp.sum(unnormed, axis=0, keepdims=True))
        rounded = probs.astype(BF16)
        grad_probs = dot(v, da, (0, 0))
        inner = jnp.sum(grad_probs * probs, axis=0, keepdims=True)
        grad_scores = (probs * (grad_probs - inner)).astype(BF16)
        gv.append(dot(da, rounded, (1, 1)))
        gk.append(dot(q, grad_scores, (1, 1)))
        gq.append(dot(k, grad_scores, (1, 0)) * SCALE)
    return [jnp.concatenate(g, axis=0) for g in (gq, gk, gv)]


def gated_half(me, d, ga, gb, mod, rows):
    rows[core_of(me, d), :] = (mod[2, 0:1, :] * ga[...].astype(F32)).astype(BF16)
    rows[core_of(me, d ^ 1), :] = (mod[2, 0:1, :] * gb[...].astype(F32)).astype(BF16)
    return rows[...]


def spatial_backward_own(
    me_ref, g0, g1, q_r, k_r, v_r, mod, wo, gq_o, gk_o, gv_o, rows
):
    me = me_ref[0]
    gated = gated_half(me, 0, g0, g1, mod, rows)
    grad_att = dot(wo[...], gated, (1, 1)).astype(BF16)
    gq, gk, gv = backward_half(q_r[:, half_of(me, 0)], grad_att, k_r, v_r)
    gq_o[...] = gq.astype(BF16)
    gk_o[...] = gk
    gv_o[...] = gv


def block_back(me, d, stacked, x, st, modc, wn, partial):
    term = dot(wn[part_of(me, d), :], stacked, (1, 0))
    partial[...] = term.astype(BF16)
    scaled = term * (1.0 + modc[part_of(me, d), 1:2])
    centred = (x[...].astype(F32) - st[8:9, :]) * st[9:10, :]
    return (
        jnp.sum(scaled, axis=0, keepdims=True),
        jnp.sum(scaled * centred, axis=0, keepdims=True),
    )


def spatial_backward_far(
    me_ref, g2, g3, x2, x3, q_r, k_r, v_r, st, gq_r, gk_r, gv_r, mod, modc, gains, wo, wn,
    p2, p3, stacked_o, rs_o, rows, gq_s, square,
):
    me = me_ref[0]
    gated = gated_half(me, 2, g2, g3, mod, rows)
    grad_att = dot(wo[...], gated, (1, 1)).astype(BF16)
    gq, gk, gv = backward_half(q_r[:, half_of(me, 1)], grad_att, k_r, v_r)
    gain_q, gain_k = gain_columns(gains, 0, square)
    gq_s[:, half_of(me, 0)] = gq_r[...]
    gq_s[:, half_of(me, 1)] = gq.astype(BF16)
    gk = ((gk + gk_r[...]) * SCALE).astype(BF16)
    inv_q = st[0:4, :].reshape(PER, 1, ROWS)
    inv_k = st[4:8, :].reshape(PER, 1, ROWS)
    stacked_o[:PART, :] = head_back_t(gq_s[...], q_r[...], inv_q, gain_q)
    stacked_o[PART : 2 * PART, :] = head_back_t(gk, k_r[...], inv_k, gain_k)
    stacked_o[2 * PART :, :] = (gv + gv_r[...]).astype(BF16)
    stacked = stacked_o[...]
    first, second = block_back(me, 3, stacked, x3, st, modc, wn, p3)
    more, again = block_back(me, 2, stacked, x2, st, modc, wn, p2)
    rs_o[...] = jnp.zeros_like(rs_o)
    rs_o[0:1, :] = first + more
    rs_o[1:2, :] = second + again


def spatial_backward_last(
    me_ref, stacked_r, x0, x1, st, rs_r, modc, wn, g0, g1, g2, g3, p0, p1, rs_o, gown, rows
):
    me = me_ref[0]
    stacked = stacked_r[...]
    first, second = block_back(me, 1, stacked, x1, st, modc, wn, p1)
    more, again = block_back(me, 0, stacked, x0, st, modc, wn, p0)
    rs_o[...] = jnp.zeros_like(rs_o)
    rs_o[0:1, :] = rs_r[0:1, :] + first + more
    rs_o[1:2, :] = rs_r[1:2, :] + second + again
    for d, g in enumerate((g0, g1, g2, g3)):
        rows[...] = g[...].astype(F32).T
        gown[:, own_of(me, d)] = rows[part_of(me, 0), :].astype(BF16)


def spatial_finish(me_ref, p0, m1, o2, rs, st, x0, gown, modc, out_o):
    grad = p0[...].astype(F32) + m1[...].astype(F32) + o2[...].astype(F32)
    inverse = st[9:10, :]
    scaled = grad * (1.0 + modc[part_of(me_ref[0], 0), 1:2])
    centred = (x0[...].astype(F32) - st[8:9, :]) * inverse
    first = rs[0:1, :] * (1.0 / WIDE)
    second = rs[1:2, :] * (1.0 / WIDE)
    out_o[...] = (gown[...].astype(F32) + inverse * (scaled - first - centred * second)).astype(BF16)


def split_columns(me_ref, columns, c0, c1, c23):
    me = me_ref[0]
    c0[...] = columns[:, own_of(me, 0)]
    c1[...] = columns[:, own_of(me, 1)]
    c23[:PART, :] = columns[:, own_of(me, 2)]
    c23[PART:, :] = columns[:, own_of(me, 3)]


def place_columns(me_ref, c0, c1, c2, c3, out_o):
    me = me_ref[0]
    for d, c in enumerate((c0[...], c1[...], c2[:PART, :], c3[PART:, :])):
        out_o[:, own_of(me, d)] = c


def gather_rows(me_ref, c0, c1, c2, c3, rows_o, cs):
    me = me_ref[0]
    for d, c in enumerate((c0[...], c1[...], c2[:PART, :], c3[PART:, :])):
        cs[part_of(me, d), :] = c.astype(F32)
    rows_o[...] = cs[...].T.astype(BF16)


def split_rows(me_ref, rows, c0, c1, c23, cs):
    me = me_ref[0]
    cs[...] = rows[...].astype(F32).T
    c0[...] = cs[part_of(me, 0), :].astype(BF16)
    c1[...] = cs[part_of(me, 1), :].astype(BF16)
    c23[:PART, :] = cs[part_of(me, 2), :].astype(BF16)
    c23[PART:, :] = cs[part_of(me, 3), :].astype(BF16)


def swap(values, d):
    return lax.ppermute(values, "head", [(i, i ^ d) for i in range(4)])


def swap_halves(values):
    half = values.shape[0] // 2
    return jnp.concatenate([swap(values[:half], 1), swap(values[half:], 1)], axis=0)


def exchange(parts):
    mine, mate, both = parts
    far = swap(both, 2)
    return [mine, swap(mate, 1), far, swap(far, 1)]


def across_seq(one, two):
    rows = jnp.concatenate([v.reshape(64, 2, WIDE) for v in (one, two)], axis=1)
    moved = lax.all_to_all(rows, "seq", split_axis=0, concat_axis=0, tiled=True)
    return moved[:, :2].reshape(OWN, WIDE), moved[:, 2:].reshape(OWN, WIDE)


def from_neighbour(chunk):
    index = [(s, h) for s in range(64) for h in range(4)]
    near = [(s * 4 + h, (s ^ 4) * 4 + (h ^ 2)) for s, h in index]
    return lax.ppermute(chunk, ("seq", "head"), near)


def round_x(chunk, d):
    return lax.ppermute(chunk, "seq", [(s // 4 * 4 + (s + d) % 4, s) for s in range(64)])


def on_device(tokens, cotangent, qkv_weight, out_weight, modulation, head_gains):
    me = lax.axis_index("head")
    mine = me.astype(jnp.int32).reshape(1)
    at = (lax.axis_index("seq") & 3).astype(jnp.int32)
    wt = jnp.transpose(qkv_weight, (0, 2, 3, 1))
    mod = jnp.transpose(modulation, (1, 0, 2))
    row = out((OWN, WIDE))
    col = out((PART, ROWS))
    piece = out((PART, OWN))
    square = pltpu.VMEM((8, 128), F32)

    x0 = tokens.T
    x2 = swap(x0, 2)
    x1 = swap(x0, 1)
    pieces = [piece, piece, out((2 * PART, OWN))]
    parts = call(split_columns, pieces, [mine, cotangent.T], smem=1)
    chunk = lax.select_n(at, wt[1, 0], wt[1, 1], wt[1, 2], out_weight[1])
    x2, chunk, *parts = lax.optimization_barrier((x2, chunk, *parts))
    x3 = swap(x2, 1)
    parts = exchange(parts)
    near = from_neighbour(chunk)
    others = [near] + [round_x(near, d) for d in (1, 2, 3)]

    query, key, value, stats, p2, p3, modc = call(
        spatial_forward,
        [col] * 3 + [out((16, ROWS), F32)] + [row] * 2 + [out((WIDE, 8), F32)],
        [mine, x0, x1, x2, x3, mod, head_gains, wt[0], out_weight[0]],
        [pltpu.VMEM((WIDE, ROWS), BF16), pltpu.VMEM((PART, 2 * OWN), BF16),
         pltpu.VMEM((8, WIDE), F32), square],
        smem=1,
    )
    m3 = swap(p3, 1)
    m3, *parts = lax.optimization_barrier((m3, *parts))
    chip = (p2.astype(F32) + m3.astype(F32)).astype(BF16)
    far = swap(chip, 2)
    p0, p1, xrow, wn = call(
        spatial_forward_own, [row] * 3 + [out((WIDE, 3 * PART))],
        [mine, x0, x1, x2, x3, query, key, value, out_weight[0], wt[0]],
        [pltpu.VMEM((WIDE, OWN), F32), pltpu.VMEM((PART, 2 * OWN), BF16)],
        smem=1, behind=[chip, swap(near[:16], 1)],
    )
    m1 = swap_halves(p1)
    (cot0,) = call(
        gather_rows, [row], [mine, *parts], [pltpu.VMEM((WIDE, OWN), F32)], smem=1, behind=[p1]
    )

    branch = p0.astype(F32) + m1.astype(F32) + far.astype(F32)
    middle = (xrow.astype(F32) + modulation[0, 2][None] * branch).astype(BF16)

    t0, cot0 = across_seq(middle, cot0)
    t1, cot1 = swap(t0, 1), swap(cot0, 1)
    gn, br, normed, gated = call(
        temporal_own, [out((2 * OWN, WIDE))] * 4,
        [t0, t1, cot0, cot1, mod, head_gains, wt[1], out_weight[1]],
        [square],
    )
    gn0, gn1, op0, op1 = call(
        temporal_far,
        [out((OWN, WIDE), F32), row, out((OWN, WIDE), F32), row],
        [at.reshape(1), normed, gated, gn, br, head_gains, *others],
        [pltpu.VMEM((4 * PART, WIDE), BF16), square],
        smem=1,
    )
    gn1, op1 = swap(gn1, 1), swap(op1, 1)
    grad_middle, mixed_rows = call(
        temporal_finish, [row] * 2, [t0, cot0, gn0, gn1, op0, op1, mod]
    )

    g0, mixed_rows = across_seq(grad_middle, mixed_rows)
    g2 = swap(g0, 2)
    g1 = swap(g0, 1)
    gq, gk, gv = call(
        spatial_backward_own,
        [out((PART, 2 * OWN)), out((PART, ROWS), F32), out((PART, ROWS), F32)],
        [mine, g0, g1, query, key, value, mod, out_weight[0]],
        [pltpu.VMEM((2 * OWN, WIDE), BF16)],
        smem=1,
    )
    parts = call(
        split_rows, pieces, [mine, mixed_rows], [pltpu.VMEM((WIDE, OWN), F32)], smem=1
    )
    g2, gq, *parts = lax.optimization_barrier((g2, gq, *parts))
    g3 = swap(g2, 1)
    parts = exchange(parts)
    p2, p3, stacked, sums = call(
        spatial_backward_far,
        [col, col, out((3 * PART, ROWS)), out((8, ROWS), F32)],
        [mine, g2, g3, x2, x3, query, key, value, stats, gq, gk, gv, mod, modc,
         head_gains, out_weight[0], wn],
        [pltpu.VMEM((2 * OWN, WIDE), BF16), pltpu.VMEM((PART, ROWS), BF16), square],
        smem=1,
    )
    m3, *parts = lax.optimization_barrier((swap(p3, 1), *parts))
    chip = (p2.astype(F32) + m3.astype(F32)).astype(BF16)
    far = swap(chip, 2)
    p0, p1, sums, gown = call(
        spatial_backward_last,
        [col, col, out((8, ROWS), F32), col],
        [mine, stacked, x0, x1, stats, sums, modc, wn, g0, g1, g2, g3],
        [pltpu.VMEM((WIDE, OWN), F32)],
        smem=1,
        behind=[chip],
    )
    m1 = swap_halves(p1)
    sums = sums + swap(sums, 1)
    sums = sums + swap(sums, 2)

    (mixed,) = call(place_columns, [col], [mine, *parts], smem=1, behind=[p1])

    (grad,) = call(
        spatial_finish, [col], [mine, p0, m1, far, sums, stats, x0, gown, modc], smem=1
    )
    return (mixed.T, grad.T)


def solution(mesh):
    in_specs = (
        P("seq", "head"),
        P("seq", "head"),
        P(None, None, None, "head"),
        P(None, "head", None),
        P(),
        P(),
    )
    out_specs = (P("seq", "head"), P("seq", "head"))
    return jax.shard_map(
        on_device, mesh=mesh, in_specs=in_specs, out_specs=out_specs, check_vma=False
    )
```

```python
import jax
import jax.numpy as jnp
from jax import lax
from jax.experimental import pallas as pl
from jax.experimental.pallas import tpu as pltpu
from jax.sharding import PartitionSpec as P

EPS = 1e-06
HEAD = 72
PER = 4
WIDE = 1152
PART = 288
ROWS = 512
OWN = 128
LOG2E = 1.4426950408889634
SCALE = HEAD**-0.5
F32 = jnp.float32
BF16 = jnp.bfloat16
VMEM_LIMIT = 56 * 1024 * 1024


def dot(a, b, over):
    return lax.dot_general(a, b, (((over[0],), (over[1],)), ((), ())), preferred_element_type=F32)


def call(body, outs, operands, scratch=(), smem=0, behind=()):
    n, skip = len(operands), len(behind)
    specs = [
        pl.BlockSpec(memory_space=pltpu.SMEM if i < smem else pltpu.VMEM) for i in range(n)
    ] + [pl.BlockSpec(memory_space=pl.ANY)] * skip

    def run(*refs):
        body(*refs[:n], *refs[n + skip :])

    return pl.pallas_call(
        run,
        out_shape=list(outs),
        in_specs=specs,
        out_specs=[pl.BlockSpec(memory_space=pltpu.VMEM)] * len(outs),
        scratch_shapes=list(scratch),
        compiler_params=pltpu.CompilerParams(vmem_limit_bytes=VMEM_LIMIT),
        cost_estimate=pl.CostEstimate(flops=1, bytes_accessed=1, transcendentals=0),
    )(*operands, *behind)


def out(shape, dtype=BF16):
    return jax.ShapeDtypeStruct(shape, dtype)


def head_norm_t(part, gains):
    n = part.shape[1]
    cube = part.reshape(PER, HEAD, n)
    inverse = lax.rsqrt(jnp.sum(cube * cube, axis=1, keepdims=True) * (1.0 / HEAD) + EPS)
    return (cube * inverse * gains.reshape(PER, HEAD, 1)).reshape(PART, n).astype(BF16), inverse


def head_back_t(incoming, normed, inverse, gains):
    n = incoming.shape[1]
    grad = incoming.astype(F32).reshape(PER, HEAD, n)
    norm = normed.astype(F32).reshape(PER, HEAD, n)
    gain = gains.reshape(PER, HEAD, 1)
    inner = jnp.sum(norm * grad, axis=1, keepdims=True) * (1.0 / HEAD)
    return (inverse * (gain * grad - norm * (1.0 / gain) * inner)).reshape(PART, n).astype(BF16)


def gain_columns(gains, block, square):
    square[...] = jnp.zeros_like(square)
    square[0:2, 0:HEAD] = gains[block]
    turned = square[...].T
    return [jnp.concatenate([turned[:HEAD, i : i + 1]] * PER, axis=0) for i in range(2)]


def softmax_pieces(query, key, value):
    pieces = []
    for h in range(PER):
        rows = slice(h * HEAD, (h + 1) * HEAD)
        scores = dot(key[rows], query[rows], (0, 0))
        unnormed = jnp.exp2(scores * (SCALE * LOG2E))
        total = jnp.sum(unnormed, axis=0, keepdims=True)
        pieces.append(dot(value[rows], unnormed.astype(BF16), (1, 0)) * (1.0 / total))
    return jnp.concatenate(pieces, axis=0).astype(BF16)


def half_of(me, other):
    return pl.ds(pl.multiple_of(((me // 2) ^ other) * 2 * OWN, 2 * OWN), 2 * OWN)


def core_of(me, d):
    return pl.ds(pl.multiple_of(((me ^ d) & 1) * OWN, OWN), OWN)


def part_of(me, d):
    return pl.ds(pl.multiple_of((me ^ d) * PART, 32), PART)


def own_of(me, d):
    return pl.ds(pl.multiple_of((me ^ d) * OWN, OWN), OWN)


def spatial_forward(
    me_ref, x0, x1, x2, x3, mod, gains, wt, wo, q_o, k_o, v_o, st_o, p0, p1, p2, p3, modc, xrow,
    uw, xs, both, lines, square,
):
    me = me_ref[0]
    gain_q, gain_k = gain_columns(gains, 0, square)
    lines[...] = jnp.zeros_like(lines)
    for i in range(3):
        lines[i : i + 1, :] = mod[i, 0:1, :]
    lines[3:4, :] = 1.0 + mod[1, 0:1, :]
    modc[...] = lines[...].T
    for d, x in enumerate((x0, x1, x2, x3)):
        xs[part_of(me, d), :] = x[...]
    stream = xs[...].astype(F32)
    mean = jnp.sum(stream, axis=0, keepdims=True) * (1.0 / WIDE)
    centred = stream - mean
    inverse = lax.rsqrt(jnp.sum(centred * centred, axis=0, keepdims=True) * (1.0 / WIDE) + EPS)
    normed = (centred * inverse * (1.0 + modc[:, 1:2]) + modc[:, 0:1]).astype(BF16)
    weights = wt[...].reshape(3 * PART, WIDE)
    projected = dot(weights, normed, (1, 0))
    uw[...] = dot(weights, modc[...].astype(BF16), (1, 0))
    query, inv_q = head_norm_t(projected[:PART], gain_q)
    key, inv_k = head_norm_t(projected[PART : 2 * PART], gain_k)
    q_o[...] = query
    k_o[...] = key
    v_o[...] = projected[2 * PART :].astype(BF16)
    st_o[0:4, :] = inv_q.reshape(PER, ROWS)
    st_o[4:8, :] = inv_k.reshape(PER, ROWS)
    st_o[8:9, :] = mean
    st_o[9:10, :] = inverse
    attended = softmax_pieces(query, key, v_o[...])
    branch = dot(attended, wo[...], (0, 0)).astype(BF16)
    both[...] = branch
    for d, partial in enumerate((p0, p1, p2, p3)):
        partial[...] = both[own_of(me, d), :]
    xrow[...] = xs[:, own_of(me, 0)].astype(F32).T.astype(BF16)


def temporal_group(normed, gated, gain_q, gain_k, weights, wo):
    n = normed.shape[0]
    left = lax.broadcasted_iota(jnp.int32, (n, n), 0)
    right = lax.broadcasted_iota(jnp.int32, (n, n), 1)
    mask = ((left & 1) == (right & 1)) & ((left // OWN) == (right // OWN))
    projected = dot(weights, normed, (1, 1))
    query, inv_q = head_norm_t(projected[:PART], gain_q)
    key, inv_k = head_norm_t(projected[PART : 2 * PART], gain_k)
    value = projected[2 * PART :].astype(BF16)
    grad_att = dot(wo, gated, (1, 1)).astype(BF16)
    attended, gq, gk, gv = [], [], [], []
    for h in range(PER):
        rows = slice(h * HEAD, (h + 1) * HEAD)
        q, k, v, da = query[rows], key[rows], value[rows], grad_att[rows]
        scores = dot(k, q, (0, 0))
        unnormed = jnp.where(mask, jnp.exp2(scores * (SCALE * LOG2E)), 0.0)
        probs = unnormed * (1.0 / jnp.sum(unnormed, axis=0, keepdims=True))
        rounded = probs.astype(BF16)
        attended.append(dot(v, rounded, (1, 0)))
        grad_probs = dot(v, da, (0, 0))
        inner = jnp.sum(grad_probs * probs, axis=0, keepdims=True)
        grad_scores = (probs * (grad_probs - inner)).astype(BF16)
        gv.append(dot(da, rounded, (1, 1)))
        gq.append(dot(k, grad_scores, (1, 0)) * SCALE)
        gk.append(dot(q, grad_scores, (1, 1)) * SCALE)
    attended = jnp.concatenate(attended, axis=0).astype(BF16)
    gq = jnp.concatenate(gq, axis=0).astype(BF16)
    gk = jnp.concatenate(gk, axis=0).astype(BF16)
    gv = jnp.concatenate(gv, axis=0).astype(BF16)
    dq = head_back_t(gq, query, inv_q, gain_q)
    dk = head_back_t(gk, key, inv_k, gain_k)
    stacked = jnp.concatenate([dq, dk, gv], axis=0)
    return dot(stacked, weights, (0, 0)), dot(attended, wo, (0, 0))


def temporal_own(x0, x1, c0, c1, mod, gains, wt, wo, gn_o, br_o, normed_o, gated_o, square):
    stream = jnp.concatenate([x0[...], x1[...]], axis=0).astype(F32)
    incoming = jnp.concatenate([c0[...], c1[...]], axis=0).astype(F32)
    mean = jnp.sum(stream, axis=1, keepdims=True) * (1.0 / WIDE)
    centred = stream - mean
    inverse = lax.rsqrt(jnp.sum(centred * centred, axis=1, keepdims=True) * (1.0 / WIDE) + EPS)
    normed = (centred * inverse * (1.0 + mod[1, 1:2, :]) + mod[0, 1:2, :]).astype(BF16)
    gated = (mod[2, 1:2, :] * incoming).astype(BF16)
    normed_o[...] = normed
    gated_o[...] = gated
    term, branch = temporal_group(
        normed, gated, *gain_columns(gains, 1, square), wt[...].reshape(3 * PART, WIDE), wo[...]
    )
    gn_o[...] = term.astype(BF16)
    br_o[...] = branch.astype(BF16)


def temporal_far(
    at_ref, normed, gated, gn_r, br_r, gains, w0, w1, w2, w3, gn0, gn1, op0, op1, ws, square
):
    for d, w in enumerate((w0, w1, w2, w3)):
        ws[pl.ds(pl.multiple_of(((at_ref[0] + d) & 3) * PART, 32), PART), :] = w[...]
    term, branch = temporal_group(
        normed[...],
        gated[...],
        *gain_columns(gains, 1, square),
        ws[: 3 * PART, :],
        ws[3 * PART :, :],
    )
    term = term + gn_r[...].astype(F32)
    branch = branch + br_r[...].astype(F32)
    gn0[...] = term[:OWN]
    gn1[...] = term[OWN:].astype(BF16)
    op0[...] = branch[:OWN]
    op1[...] = branch[OWN:].astype(BF16)


def temporal_finish(x0, c0, gn0, gn1, op0, op1, mod, gm_o, mixed_o):
    stream = x0[...].astype(F32)
    mean = jnp.sum(stream, axis=1, keepdims=True) * (1.0 / WIDE)
    shifted = stream - mean
    inverse = lax.rsqrt(jnp.sum(shifted * shifted, axis=1, keepdims=True) * (1.0 / WIDE) + EPS)
    centred = shifted * inverse
    scaled = (gn0[...] + gn1[...].astype(F32)) * (1.0 + mod[1, 1:2, :])
    first = jnp.sum(scaled, axis=1, keepdims=True) * (1.0 / WIDE)
    second = jnp.sum(scaled * centred, axis=1, keepdims=True) * (1.0 / WIDE)
    gm_o[...] = (c0[...].astype(F32) + inverse * (scaled - first - centred * second)).astype(BF16)
    mixed_o[...] = (stream + mod[2, 1:2, :] * (op0[...] + op1[...].astype(F32))).astype(BF16)


def backward_half(queries, grad_att, k_r, v_r):
    gq, gk, gv = [], [], []
    for h in range(PER):
        rows = slice(h * HEAD, (h + 1) * HEAD)
        q, k, v, da = queries[rows], k_r[rows, :], v_r[rows, :], grad_att[rows]
        scores = dot(k, q, (0, 0))
        unnormed = jnp.exp2(scores * (SCALE * LOG2E))
        probs = unnormed * (1.0 / jnp.sum(unnormed, axis=0, keepdims=True))
        rounded = probs.astype(BF16)
        grad_probs = dot(v, da, (0, 0))
        inner = jnp.sum(grad_probs * probs, axis=0, keepdims=True)
        grad_scores = (probs * (grad_probs - inner)).astype(BF16)
        gv.append(dot(da, rounded, (1, 1)))
        gk.append(dot(q, grad_scores, (1, 1)))
        gq.append(dot(k, grad_scores, (1, 0)) * SCALE)
    return [jnp.concatenate(g, axis=0) for g in (gq, gk, gv)]


def gated_half(me, d, ga, gb, mod, rows):
    rows[core_of(me, d), :] = (mod[2, 0:1, :] * ga[...].astype(F32)).astype(BF16)
    rows[core_of(me, d ^ 1), :] = (mod[2, 0:1, :] * gb[...].astype(F32)).astype(BF16)
    return rows[...]


def spatial_backward_own(
    me_ref, g0, g1, q_r, k_r, v_r, mod, wo, gq_o, gk_o, gv_o, rows
):
    me = me_ref[0]
    gated = gated_half(me, 0, g0, g1, mod, rows)
    grad_att = dot(wo[...], gated, (1, 1)).astype(BF16)
    gq, gk, gv = backward_half(q_r[:, half_of(me, 0)], grad_att, k_r, v_r)
    gq_o[...] = gq.astype(BF16)
    gk_o[...] = gk
    gv_o[...] = gv


def norm_sums(part, normed, inverse, gains, uw, start):
    n = part.shape[1]
    grad = part.astype(F32)
    before = normed.astype(F32)
    if inverse is not None:
        before = (before * (1.0 / gains)).reshape(PER, HEAD, n) * (1.0 / inverse)
        before = before.reshape(PART, n)
    shift, scale = uw[start : start + PART, 0:1], uw[start : start + PART, 3:4]
    first = jnp.sum(grad * scale, axis=0, keepdims=True)
    return first, jnp.sum(grad * (before - shift), axis=0, keepdims=True)


def spatial_backward_far(
    me_ref, g2, g3, q_r, k_r, v_r, st, gq_r, gk_r, gv_r, mod, gains, uw, wo, wn,
    p2, p3, stacked_o, rs_o, rows, gq_s, square,
):
    me = me_ref[0]
    gated = gated_half(me, 2, g2, g3, mod, rows)
    grad_att = dot(wo[...], gated, (1, 1)).astype(BF16)
    gq, gk, gv = backward_half(q_r[:, half_of(me, 1)], grad_att, k_r, v_r)
    gain_q, gain_k = gain_columns(gains, 0, square)
    gq_s[:, half_of(me, 0)] = gq_r[...]
    gq_s[:, half_of(me, 1)] = gq.astype(BF16)
    gk = ((gk + gk_r[...]) * SCALE).astype(BF16)
    inv_q = st[0:4, :].reshape(PER, 1, ROWS)
    inv_k = st[4:8, :].reshape(PER, 1, ROWS)
    stacked_o[:PART, :] = head_back_t(gq_s[...], q_r[...], inv_q, gain_q)
    stacked_o[PART : 2 * PART, :] = head_back_t(gk, k_r[...], inv_k, gain_k)
    stacked_o[2 * PART :, :] = (gv + gv_r[...]).astype(BF16)
    stacked = stacked_o[...]
    turned = wn
    for d, partial in ((3, p3), (2, p2)):
        partial[...] = dot(turned[part_of(me, d), :], stacked, (1, 0)).astype(BF16)
    sums = [
        norm_sums(stacked[:PART], q_r[...], inv_q, gain_q, uw, 0),
        norm_sums(stacked[PART : 2 * PART], k_r[...], inv_k, gain_k, uw, PART),
        norm_sums(stacked[2 * PART :], v_r[...], None, None, uw, 2 * PART),
    ]
    rs_o[...] = jnp.zeros_like(rs_o)
    rs_o[0:1, :] = sums[0][0] + sums[1][0] + sums[2][0]
    rs_o[1:2, :] = sums[0][1] + sums[1][1] + sums[2][1]


def spatial_backward_last(me_ref, stacked_r, g0, g1, g2, g3, wn, p0, p1a, p1b, gown, rows):
    me = me_ref[0]
    stacked = stacked_r[...]
    turned = wn
    part = dot(turned[part_of(me, 1), :], stacked, (1, 0)).astype(BF16)
    p1a[...] = part[: PART // 2]
    p1b[...] = part[PART // 2 :]
    p0[...] = dot(turned[part_of(me, 0), :], stacked, (1, 0)).astype(BF16)
    for d, g in enumerate((g0, g1, g2, g3)):
        rows[...] = g[...].astype(F32).T
        gown[:, own_of(me, d)] = rows[part_of(me, 0), :].astype(BF16)


def spatial_finish(me_ref, p0, m1a, m1b, o2, rs, st, x0, gown, modc, out_o):
    m1 = jnp.concatenate([m1a[...], m1b[...]], axis=0)
    grad = p0[...].astype(F32) + m1.astype(F32) + o2[...].astype(F32)
    inverse = st[9:10, :]
    scaled = grad * (1.0 + modc[part_of(me_ref[0], 0), 1:2])
    centred = (x0[...].astype(F32) - st[8:9, :]) * inverse
    first = rs[0:1, :] * (1.0 / WIDE)
    second = rs[1:2, :] * (1.0 / WIDE)
    out_o[...] = (gown[...].astype(F32) + inverse * (scaled - first - centred * second)).astype(BF16)


def split_columns(me_ref, columns, c0, c1, c23):
    me = me_ref[0]
    c0[...] = columns[:, own_of(me, 0)]
    c1[...] = columns[:, own_of(me, 1)]
    c23[:PART, :] = columns[:, own_of(me, 2)]
    c23[PART:, :] = columns[:, own_of(me, 3)]


def place_columns(me_ref, c0, c1, c2, c3, out_o):
    me = me_ref[0]
    for d, c in enumerate((c0[...], c1[...], c2[:PART, :], c3[PART:, :])):
        out_o[:, own_of(me, d)] = c


def gather_rows(me_ref, c0, c1, c2, c3, wt, rows_o, wn_o, cs):
    me = me_ref[0]
    wn_o[...] = wt[...].reshape(3 * PART, WIDE).T
    for d, c in enumerate((c0[...], c1[...], c2[:PART, :], c3[PART:, :])):
        cs[part_of(me, d), :] = c.astype(F32)
    rows_o[...] = cs[...].T.astype(BF16)


def split_rows(me_ref, rows, c0, c1, c23, cs):
    me = me_ref[0]
    cs[...] = rows[...].astype(F32).T
    c0[...] = cs[part_of(me, 0), :].astype(BF16)
    c1[...] = cs[part_of(me, 1), :].astype(BF16)
    c23[:PART, :] = cs[part_of(me, 2), :].astype(BF16)
    c23[PART:, :] = cs[part_of(me, 3), :].astype(BF16)


def swap(values, d):
    return lax.ppermute(values, "head", [(i, i ^ d) for i in range(4)])


def exchange(parts):
    mine, mate, both = parts
    far = swap(both, 2)
    return [mine, swap(mate, 1), far, swap(far, 1)]


def across_seq(one, two):
    rows = jnp.concatenate([v.reshape(64, 2, WIDE) for v in (one, two)], axis=1)
    moved = lax.all_to_all(rows, "seq", split_axis=0, concat_axis=0, tiled=True)
    return moved[:, :2].reshape(OWN, WIDE), moved[:, 2:].reshape(OWN, WIDE)


def from_neighbour(chunk):
    index = [(s, h) for s in range(64) for h in range(4)]
    near = [(s * 4 + h, (s ^ 4) * 4 + (h ^ 2)) for s, h in index]
    return lax.ppermute(chunk, ("seq", "head"), near)


def round_x(chunk, d):
    return lax.ppermute(chunk, "seq", [(s // 4 * 4 + (s + d) % 4, s) for s in range(64)])


def on_device(tokens, cotangent, qkv_weight, out_weight, modulation, head_gains):
    me = lax.axis_index("head")
    mine = me.astype(jnp.int32).reshape(1)
    at = (lax.axis_index("seq") & 3).astype(jnp.int32)
    wt = jnp.transpose(qkv_weight, (0, 2, 3, 1))
    mod = jnp.transpose(modulation, (1, 0, 2))
    row = out((OWN, WIDE))
    col = out((PART, ROWS))
    piece = out((PART, OWN))
    square = pltpu.VMEM((8, 128), F32)

    x0 = tokens.T
    x2 = swap(x0, 2)
    x1 = swap(x0, 1)
    pieces = [piece, piece, out((2 * PART, OWN))]
    parts = call(split_columns, pieces, [mine, cotangent.T], smem=1)
    weights = [wt[0], wt[1], out_weight[0], out_weight[1]]
    x2, weights, parts = lax.optimization_barrier((x2, weights, parts))
    wt_s, wt_t, wo_s, wo_t = weights
    x3 = swap(x2, 1)
    parts = exchange(parts)
    query, key, value, stats, p0, p1, p2, p3, modc, xrow, uw = call(
        spatial_forward,
        [col] * 3 + [out((16, ROWS), F32)] + [row] * 4 + [out((WIDE, 8), F32), row]
        + [out((3 * PART, 8), F32)],
        [mine, x0, x1, x2, x3, mod, head_gains, wt_s, wo_s],
        [pltpu.VMEM((WIDE, ROWS), BF16), pltpu.VMEM((ROWS, WIDE), BF16),
         pltpu.VMEM((8, WIDE), F32), square],
        smem=1,
    )
    m3, *parts = lax.optimization_barrier((swap(p3, 1), *parts))
    m1 = swap(p1, 1)
    chip = (p2.astype(F32) + m3.astype(F32)).astype(BF16)
    far = swap(chip, 2)
    cot0, wn = call(
        gather_rows, [row, out((WIDE, 3 * PART))], [mine, *parts, wt_s],
        [pltpu.VMEM((WIDE, OWN), F32)], smem=1, behind=[chip],
    )

    chunks = [lax.select_n(at ^ d, wt[1, 0], wt[1, 1], wt[1, 2], out_weight[1]) for d in (0, 2)]
    (chunk, chunk2), far = lax.optimization_barrier((chunks, far))
    near, second = from_neighbour(chunk), from_neighbour(chunk2)
    others = [near, round_x(near, 1), second, round_x(near, 3)]

    branch = p0.astype(F32) + m1.astype(F32) + far.astype(F32)
    middle = (xrow.astype(F32) + modulation[0, 2][None] * branch).astype(BF16)

    t0, cot0 = across_seq(middle, cot0)
    t1, cot1 = swap(t0, 1), swap(cot0, 1)
    gn, br, normed, gated = call(
        temporal_own, [out((2 * OWN, WIDE))] * 4,
        [t0, t1, cot0, cot1, mod, head_gains, wt_t, wo_t],
        [square],
    )
    gn0, gn1, op0, op1 = call(
        temporal_far,
        [out((OWN, WIDE), F32), row, out((OWN, WIDE), F32), row],
        [at.reshape(1), normed, gated, gn, br, head_gains, *others],
        [pltpu.VMEM((4 * PART, WIDE), BF16), square],
        smem=1,
    )
    gn1, op1 = swap(gn1, 1), swap(op1, 1)
    grad_middle, mixed_rows = call(
        temporal_finish, [row] * 2, [t0, cot0, gn0, gn1, op0, op1, mod]
    )

    g0, mixed_rows = across_seq(grad_middle, mixed_rows)
    g2 = swap(g0, 2)
    g1 = swap(g0, 1)
    gq, gk, gv = call(
        spatial_backward_own,
        [out((PART, 2 * OWN)), out((PART, ROWS), F32), out((PART, ROWS), F32)],
        [mine, g0, g1, query, key, value, mod, wo_s],
        [pltpu.VMEM((2 * OWN, WIDE), BF16)],
        smem=1,
    )
    parts = call(
        split_rows, pieces, [mine, mixed_rows], [pltpu.VMEM((WIDE, OWN), F32)], smem=1
    )
    g2, gq, *parts = lax.optimization_barrier((g2, gq, *parts))
    g3 = swap(g2, 1)
    parts = exchange(parts)
    p2, p3, stacked, sums = call(
        spatial_backward_far,
        [col, col, out((3 * PART, ROWS)), out((8, ROWS), F32)],
        [mine, g2, g3, query, key, value, stats, gq, gk, gv, mod, head_gains, uw, wo_s,
         wn],
        [pltpu.VMEM((2 * OWN, WIDE), BF16), pltpu.VMEM((PART, ROWS), BF16), square],
        smem=1,
    )
    m3, other, *parts = lax.optimization_barrier((swap(p3, 1), swap(sums, 1), *parts))
    chip = (p2.astype(F32) + m3.astype(F32)).astype(BF16)
    far = swap(chip, 2)
    sums = sums + other
    sums = sums + swap(sums, 2)
    p0, p1a, p1b, gown = call(
        spatial_backward_last,
        [col, out((PART // 2, ROWS)), out((PART // 2, ROWS)), col],
        [mine, stacked, g0, g1, g2, g3, wn],
        [pltpu.VMEM((WIDE, OWN), F32)],
        smem=1,
        behind=[chip],
    )
    m1a, m1b = swap(p1a, 1), swap(p1b, 1)

    (mixed,) = call(place_columns, [col], [mine, *parts], smem=1, behind=[p0])

    (grad,) = call(
        spatial_finish, [col], [mine, p0, m1a, m1b, far, sums, stats, x0, gown, modc],
        smem=1,
    )
    return (mixed.T, grad.T)


def solution(mesh):
    in_specs = (
        P("seq", "head"),
        P("seq", "head"),
        P(None, None, None, "head"),
        P(None, "head", None),
        P(),
        P(),
    )
    out_specs = (P("seq", "head"), P("seq", "head"))
    return jax.shard_map(
        on_device, mesh=mesh, in_specs=in_specs, out_specs=out_specs, check_vma=False
    )
```

```python
import jax
import jax.numpy as jnp
from jax import lax
from jax.experimental import pallas as pl
from jax.experimental.pallas import tpu as pltpu
from jax.sharding import PartitionSpec as P

EPS = 1e-06
HEAD = 72
PER = 4
WIDE = 1152
PART = 288
ROWS = 512
OWN = 128
LOG2E = 1.4426950408889634
SCALE = HEAD**-0.5
F32 = jnp.float32
BF16 = jnp.bfloat16
VMEM_LIMIT = 56 * 1024 * 1024


def dot(a, b, over):
    return lax.dot_general(a, b, (((over[0],), (over[1],)), ((), ())), preferred_element_type=F32)


def call(body, outs, operands, scratch=(), smem=0, behind=()):
    n, skip = len(operands), len(behind)
    specs = [
        pl.BlockSpec(memory_space=pltpu.SMEM if i < smem else pltpu.VMEM) for i in range(n)
    ] + [pl.BlockSpec(memory_space=pl.ANY)] * skip

    def run(*refs):
        body(*refs[:n], *refs[n + skip :])

    return pl.pallas_call(
        run,
        out_shape=list(outs),
        in_specs=specs,
        out_specs=[pl.BlockSpec(memory_space=pltpu.VMEM)] * len(outs),
        scratch_shapes=list(scratch),
        compiler_params=pltpu.CompilerParams(vmem_limit_bytes=VMEM_LIMIT),
        cost_estimate=pl.CostEstimate(flops=1, bytes_accessed=1, transcendentals=0),
    )(*operands, *behind)


def out(shape, dtype=BF16):
    return jax.ShapeDtypeStruct(shape, dtype)


def head_norm_t(part, gains):
    n = part.shape[1]
    cube = part.reshape(PER, HEAD, n)
    inverse = lax.rsqrt(jnp.sum(cube * cube, axis=1, keepdims=True) * (1.0 / HEAD) + EPS)
    return (cube * inverse * gains.reshape(PER, HEAD, 1)).reshape(PART, n).astype(BF16), inverse


def head_back_t(incoming, normed, inverse, gains):
    n = incoming.shape[1]
    grad = incoming.astype(F32).reshape(PER, HEAD, n)
    norm = normed.astype(F32).reshape(PER, HEAD, n)
    gain = gains.reshape(PER, HEAD, 1)
    inner = jnp.sum(norm * grad, axis=1, keepdims=True) * (1.0 / HEAD)
    return (inverse * (gain * grad - norm * (1.0 / gain) * inner)).reshape(PART, n).astype(BF16)


def gain_columns(gains, block, square):
    square[...] = jnp.zeros_like(square)
    square[0:2, 0:HEAD] = gains[block]
    turned = square[...].T
    return [jnp.concatenate([turned[:HEAD, i : i + 1]] * PER, axis=0) for i in range(2)]


def softmax_pieces(query, key, value):
    pieces = []
    for h in range(PER):
        rows = slice(h * HEAD, (h + 1) * HEAD)
        scores = dot(key[rows], query[rows], (0, 0))
        unnormed = jnp.exp2(scores * (SCALE * LOG2E))
        total = jnp.sum(unnormed, axis=0, keepdims=True)
        pieces.append(dot(value[rows], unnormed.astype(BF16), (1, 0)) * (1.0 / total))
    return jnp.concatenate(pieces, axis=0).astype(BF16)


def half_of(me, other):
    return pl.ds(pl.multiple_of(((me // 2) ^ other) * 2 * OWN, 2 * OWN), 2 * OWN)


def core_of(me, d):
    return pl.ds(pl.multiple_of(((me ^ d) & 1) * OWN, OWN), OWN)


def part_of(me, d):
    return pl.ds(pl.multiple_of((me ^ d) * PART, 32), PART)


def own_of(me, d):
    return pl.ds(pl.multiple_of((me ^ d) * OWN, OWN), OWN)


def spatial_forward(
    me_ref, x0, x1, x2, x3, mod, gains, wt, wo, q_o, k_o, v_o, st_o, p0, p1, p2, p3, modc, xrow,
    uw, xs, both, lines, square,
):
    me = me_ref[0]
    gain_q, gain_k = gain_columns(gains, 0, square)
    lines[...] = jnp.zeros_like(lines)
    for i in range(3):
        lines[i : i + 1, :] = mod[i, 0:1, :]
    lines[3:4, :] = 1.0 + mod[1, 0:1, :]
    modc[...] = lines[...].T
    for d, x in enumerate((x0, x1, x2, x3)):
        xs[part_of(me, d), :] = x[...]
    stream = xs[...].astype(F32)
    mean = jnp.sum(stream, axis=0, keepdims=True) * (1.0 / WIDE)
    centred = stream - mean
    inverse = lax.rsqrt(jnp.sum(centred * centred, axis=0, keepdims=True) * (1.0 / WIDE) + EPS)
    normed = (centred * inverse * (1.0 + modc[:, 1:2]) + modc[:, 0:1]).astype(BF16)
    weights = wt[...].reshape(3 * PART, WIDE)
    projected = dot(weights, normed, (1, 0))
    uw[...] = dot(weights, modc[...].astype(BF16), (1, 0))
    query, inv_q = head_norm_t(projected[:PART], gain_q)
    key, inv_k = head_norm_t(projected[PART : 2 * PART], gain_k)
    q_o[...] = query
    k_o[...] = key
    v_o[...] = projected[2 * PART :].astype(BF16)
    st_o[0:4, :] = inv_q.reshape(PER, ROWS)
    st_o[4:8, :] = inv_k.reshape(PER, ROWS)
    st_o[8:9, :] = mean
    st_o[9:10, :] = inverse
    attended = softmax_pieces(query, key, v_o[...])
    branch = dot(attended, wo[...], (0, 0)).astype(BF16)
    both[...] = branch
    for d, partial in enumerate((p0, p1, p2, p3)):
        partial[...] = both[own_of(me, d), :]
    xrow[...] = xs[:, own_of(me, 0)].astype(F32).T.astype(BF16)


def temporal_group(normed, gated, gain_q, gain_k, weights, wo):
    n = normed.shape[0]
    left = lax.broadcasted_iota(jnp.int32, (n, n), 0)
    right = lax.broadcasted_iota(jnp.int32, (n, n), 1)
    mask = ((left & 1) == (right & 1)) & ((left // OWN) == (right // OWN))
    projected = dot(weights, normed, (1, 1))
    query, inv_q = head_norm_t(projected[:PART], gain_q)
    key, inv_k = head_norm_t(projected[PART : 2 * PART], gain_k)
    value = projected[2 * PART :].astype(BF16)
    grad_att = dot(wo, gated, (1, 1)).astype(BF16)
    attended, gq, gk, gv = [], [], [], []
    for h in range(PER):
        rows = slice(h * HEAD, (h + 1) * HEAD)
        q, k, v, da = query[rows], key[rows], value[rows], grad_att[rows]
        scores = dot(k, q, (0, 0))
        unnormed = jnp.where(mask, jnp.exp2(scores * (SCALE * LOG2E)), 0.0)
        probs = unnormed * (1.0 / jnp.sum(unnormed, axis=0, keepdims=True))
        rounded = probs.astype(BF16)
        attended.append(dot(v, rounded, (1, 0)))
        grad_probs = dot(v, da, (0, 0))
        inner = jnp.sum(grad_probs * probs, axis=0, keepdims=True)
        grad_scores = (probs * (grad_probs - inner)).astype(BF16)
        gv.append(dot(da, rounded, (1, 1)))
        gq.append(dot(k, grad_scores, (1, 0)) * SCALE)
        gk.append(dot(q, grad_scores, (1, 1)) * SCALE)
    attended = jnp.concatenate(attended, axis=0).astype(BF16)
    gq = jnp.concatenate(gq, axis=0).astype(BF16)
    gk = jnp.concatenate(gk, axis=0).astype(BF16)
    gv = jnp.concatenate(gv, axis=0).astype(BF16)
    dq = head_back_t(gq, query, inv_q, gain_q)
    dk = head_back_t(gk, key, inv_k, gain_k)
    stacked = jnp.concatenate([dq, dk, gv], axis=0)
    return dot(stacked, weights, (0, 0)), dot(attended, wo, (0, 0))


def temporal_own(x0, x1, c0, c1, mod, gains, wt, wo, gn_o, br_o, normed_o, gated_o, square):
    stream = jnp.concatenate([x0[...], x1[...]], axis=0).astype(F32)
    incoming = jnp.concatenate([c0[...], c1[...]], axis=0).astype(F32)
    mean = jnp.sum(stream, axis=1, keepdims=True) * (1.0 / WIDE)
    centred = stream - mean
    inverse = lax.rsqrt(jnp.sum(centred * centred, axis=1, keepdims=True) * (1.0 / WIDE) + EPS)
    normed = (centred * inverse * (1.0 + mod[1, 1:2, :]) + mod[0, 1:2, :]).astype(BF16)
    gated = (mod[2, 1:2, :] * incoming).astype(BF16)
    normed_o[...] = normed
    gated_o[...] = gated
    term, branch = temporal_group(
        normed, gated, *gain_columns(gains, 1, square), wt[...].reshape(3 * PART, WIDE), wo[...]
    )
    gn_o[...] = term.astype(BF16)
    br_o[...] = branch.astype(BF16)


def temporal_far(
    at_ref, normed, gated, gn_r, br_r, gains, w0, w1, w2, w3, gn0, gn1, op0, op1, ws, square
):
    for d, w in enumerate((w0, w1, w2, w3)):
        ws[pl.ds(pl.multiple_of(((at_ref[0] + d) & 3) * PART, 32), PART), :] = w[...]
    term, branch = temporal_group(
        normed[...],
        gated[...],
        *gain_columns(gains, 1, square),
        ws[: 3 * PART, :],
        ws[3 * PART :, :],
    )
    term = term + gn_r[...].astype(F32)
    branch = branch + br_r[...].astype(F32)
    gn0[...] = term[:OWN]
    gn1[...] = term[OWN:].astype(BF16)
    op0[...] = branch[:OWN]
    op1[...] = branch[OWN:].astype(BF16)


def temporal_finish(x0, c0, gn0, gn1, op0, op1, mod, gm_o, mixed_o):
    stream = x0[...].astype(F32)
    mean = jnp.sum(stream, axis=1, keepdims=True) * (1.0 / WIDE)
    shifted = stream - mean
    inverse = lax.rsqrt(jnp.sum(shifted * shifted, axis=1, keepdims=True) * (1.0 / WIDE) + EPS)
    centred = shifted * inverse
    scaled = (gn0[...] + gn1[...].astype(F32)) * (1.0 + mod[1, 1:2, :])
    first = jnp.sum(scaled, axis=1, keepdims=True) * (1.0 / WIDE)
    second = jnp.sum(scaled * centred, axis=1, keepdims=True) * (1.0 / WIDE)
    gm_o[...] = (c0[...].astype(F32) + inverse * (scaled - first - centred * second)).astype(BF16)
    mixed_o[...] = (stream + mod[2, 1:2, :] * (op0[...] + op1[...].astype(F32))).astype(BF16)


def backward_half(queries, grad_att, k_r, v_r):
    gq, gk, gv = [], [], []
    for h in range(PER):
        rows = slice(h * HEAD, (h + 1) * HEAD)
        q, k, v, da = queries[rows], k_r[rows, :], v_r[rows, :], grad_att[rows]
        scores = dot(k, q, (0, 0))
        unnormed = jnp.exp2(scores * (SCALE * LOG2E))
        probs = unnormed * (1.0 / jnp.sum(unnormed, axis=0, keepdims=True))
        rounded = probs.astype(BF16)
        grad_probs = dot(v, da, (0, 0))
        inner = jnp.sum(grad_probs * probs, axis=0, keepdims=True)
        grad_scores = (probs * (grad_probs - inner)).astype(BF16)
        gv.append(dot(da, rounded, (1, 1)))
        gk.append(dot(q, grad_scores, (1, 1)))
        gq.append(dot(k, grad_scores, (1, 0)) * SCALE)
    return [jnp.concatenate(g, axis=0) for g in (gq, gk, gv)]


def gated_half(me, d, ga, gb, mod, rows):
    rows[core_of(me, d), :] = (mod[2, 0:1, :] * ga[...].astype(F32)).astype(BF16)
    rows[core_of(me, d ^ 1), :] = (mod[2, 0:1, :] * gb[...].astype(F32)).astype(BF16)
    return rows[...]


def spatial_backward_own(
    me_ref, g0, g1, q_r, k_r, v_r, mod, wo, gq_o, gk_o, gv_o, rows
):
    me = me_ref[0]
    gated = gated_half(me, 0, g0, g1, mod, rows)
    grad_att = dot(wo[...], gated, (1, 1)).astype(BF16)
    gq, gk, gv = backward_half(q_r[:, half_of(me, 0)], grad_att, k_r, v_r)
    gq_o[...] = gq.astype(BF16)
    gk_o[...] = gk
    gv_o[...] = gv


def norm_sums(part, normed, inverse, gains, uw, start):
    n = part.shape[1]
    grad = part.astype(F32)
    before = normed.astype(F32)
    if inverse is not None:
        before = (before * (1.0 / gains)).reshape(PER, HEAD, n) * (1.0 / inverse)
        before = before.reshape(PART, n)
    shift, scale = uw[start : start + PART, 0:1], uw[start : start + PART, 3:4]
    first = jnp.sum(grad * scale, axis=0, keepdims=True)
    return first, jnp.sum(grad * (before - shift), axis=0, keepdims=True)


def spatial_backward_far(
    me_ref, g2, g3, q_r, k_r, v_r, st, gq_r, gk_r, gv_r, mod, gains, uw, wo, wn,
    p2, p3, stacked_o, rs_o, rows, gq_s, square,
):
    me = me_ref[0]
    gated = gated_half(me, 2, g2, g3, mod, rows)
    grad_att = dot(wo[...], gated, (1, 1)).astype(BF16)
    gq, gk, gv = backward_half(q_r[:, half_of(me, 1)], grad_att, k_r, v_r)
    gain_q, gain_k = gain_columns(gains, 0, square)
    gq_s[:, half_of(me, 0)] = gq_r[...]
    gq_s[:, half_of(me, 1)] = gq.astype(BF16)
    gk = ((gk + gk_r[...]) * SCALE).astype(BF16)
    inv_q = st[0:4, :].reshape(PER, 1, ROWS)
    inv_k = st[4:8, :].reshape(PER, 1, ROWS)
    stacked_o[:PART, :] = head_back_t(gq_s[...], q_r[...], inv_q, gain_q)
    stacked_o[PART : 2 * PART, :] = head_back_t(gk, k_r[...], inv_k, gain_k)
    stacked_o[2 * PART :, :] = (gv + gv_r[...]).astype(BF16)
    stacked = stacked_o[...]
    turned = wn
    for d, partial in ((3, p3), (2, p2)):
        partial[...] = dot(turned[part_of(me, d), :], stacked, (1, 0)).astype(BF16)
    sums = [
        norm_sums(stacked[:PART], q_r[...], inv_q, gain_q, uw, 0),
        norm_sums(stacked[PART : 2 * PART], k_r[...], inv_k, gain_k, uw, PART),
        norm_sums(stacked[2 * PART :], v_r[...], None, None, uw, 2 * PART),
    ]
    rs_o[...] = jnp.zeros_like(rs_o)
    rs_o[0:1, :] = sums[0][0] + sums[1][0] + sums[2][0]
    rs_o[1:2, :] = sums[0][1] + sums[1][1] + sums[2][1]


def spatial_backward_last(me_ref, stacked_r, g0, g1, g2, g3, wn, p0, p1a, p1b, gown, rows):
    me = me_ref[0]
    stacked = stacked_r[...]
    turned = wn
    part = dot(turned[part_of(me, 1), :], stacked, (1, 0)).astype(BF16)
    p1a[...] = part[: PART // 2]
    p1b[...] = part[PART // 2 :]
    p0[...] = dot(turned[part_of(me, 0), :], stacked, (1, 0)).astype(BF16)
    for d, g in enumerate((g0, g1, g2, g3)):
        rows[...] = g[...].astype(F32).T
        gown[:, own_of(me, d)] = rows[part_of(me, 0), :].astype(BF16)


def spatial_finish(me_ref, p0, m1a, m1b, o2, rs, st, x0, gown, modc, out_o):
    m1 = jnp.concatenate([m1a[...], m1b[...]], axis=0)
    grad = p0[...].astype(F32) + m1.astype(F32) + o2[...].astype(F32)
    inverse = st[9:10, :]
    scaled = grad * (1.0 + modc[part_of(me_ref[0], 0), 1:2])
    centred = (x0[...].astype(F32) - st[8:9, :]) * inverse
    first = rs[0:1, :] * (1.0 / WIDE)
    second = rs[1:2, :] * (1.0 / WIDE)
    out_o[...] = (gown[...].astype(F32) + inverse * (scaled - first - centred * second)).astype(BF16)


def split_columns(me_ref, columns, c0, c1, c23):
    me = me_ref[0]
    c0[...] = columns[:, own_of(me, 0)]
    c1[...] = columns[:, own_of(me, 1)]
    c23[:PART, :] = columns[:, own_of(me, 2)]
    c23[PART:, :] = columns[:, own_of(me, 3)]


def place_columns(me_ref, c0, c1, c2, c3, out_o):
    me = me_ref[0]
    for d, c in enumerate((c0[...], c1[...], c2[:PART, :], c3[PART:, :])):
        out_o[:, own_of(me, d)] = c


def gather_rows(me_ref, c0, c1, c2, c3, wt, rows_o, wn_o, cs):
    me = me_ref[0]
    wn_o[...] = wt[...].reshape(3 * PART, WIDE).T
    for d, c in enumerate((c0[...], c1[...], c2[:PART, :], c3[PART:, :])):
        cs[part_of(me, d), :] = c.astype(F32)
    rows_o[...] = cs[...].T.astype(BF16)


def split_rows(me_ref, rows, c0, c1, c23, cs):
    me = me_ref[0]
    cs[...] = rows[...].astype(F32).T
    c0[...] = cs[part_of(me, 0), :].astype(BF16)
    c1[...] = cs[part_of(me, 1), :].astype(BF16)
    c23[:PART, :] = cs[part_of(me, 2), :].astype(BF16)
    c23[PART:, :] = cs[part_of(me, 3), :].astype(BF16)


def swap(values, d):
    return lax.ppermute(values, "head", [(i, i ^ d) for i in range(4)])


def exchange(parts):
    mine, mate, both = parts
    far = swap(both, 2)
    return [mine, swap(mate, 1), far, swap(far, 1)]


def across_seq(one, two):
    rows = jnp.concatenate([one, two], axis=1).reshape(64, 2, 2 * WIDE)
    moved = lax.all_to_all(rows, "seq", split_axis=0, concat_axis=0, tiled=True)
    moved = moved.reshape(OWN, 2 * WIDE)
    return moved[:, :WIDE], moved[:, WIDE:]


def from_neighbour(chunk):
    index = [(s, h) for s in range(64) for h in range(4)]
    near = [(s * 4 + h, (s ^ 4) * 4 + (h ^ 2)) for s, h in index]
    return lax.ppermute(chunk, ("seq", "head"), near)


def round_x(chunk, d):
    return lax.ppermute(chunk, "seq", [(s // 4 * 4 + (s + d) % 4, s) for s in range(64)])


def on_device(tokens, cotangent, qkv_weight, out_weight, modulation, head_gains):
    me = lax.axis_index("head")
    mine = me.astype(jnp.int32).reshape(1)
    at = (lax.axis_index("seq") & 3).astype(jnp.int32)
    wt = jnp.transpose(qkv_weight, (0, 2, 3, 1))
    mod = jnp.transpose(modulation, (1, 0, 2))
    row = out((OWN, WIDE))
    col = out((PART, ROWS))
    piece = out((PART, OWN))
    square = pltpu.VMEM((8, 128), F32)

    x0 = tokens.T
    x2 = swap(x0, 2)
    x1 = swap(x0, 1)
    pieces = [piece, piece, out((2 * PART, OWN))]
    parts = call(split_columns, pieces, [mine, cotangent.T], smem=1)
    weights = [wt[0], wt[1], out_weight[0], out_weight[1]]
    chunk = lax.select_n(at, wt[1, 0], wt[1, 1], wt[1, 2], out_weight[1])
    x2, chunk, weights, parts = lax.optimization_barrier((x2, chunk, weights, parts))
    wt_s, wt_t, wo_s, wo_t = weights
    x3 = swap(x2, 1)
    parts = exchange(parts)
    near = from_neighbour(chunk)

    query, key, value, stats, p0, p1, p2, p3, modc, xrow, uw = call(
        spatial_forward,
        [col] * 3 + [out((16, ROWS), F32)] + [row] * 4 + [out((WIDE, 8), F32), row]
        + [out((3 * PART, 8), F32)],
        [mine, x0, x1, x2, x3, mod, head_gains, wt_s, wo_s],
        [pltpu.VMEM((WIDE, ROWS), BF16), pltpu.VMEM((ROWS, WIDE), BF16),
         pltpu.VMEM((8, WIDE), F32), square],
        smem=1,
    )
    m3, near, *parts = lax.optimization_barrier((swap(p3, 1), near, *parts))
    m1 = swap(p1, 1)
    chip = (p2.astype(F32) + m3.astype(F32)).astype(BF16)
    far = swap(chip, 2)
    cot0, wn = call(
        gather_rows, [row, out((WIDE, 3 * PART))], [mine, *parts, wt_s],
        [pltpu.VMEM((WIDE, OWN), F32)], smem=1, behind=[chip],
    )

    chunk = lax.select_n(at ^ 2, wt[1, 0], wt[1, 1], wt[1, 2], out_weight[1])
    chunk, far = lax.optimization_barrier((chunk, far))
    second = from_neighbour(chunk)
    others = [near, round_x(near, 1), second, round_x(near, 3)]

    branch = p0.astype(F32) + m1.astype(F32) + far.astype(F32)
    middle = (xrow.astype(F32) + modulation[0, 2][None] * branch).astype(BF16)

    t0, cot0 = across_seq(middle, cot0)
    t1, cot1 = swap(t0, 1), swap(cot0, 1)
    gn, br, normed, gated = call(
        temporal_own, [out((2 * OWN, WIDE))] * 4,
        [t0, t1, cot0, cot1, mod, head_gains, wt_t, wo_t],
        [square],
    )
    gn0, gn1, op0, op1 = call(
        temporal_far,
        [out((OWN, WIDE), F32), row, out((OWN, WIDE), F32), row],
        [at.reshape(1), normed, gated, gn, br, head_gains, *others],
        [pltpu.VMEM((4 * PART, WIDE), BF16), square],
        smem=1,
    )
    gn1, op1 = swap(gn1, 1), swap(op1, 1)
    grad_middle, mixed_rows = call(
        temporal_finish, [row] * 2, [t0, cot0, gn0, gn1, op0, op1, mod]
    )

    g0, mixed_rows = across_seq(grad_middle, mixed_rows)
    g2 = swap(g0, 2)
    g1 = swap(g0, 1)
    gq, gk, gv = call(
        spatial_backward_own,
        [out((PART, 2 * OWN)), out((PART, ROWS), F32), out((PART, ROWS), F32)],
        [mine, g0, g1, query, key, value, mod, wo_s],
        [pltpu.VMEM((2 * OWN, WIDE), BF16)],
        smem=1,
    )
    parts = call(
        split_rows, pieces, [mine, mixed_rows], [pltpu.VMEM((WIDE, OWN), F32)], smem=1
    )
    g2, gq, *parts = lax.optimization_barrier((g2, gq, *parts))
    g3 = swap(g2, 1)
    parts = exchange(parts)
    p2, p3, stacked, sums = call(
        spatial_backward_far,
        [col, col, out((3 * PART, ROWS)), out((8, ROWS), F32)],
        [mine, g2, g3, query, key, value, stats, gq, gk, gv, mod, head_gains, uw, wo_s,
         wn],
        [pltpu.VMEM((2 * OWN, WIDE), BF16), pltpu.VMEM((PART, ROWS), BF16), square],
        smem=1,
    )
    m3, other, *parts = lax.optimization_barrier((swap(p3, 1), swap(sums, 1), *parts))
    chip = (p2.astype(F32) + m3.astype(F32)).astype(BF16)
    far = swap(chip, 2)
    sums = sums + other
    sums = sums + swap(sums, 2)
    p0, p1a, p1b, gown = call(
        spatial_backward_last,
        [col, out((PART // 2, ROWS)), out((PART // 2, ROWS)), col],
        [mine, stacked, g0, g1, g2, g3, wn],
        [pltpu.VMEM((WIDE, OWN), F32)],
        smem=1,
        behind=[chip],
    )
    m1a, m1b = swap(p1a, 1), swap(p1b, 1)

    (mixed,) = call(place_columns, [col], [mine, *parts], smem=1, behind=[p0])

    (grad,) = call(
        spatial_finish, [col], [mine, p0, m1a, m1b, far, sums, stats, x0, gown, modc],
        smem=1,
    )
    return (mixed.T, grad.T)


def solution(mesh):
    in_specs = (
        P("seq", "head"),
        P("seq", "head"),
        P(None, None, None, "head"),
        P(None, "head", None),
        P(),
        P(),
    )
    out_specs = (P("seq", "head"), P("seq", "head"))
    return jax.shard_map(
        on_device, mesh=mesh, in_specs=in_specs, out_specs=out_specs, check_vma=False
    )
```

```python
import jax
import jax.numpy as jnp
from jax import lax
from jax.experimental import pallas as pl
from jax.experimental.pallas import tpu as pltpu
from jax.sharding import PartitionSpec as P

EPS = 1e-06
HEAD = 72
PER = 4
WIDE = 1152
PART = 288
ROWS = 512
OWN = 128
LOG2E = 1.4426950408889634
SCALE = HEAD**-0.5
F32 = jnp.float32
BF16 = jnp.bfloat16
VMEM_LIMIT = 56 * 1024 * 1024


def dot(a, b, over):
    return lax.dot_general(a, b, (((over[0],), (over[1],)), ((), ())), preferred_element_type=F32)


def call(body, outs, operands, scratch=(), smem=0, behind=()):
    n, skip = len(operands), len(behind)
    specs = [
        pl.BlockSpec(memory_space=pltpu.SMEM if i < smem else pltpu.VMEM) for i in range(n)
    ] + [pl.BlockSpec(memory_space=pl.ANY)] * skip

    def run(*refs):
        body(*refs[:n], *refs[n + skip :])

    return pl.pallas_call(
        run,
        out_shape=list(outs),
        in_specs=specs,
        out_specs=[pl.BlockSpec(memory_space=pltpu.VMEM)] * len(outs),
        scratch_shapes=list(scratch),
        compiler_params=pltpu.CompilerParams(vmem_limit_bytes=VMEM_LIMIT),
        cost_estimate=pl.CostEstimate(flops=1, bytes_accessed=1, transcendentals=0),
    )(*operands, *behind)


def out(shape, dtype=BF16):
    return jax.ShapeDtypeStruct(shape, dtype)


def head_norm_t(part, gains):
    n = part.shape[1]
    cube = part.reshape(PER, HEAD, n)
    inverse = lax.rsqrt(jnp.sum(cube * cube, axis=1, keepdims=True) * (1.0 / HEAD) + EPS)
    return (cube * inverse * gains.reshape(PER, HEAD, 1)).reshape(PART, n).astype(BF16), inverse


def head_back_t(incoming, normed, inverse, gains):
    n = incoming.shape[1]
    grad = incoming.astype(F32).reshape(PER, HEAD, n)
    norm = normed.astype(F32).reshape(PER, HEAD, n)
    gain = gains.reshape(PER, HEAD, 1)
    inner = jnp.sum(norm * grad, axis=1, keepdims=True) * (1.0 / HEAD)
    return (inverse * (gain * grad - norm * (1.0 / gain) * inner)).reshape(PART, n).astype(BF16)


def turned_lines(mod, lines):
    lines[...] = jnp.zeros_like(lines)
    for i in range(3):
        lines[i : i + 1, :] = mod[i, 0:1, :]
    lines[3:4, :] = 1.0 + mod[1, 0:1, :]
    return lines[...].T


def gain_columns(gains, block, square):
    square[...] = jnp.zeros_like(square)
    square[0:2, 0:HEAD] = gains[block]
    turned = square[...].T
    return [jnp.concatenate([turned[:HEAD, i : i + 1]] * PER, axis=0) for i in range(2)]


def one_ahead(start, depth=2):
    heads = [slice(h * HEAD, (h + 1) * HEAD) for h in range(PER)]
    ahead = [start(rows) for rows in heads[:depth]]
    for h, rows in enumerate(heads):
        if h + depth < PER:
            ahead.append(start(heads[h + depth]))
        yield rows, ahead.pop(0)


def softmax_pieces(query, key, value):
    pieces = []
    for rows, scores in one_ahead(lambda rows: dot(key[rows], query[rows], (0, 0))):
        unnormed = jnp.exp2(scores * (SCALE * LOG2E))
        total = jnp.sum(unnormed, axis=0, keepdims=True)
        pieces.append(dot(value[rows], unnormed.astype(BF16), (1, 0)) * (1.0 / total))
    return jnp.concatenate(pieces, axis=0).astype(BF16)


def half_of(me, other):
    return pl.ds(pl.multiple_of(((me // 2) ^ other) * 2 * OWN, 2 * OWN), 2 * OWN)


def core_of(me, d):
    return pl.ds(pl.multiple_of(((me ^ d) & 1) * OWN, OWN), OWN)


def part_of(me, d):
    return pl.ds(pl.multiple_of((me ^ d) * PART, 32), PART)


def own_of(me, d):
    return pl.ds(pl.multiple_of((me ^ d) * OWN, OWN), OWN)


def spatial_forward(
    me_ref, x0, x1, x2, x3, mod, gains, wt, wo, q_o, k_o, v_o, st_o, p0, p1, p2, p3, xrow,
    modc, xs, both, lines, square,
):
    me = me_ref[0]
    gain_q, gain_k = gain_columns(gains, 0, square)
    modc[...] = turned_lines(mod, lines)
    for d, x in enumerate((x0, x1, x2, x3)):
        xs[part_of(me, d), :] = x[...]
    stream = xs[...].astype(F32)
    mean = jnp.sum(stream, axis=0, keepdims=True) * (1.0 / WIDE)
    centred = stream - mean
    inverse = lax.rsqrt(jnp.sum(centred * centred, axis=0, keepdims=True) * (1.0 / WIDE) + EPS)
    normed = (centred * inverse * (1.0 + modc[:, 1:2]) + modc[:, 0:1]).astype(BF16)
    weights = wt[...].reshape(3 * PART, WIDE)
    projected = dot(weights, normed, (1, 0))
    query, inv_q = head_norm_t(projected[:PART], gain_q)
    key, inv_k = head_norm_t(projected[PART : 2 * PART], gain_k)
    q_o[...] = query
    k_o[...] = key
    v_o[...] = projected[2 * PART :].astype(BF16)
    st_o[0:4, :] = inv_q.reshape(PER, ROWS)
    st_o[4:8, :] = inv_k.reshape(PER, ROWS)
    st_o[8:9, :] = mean
    st_o[9:10, :] = inverse
    attended = softmax_pieces(query, key, v_o[...])
    branch = dot(attended, wo[...], (0, 0)).astype(BF16)
    both[...] = branch
    for d, partial in enumerate((p0, p1, p2, p3)):
        partial[...] = both[own_of(me, d), :]
    xrow[...] = xs[:, own_of(me, 0)].astype(F32).T.astype(BF16)


def temporal_group(normed, gated, gain_q, gain_k, weights, wo):
    n = normed.shape[0]
    left = lax.broadcasted_iota(jnp.int32, (n, n), 0)
    right = lax.broadcasted_iota(jnp.int32, (n, n), 1)
    mask = ((left & 1) == (right & 1)) & ((left // OWN) == (right // OWN))
    projected = dot(weights, normed, (1, 1))
    query, inv_q = head_norm_t(projected[:PART], gain_q)
    key, inv_k = head_norm_t(projected[PART : 2 * PART], gain_k)
    value = projected[2 * PART :].astype(BF16)
    grad_att = dot(wo, gated, (1, 1)).astype(BF16)
    attended, gq, gk, gv = [], [], [], []

    def start(rows):
        return dot(key[rows], query[rows], (0, 0)), dot(value[rows], grad_att[rows], (0, 0))

    for rows, (scores, grad_probs) in one_ahead(start):
        q, k, v, da = query[rows], key[rows], value[rows], grad_att[rows]
        unnormed = jnp.where(mask, jnp.exp2(scores * (SCALE * LOG2E)), 0.0)
        probs = unnormed * (1.0 / jnp.sum(unnormed, axis=0, keepdims=True))
        rounded = probs.astype(BF16)
        attended.append(dot(v, rounded, (1, 0)))
        inner = jnp.sum(grad_probs * probs, axis=0, keepdims=True)
        grad_scores = (probs * (grad_probs - inner)).astype(BF16)
        gv.append(dot(da, rounded, (1, 1)))
        gq.append(dot(k, grad_scores, (1, 0)) * SCALE)
        gk.append(dot(q, grad_scores, (1, 1)) * SCALE)
    attended = jnp.concatenate(attended, axis=0).astype(BF16)
    gq = jnp.concatenate(gq, axis=0).astype(BF16)
    gk = jnp.concatenate(gk, axis=0).astype(BF16)
    gv = jnp.concatenate(gv, axis=0).astype(BF16)
    dq = head_back_t(gq, query, inv_q, gain_q)
    dk = head_back_t(gk, key, inv_k, gain_k)
    stacked = jnp.concatenate([dq, dk, gv], axis=0)
    return dot(stacked, weights, (0, 0)), dot(attended, wo, (0, 0))


def temporal_own(tc0, tc1, mod, gains, wt, wo, gn_o, br_o, normed_o, gated_o, square):
    both = jnp.concatenate([tc0[...], tc1[...]], axis=0)
    stream, incoming = both[:, :WIDE].astype(F32), both[:, WIDE:].astype(F32)
    mean = jnp.sum(stream, axis=1, keepdims=True) * (1.0 / WIDE)
    centred = stream - mean
    inverse = lax.rsqrt(jnp.sum(centred * centred, axis=1, keepdims=True) * (1.0 / WIDE) + EPS)
    normed = (centred * inverse * (1.0 + mod[1, 1:2, :]) + mod[0, 1:2, :]).astype(BF16)
    gated = (mod[2, 1:2, :] * incoming).astype(BF16)
    normed_o[...] = normed
    gated_o[...] = gated
    term, branch = temporal_group(
        normed, gated, *gain_columns(gains, 1, square), wt[...].reshape(3 * PART, WIDE), wo[...]
    )
    gn_o[...] = term.astype(BF16)
    br_o[...] = branch.astype(BF16)


def temporal_far(
    at_ref, normed, gated, gn_r, br_r, gains, w0, w1, w2, w3, gn0, gn1, op0, op1, ws, square
):
    for d, w in enumerate((w0, w1, w2, w3)):
        ws[pl.ds(pl.multiple_of(((at_ref[0] + d) & 3) * PART, 32), PART), :] = w[...]
    term, branch = temporal_group(
        normed[...],
        gated[...],
        *gain_columns(gains, 1, square),
        ws[: 3 * PART, :],
        ws[3 * PART :, :],
    )
    term = term + gn_r[...].astype(F32)
    branch = branch + br_r[...].astype(F32)
    gn0[...] = term[:OWN]
    gn1[...] = term[OWN:].astype(BF16)
    op0[...] = branch[:OWN]
    op1[...] = branch[OWN:].astype(BF16)


def temporal_finish(tc0, gn0, gn1, op0, op1, mod, gm_o, mixed_o):
    stream = tc0[:, :WIDE].astype(F32)
    mean = jnp.sum(stream, axis=1, keepdims=True) * (1.0 / WIDE)
    shifted = stream - mean
    inverse = lax.rsqrt(jnp.sum(shifted * shifted, axis=1, keepdims=True) * (1.0 / WIDE) + EPS)
    centred = shifted * inverse
    scaled = (gn0[...] + gn1[...].astype(F32)) * (1.0 + mod[1, 1:2, :])
    first = jnp.sum(scaled, axis=1, keepdims=True) * (1.0 / WIDE)
    second = jnp.sum(scaled * centred, axis=1, keepdims=True) * (1.0 / WIDE)
    gm_o[...] = (tc0[:, WIDE:].astype(F32) + inverse * (scaled - first - centred * second)).astype(BF16)
    mixed_o[...] = (stream + mod[2, 1:2, :] * (op0[...] + op1[...].astype(F32))).astype(BF16)


def backward_half(queries, grad_att, k_r, v_r):
    gq, gk, gv = [], [], []

    def start(rows):
        return dot(k_r[rows, :], queries[rows], (0, 0)), dot(v_r[rows, :], grad_att[rows], (0, 0))

    for rows, (scores, grad_probs) in one_ahead(start):
        q, k, da = queries[rows], k_r[rows, :], grad_att[rows]
        unnormed = jnp.exp2(scores * (SCALE * LOG2E))
        probs = unnormed * (1.0 / jnp.sum(unnormed, axis=0, keepdims=True))
        rounded = probs.astype(BF16)
        inner = jnp.sum(grad_probs * probs, axis=0, keepdims=True)
        grad_scores = (probs * (grad_probs - inner)).astype(BF16)
        gv.append(dot(da, rounded, (1, 1)))
        gk.append(dot(q, grad_scores, (1, 1)))
        gq.append(dot(k, grad_scores, (1, 0)) * SCALE)
    return [jnp.concatenate(g, axis=0) for g in (gq, gk, gv)]


def gated_half(me, d, ga, gb, mod, rows):
    rows[core_of(me, d), :] = (mod[2, 0:1, :] * ga[...].astype(F32)).astype(BF16)
    rows[core_of(me, d ^ 1), :] = (mod[2, 0:1, :] * gb[...].astype(F32)).astype(BF16)
    return rows[...]


def spatial_backward_own(
    me_ref, g0, g1, q_r, k_r, v_r, mod, wo, gq_o, gk_o, gv_o, rows
):
    me = me_ref[0]
    gated = gated_half(me, 0, g0, g1, mod, rows)
    grad_att = dot(wo[...], gated, (1, 1)).astype(BF16)
    gq, gk, gv = backward_half(q_r[:, half_of(me, 0)], grad_att, k_r, v_r)
    gq_o[...] = gq.astype(BF16)
    gk_o[...] = gk
    gv_o[...] = gv


def norm_sums(part, normed, inverse, gains, uw, start):
    n = part.shape[1]
    grad = part.astype(F32)
    before = normed.astype(F32)
    if inverse is not None:
        before = (before * (1.0 / gains)).reshape(PER, HEAD, n) * (1.0 / inverse)
        before = before.reshape(PART, n)
    shift, scale = uw[start : start + PART, 0:1], uw[start : start + PART, 3:4]
    first = jnp.sum(grad * scale, axis=0, keepdims=True)
    return first, jnp.sum(grad * (before - shift), axis=0, keepdims=True)


def spatial_backward_far(
    me_ref, g2, g3, q_r, k_r, v_r, st, gq_r, gk_r, gv_r, mod, gains, uw_r, wo, wn,
    p2, p3, stacked_o, rs_o, rows, gq_s, square,
):
    me = me_ref[0]
    gated = gated_half(me, 2, g2, g3, mod, rows)
    grad_att = dot(wo[...], gated, (1, 1)).astype(BF16)
    gq, gk, gv = backward_half(q_r[:, half_of(me, 1)], grad_att, k_r, v_r)
    gain_q, gain_k = gain_columns(gains, 0, square)
    gq_s[:, half_of(me, 0)] = gq_r[...]
    gq_s[:, half_of(me, 1)] = gq.astype(BF16)
    gk = ((gk + gk_r[...]) * SCALE).astype(BF16)
    inv_q = st[0:4, :].reshape(PER, 1, ROWS)
    inv_k = st[4:8, :].reshape(PER, 1, ROWS)
    stacked_o[:PART, :] = head_back_t(gq_s[...], q_r[...], inv_q, gain_q)
    stacked_o[PART : 2 * PART, :] = head_back_t(gk, k_r[...], inv_k, gain_k)
    stacked_o[2 * PART :, :] = (gv + gv_r[...]).astype(BF16)
    stacked = stacked_o[...]
    turned = wn
    for d, partial in ((3, p3), (2, p2)):
        partial[...] = dot(turned[part_of(me, d), :], stacked, (1, 0)).astype(BF16)
    uw = uw_r[...].T
    sums = [
        norm_sums(stacked[:PART], q_r[...], inv_q, gain_q, uw, 0),
        norm_sums(stacked[PART : 2 * PART], k_r[...], inv_k, gain_k, uw, PART),
        norm_sums(stacked[2 * PART :], v_r[...], None, None, uw, 2 * PART),
    ]
    rs_o[...] = jnp.zeros_like(rs_o)
    rs_o[0:1, :] = sums[0][0] + sums[1][0] + sums[2][0]
    rs_o[1:2, :] = sums[0][1] + sums[1][1] + sums[2][1]


def spatial_backward_last(me_ref, stacked_r, g0, g1, g2, g3, wn, p0, p1a, p1b, gown, rows):
    me = me_ref[0]
    stacked = stacked_r[...]
    turned = wn
    part = dot(turned[part_of(me, 1), :], stacked, (1, 0)).astype(BF16)
    p1a[...] = part[: PART // 2]
    p1b[...] = part[PART // 2 :]
    p0[...] = dot(turned[part_of(me, 0), :], stacked, (1, 0)).astype(BF16)
    for d, g in enumerate((g0, g1, g2, g3)):
        rows[...] = g[...].astype(F32).T
        gown[:, own_of(me, d)] = rows[part_of(me, 0), :].astype(BF16)


def spatial_finish(me_ref, p0, m1a, m1b, o2, rs, more, st, x0, gown, mod, out_o, lines, modc):
    modc[...] = turned_lines(mod, lines)
    m1 = jnp.concatenate([m1a[...], m1b[...]], axis=0)
    grad = p0[...].astype(F32) + m1.astype(F32) + o2[...].astype(F32)
    inverse = st[9:10, :]
    scaled = grad * (1.0 + modc[part_of(me_ref[0], 0), 1:2])
    centred = (x0[...].astype(F32) - st[8:9, :]) * inverse
    first = (rs[0:1, :] + more[0:1, :]) * (1.0 / WIDE)
    second = (rs[1:2, :] + more[1:2, :]) * (1.0 / WIDE)
    out_o[...] = (gown[...].astype(F32) + inverse * (scaled - first - centred * second)).astype(BF16)


def split_columns(me_ref, columns, c0, c1, c23):
    me = me_ref[0]
    c0[...] = columns[:, own_of(me, 0)]
    c1[...] = columns[:, own_of(me, 1)]
    c23[:PART, :] = columns[:, own_of(me, 2)]
    c23[PART:, :] = columns[:, own_of(me, 3)]


def place_columns(me_ref, c0, c1, c2, c3, out_o):
    me = me_ref[0]
    for d, c in enumerate((c0[...], c1[...], c2[:PART, :], c3[PART:, :])):
        out_o[:, own_of(me, d)] = c


def gather_rows(me_ref, c0, c1, c2, c3, wt, mod, rows_o, wn_o, uw_o, cs, lines):
    me = me_ref[0]
    weights = wt[...].reshape(3 * PART, WIDE)
    wn_o[...] = weights.T
    uw_o[...] = dot(weights, turned_lines(mod, lines).astype(BF16), (1, 0)).T
    for d, c in enumerate((c0[...], c1[...], c2[:PART, :], c3[PART:, :])):
        cs[part_of(me, d), :] = c.astype(F32)
    rows_o[...] = cs[...].T.astype(BF16)


def split_rows(me_ref, rows, c0, c1, c23, cs):
    me = me_ref[0]
    cs[...] = rows[:, WIDE:].astype(F32).T
    c0[...] = cs[part_of(me, 0), :].astype(BF16)
    c1[...] = cs[part_of(me, 1), :].astype(BF16)
    c23[:PART, :] = cs[part_of(me, 2), :].astype(BF16)
    c23[PART:, :] = cs[part_of(me, 3), :].astype(BF16)


def swap(values, d):
    return lax.ppermute(values, "head", [(i, i ^ d) for i in range(4)])


def exchange(parts):
    mine, mate, both = parts
    far = swap(both, 2)
    return [mine, swap(mate, 1), far, swap(far, 1)]


def across_seq(one, two):
    rows = jnp.concatenate([one, two], axis=1).reshape(64, 2, 2 * WIDE)
    moved = lax.all_to_all(rows, "seq", split_axis=0, concat_axis=0, tiled=True)
    return moved.reshape(OWN, 2 * WIDE)


def from_neighbour(chunk):
    index = [(s, h) for s in range(64) for h in range(4)]
    near = [(s * 4 + h, (s ^ 4) * 4 + (h ^ 2)) for s, h in index]
    return lax.ppermute(chunk, ("seq", "head"), near)


def round_x(chunk, d):
    return lax.ppermute(chunk, "seq", [(s // 4 * 4 + (s + d) % 4, s) for s in range(64)])


def on_device(tokens, cotangent, qkv_weight, out_weight, modulation, head_gains):
    me = lax.axis_index("head")
    mine = me.astype(jnp.int32).reshape(1)
    at = (lax.axis_index("seq") & 3).astype(jnp.int32)
    wt = jnp.transpose(qkv_weight, (0, 2, 3, 1))
    mod = jnp.transpose(modulation, (1, 0, 2))
    row = out((OWN, WIDE))
    col = out((PART, ROWS))
    piece = out((PART, OWN))
    square = pltpu.VMEM((8, 128), F32)

    x0 = tokens.T
    x2 = swap(x0, 2)
    x1 = swap(x0, 1)
    pieces = [piece, piece, out((2 * PART, OWN))]
    parts = list(call(split_columns, pieces, [mine, cotangent.T], smem=1))
    weights = [wt[0], wt[1], out_weight[0], out_weight[1]]
    chunk = lax.select_n(at, wt[1, 0], wt[1, 1], wt[1, 2], out_weight[1])
    x2, weights, parts[0] = lax.optimization_barrier((x2, weights, parts[0]))
    wt_s, wt_t, wo_s, wo_t = weights
    x3 = swap(x2, 1)
    parts = exchange(parts)
    near = from_neighbour(chunk)

    query, key, value, stats, p0, p1, p2, p3, xrow = call(
        spatial_forward,
        [col] * 3 + [out((16, ROWS), F32)] + [row] * 5,
        [mine, x0, x1, x2, x3, mod, head_gains, wt_s, wo_s],
        [pltpu.VMEM((WIDE, 8), F32), pltpu.VMEM((WIDE, ROWS), BF16),
         pltpu.VMEM((ROWS, WIDE), BF16), pltpu.VMEM((8, WIDE), F32), square],
        smem=1,
    )
    m3, near, *parts = lax.optimization_barrier((swap(p3, 1), near, *parts))
    m1 = swap(p1, 1)
    chip = (p2.astype(F32) + m3.astype(F32)).astype(BF16)
    far = swap(chip, 2)
    cot0, wn, uw = call(
        gather_rows, [row, out((WIDE, 3 * PART)), out((8, 3 * PART), F32)],
        [mine, *parts, wt_s, mod],
        [pltpu.VMEM((WIDE, OWN), F32), pltpu.VMEM((8, WIDE), F32)], smem=1, behind=[chip],
    )

    chunk = lax.select_n(at ^ 2, wt[1, 0], wt[1, 1], wt[1, 2], out_weight[1])
    chunk, far = lax.optimization_barrier((chunk, far))
    second = from_neighbour(chunk)
    others = [near, round_x(near, 1), second, round_x(near, 3)]

    branch = p0.astype(F32) + m1.astype(F32) + far.astype(F32)
    middle = (xrow.astype(F32) + modulation[0, 2][None] * branch).astype(BF16)

    tc0 = across_seq(middle, cot0)
    tc1 = swap(tc0, 1)
    gn, br, normed, gated = call(
        temporal_own, [out((2 * OWN, WIDE))] * 4,
        [tc0, tc1, mod, head_gains, wt_t, wo_t],
        [square],
    )
    gn0, gn1, op0, op1 = call(
        temporal_far,
        [out((OWN, WIDE), F32), row, out((OWN, WIDE), F32), row],
        [at.reshape(1), normed, gated, gn, br, head_gains, *others],
        [pltpu.VMEM((4 * PART, WIDE), BF16), square],
        smem=1,
    )
    gn1, op1 = swap(gn1, 1), swap(op1, 1)
    grad_middle, mixed_rows = call(
        temporal_finish, [row] * 2, [tc0, gn0, gn1, op0, op1, mod]
    )

    moved = across_seq(grad_middle, mixed_rows)
    g0 = moved[:, :WIDE]
    g2 = swap(g0, 2)
    g1 = swap(g0, 1)
    gq, gk, gv = call(
        spatial_backward_own,
        [out((PART, 2 * OWN)), out((PART, ROWS), F32), out((PART, ROWS), F32)],
        [mine, g0, g1, query, key, value, mod, wo_s],
        [pltpu.VMEM((2 * OWN, WIDE), BF16)],
        smem=1,
    )
    parts = call(
        split_rows, pieces, [mine, moved], [pltpu.VMEM((WIDE, OWN), F32)], smem=1
    )
    g2, gq, *parts = lax.optimization_barrier((g2, gq, *parts))
    g3 = swap(g2, 1)
    parts = exchange(parts)
    p2, p3, stacked, sums = call(
        spatial_backward_far,
        [col, col, out((3 * PART, ROWS)), out((8, ROWS), F32)],
        [mine, g2, g3, query, key, value, stats, gq, gk, gv, mod, head_gains, uw, wo_s,
         wn],
        [pltpu.VMEM((2 * OWN, WIDE), BF16), pltpu.VMEM((PART, ROWS), BF16), square],
        smem=1,
    )
    m3, other, *parts = lax.optimization_barrier((swap(p3, 1), swap(sums, 1), *parts))
    chip = (p2.astype(F32) + m3.astype(F32)).astype(BF16)
    far = swap(chip, 2)
    sums = sums + other
    more = swap(sums, 2)
    p0, p1a, p1b, gown = call(
        spatial_backward_last,
        [col, out((PART // 2, ROWS)), out((PART // 2, ROWS)), col],
        [mine, stacked, g0, g1, g2, g3, wn],
        [pltpu.VMEM((WIDE, OWN), F32)],
        smem=1,
        behind=[chip],
    )
    m1a, m1b = swap(p1a, 1), swap(p1b, 1)

    (mixed,) = call(place_columns, [col], [mine, *parts], smem=1, behind=[p0])

    (grad,) = call(
        spatial_finish, [col], [mine, p0, m1a, m1b, far, sums, more, stats, x0, gown, mod],
        [pltpu.VMEM((8, WIDE), F32), pltpu.VMEM((WIDE, 8), F32)],
        smem=1,
    )
    return (mixed.T, grad.T)


def solution(mesh):
    in_specs = (
        P("seq", "head"),
        P("seq", "head"),
        P(None, None, None, "head"),
        P(None, "head", None),
        P(),
        P(),
    )
    out_specs = (P("seq", "head"), P("seq", "head"))
    return jax.shard_map(
        on_device, mesh=mesh, in_specs=in_specs, out_specs=out_specs, check_vma=False
    )
```

```python
import jax
import jax.numpy as jnp
from jax import lax
from jax.experimental import pallas as pl
from jax.experimental.pallas import tpu as pltpu
from jax.sharding import PartitionSpec as P

EPS = 1e-06
HEAD = 72
PER = 4
WIDE = 1152
PART = 288
ROWS = 512
OWN = 128
LOG2E = 1.4426950408889634
SCALE = HEAD**-0.5
F32 = jnp.float32
BF16 = jnp.bfloat16
VMEM_LIMIT = 56 * 1024 * 1024


def dot(a, b, over):
    return lax.dot_general(a, b, (((over[0],), (over[1],)), ((), ())), preferred_element_type=F32)


def call(body, outs, operands, scratch=(), smem=0, behind=()):
    n, skip = len(operands), len(behind)
    specs = [
        pl.BlockSpec(memory_space=pltpu.SMEM if i < smem else pltpu.VMEM) for i in range(n)
    ] + [pl.BlockSpec(memory_space=pl.ANY)] * skip

    def run(*refs):
        body(*refs[:n], *refs[n + skip :])

    return pl.pallas_call(
        run,
        out_shape=list(outs),
        in_specs=specs,
        out_specs=[pl.BlockSpec(memory_space=pltpu.VMEM)] * len(outs),
        scratch_shapes=list(scratch),
        compiler_params=pltpu.CompilerParams(vmem_limit_bytes=VMEM_LIMIT),
        cost_estimate=pl.CostEstimate(flops=1, bytes_accessed=1, transcendentals=0),
    )(*operands, *behind)


def out(shape, dtype=BF16):
    return jax.ShapeDtypeStruct(shape, dtype)


def head_norm_t(part, gains):
    n = part.shape[1]
    cube = part.reshape(PER, HEAD, n)
    inverse = lax.rsqrt(jnp.sum(cube * cube, axis=1, keepdims=True) * (1.0 / HEAD) + EPS)
    return (cube * inverse * gains.reshape(PER, HEAD, 1)).reshape(PART, n).astype(BF16), inverse


def head_back_t(incoming, normed, inverse, gains):
    n = incoming.shape[1]
    grad = incoming.astype(F32).reshape(PER, HEAD, n)
    norm = normed.astype(F32).reshape(PER, HEAD, n)
    gain = gains.reshape(PER, HEAD, 1)
    inner = jnp.sum(norm * grad, axis=1, keepdims=True) * (1.0 / HEAD)
    return (inverse * (gain * grad - norm * (1.0 / gain) * inner)).reshape(PART, n).astype(BF16)


def turned_lines(mod, lines):
    lines[...] = jnp.zeros_like(lines)
    for i in range(3):
        lines[i : i + 1, :] = mod[i, 0:1, :]
    lines[3:4, :] = 1.0 + mod[1, 0:1, :]
    return lines[...].T


def gain_columns(gains, block, square):
    square[...] = jnp.zeros_like(square)
    square[0:2, 0:HEAD] = gains[block]
    turned = square[...].T
    return [jnp.concatenate([turned[:HEAD, i : i + 1]] * PER, axis=0) for i in range(2)]


def one_ahead(start, depth=2):
    heads = [slice(h * HEAD, (h + 1) * HEAD) for h in range(PER)]
    ahead = [start(rows) for rows in heads[:depth]]
    for h, rows in enumerate(heads):
        if h + depth < PER:
            ahead.append(start(heads[h + depth]))
        yield rows, ahead.pop(0)


def softmax_pieces(query, key, value):
    pieces = []
    for rows, scores in one_ahead(lambda rows: dot(key[rows], query[rows], (0, 0))):
        unnormed = jnp.exp2(scores * (SCALE * LOG2E))
        total = jnp.sum(unnormed, axis=0, keepdims=True)
        pieces.append(dot(value[rows], unnormed.astype(BF16), (1, 0)) * (1.0 / total))
    return jnp.concatenate(pieces, axis=0).astype(BF16)


def half_of(me, other):
    return pl.ds(pl.multiple_of(((me // 2) ^ other) * 2 * OWN, 2 * OWN), 2 * OWN)


def core_of(me, d):
    return pl.ds(pl.multiple_of(((me ^ d) & 1) * OWN, OWN), OWN)


def part_of(me, d):
    return pl.ds(pl.multiple_of((me ^ d) * PART, 32), PART)


def own_of(me, d):
    return pl.ds(pl.multiple_of((me ^ d) * OWN, OWN), OWN)


def spatial_forward(
    me_ref, x0, x1, x2, x3, mod, gains, wt, wo, q_o, k_o, v_o, st_o, p0, p1, p2, p3, xrow,
    modc, xs, both, lines, square,
):
    me = me_ref[0]
    gain_q, gain_k = gain_columns(gains, 0, square)
    modc[...] = turned_lines(mod, lines)
    for d, x in enumerate((x0, x1, x2, x3)):
        xs[part_of(me, d), :] = x[...]
    stream = xs[...].astype(F32)
    mean = jnp.sum(stream, axis=0, keepdims=True) * (1.0 / WIDE)
    centred = stream - mean
    inverse = lax.rsqrt(jnp.sum(centred * centred, axis=0, keepdims=True) * (1.0 / WIDE) + EPS)
    normed = (centred * inverse * (1.0 + modc[:, 1:2]) + modc[:, 0:1]).astype(BF16)
    weights = wt[...].reshape(3 * PART, WIDE)
    projected = dot(weights, normed, (1, 0))
    query, inv_q = head_norm_t(projected[:PART], gain_q)
    key, inv_k = head_norm_t(projected[PART : 2 * PART], gain_k)
    q_o[...] = query
    k_o[...] = key
    v_o[...] = projected[2 * PART :].astype(BF16)
    st_o[0:4, :] = inv_q.reshape(PER, ROWS)
    st_o[4:8, :] = inv_k.reshape(PER, ROWS)
    st_o[8:9, :] = mean
    st_o[9:10, :] = inverse
    attended = softmax_pieces(query, key, v_o[...])
    branch = dot(attended, wo[...], (0, 0)).astype(BF16)
    both[...] = branch
    for d, partial in enumerate((p0, p1, p2, p3)):
        partial[...] = both[own_of(me, d), :]
    xrow[...] = xs[:, own_of(me, 0)].astype(F32).T.astype(BF16)


def temporal_group(normed, gated, gain_q, gain_k, weights, wo):
    n = normed.shape[0]
    left = lax.broadcasted_iota(jnp.int32, (n, n), 0)
    right = lax.broadcasted_iota(jnp.int32, (n, n), 1)
    mask = ((left & 1) == (right & 1)) & ((left // OWN) == (right // OWN))
    projected = dot(weights, normed, (1, 1))
    query, inv_q = head_norm_t(projected[:PART], gain_q)
    key, inv_k = head_norm_t(projected[PART : 2 * PART], gain_k)
    value = projected[2 * PART :].astype(BF16)
    grad_att = dot(wo, gated, (1, 1)).astype(BF16)
    attended, gq, gk, gv = [], [], [], []

    def start(rows):
        return dot(key[rows], query[rows], (0, 0)), dot(value[rows], grad_att[rows], (0, 0))

    for rows, (scores, grad_probs) in one_ahead(start):
        q, k, v, da = query[rows], key[rows], value[rows], grad_att[rows]
        unnormed = jnp.where(mask, jnp.exp2(scores * (SCALE * LOG2E)), 0.0)
        probs = unnormed * (1.0 / jnp.sum(unnormed, axis=0, keepdims=True))
        rounded = probs.astype(BF16)
        attended.append(dot(v, rounded, (1, 0)))
        inner = jnp.sum(grad_probs * probs, axis=0, keepdims=True)
        grad_scores = (probs * (grad_probs - inner)).astype(BF16)
        gv.append(dot(da, rounded, (1, 1)))
        gq.append(dot(k, grad_scores, (1, 0)) * SCALE)
        gk.append(dot(q, grad_scores, (1, 1)) * SCALE)
    attended = jnp.concatenate(attended, axis=0).astype(BF16)
    gq = jnp.concatenate(gq, axis=0).astype(BF16)
    gk = jnp.concatenate(gk, axis=0).astype(BF16)
    gv = jnp.concatenate(gv, axis=0).astype(BF16)
    dq = head_back_t(gq, query, inv_q, gain_q)
    dk = head_back_t(gk, key, inv_k, gain_k)
    stacked = jnp.concatenate([dq, dk, gv], axis=0)
    return dot(stacked, weights, (0, 0)), dot(attended, wo, (0, 0))


def temporal_own(tc0, tc1, mod, gains, wt, wo, gn_o, br_o, normed_o, gated_o, square):
    both = jnp.concatenate([tc0[...], tc1[...]], axis=0)
    stream, incoming = both[:, :WIDE].astype(F32), both[:, WIDE:].astype(F32)
    mean = jnp.sum(stream, axis=1, keepdims=True) * (1.0 / WIDE)
    centred = stream - mean
    inverse = lax.rsqrt(jnp.sum(centred * centred, axis=1, keepdims=True) * (1.0 / WIDE) + EPS)
    normed = (centred * inverse * (1.0 + mod[1, 1:2, :]) + mod[0, 1:2, :]).astype(BF16)
    gated = (mod[2, 1:2, :] * incoming).astype(BF16)
    normed_o[...] = normed
    gated_o[...] = gated
    term, branch = temporal_group(
        normed, gated, *gain_columns(gains, 1, square), wt[...].reshape(3 * PART, WIDE), wo[...]
    )
    gn_o[...] = term.astype(BF16)
    br_o[...] = branch.astype(BF16)


def temporal_far(
    at_ref, normed, gated, gn_r, br_r, gains, w0, w1, w2, w3, gn0, gn1, op0, op1, ws, square
):
    for d, w in enumerate((w0, w1, w2, w3)):
        ws[pl.ds(pl.multiple_of(((at_ref[0] + d) & 3) * PART, 32), PART), :] = w[...]
    term, branch = temporal_group(
        normed[...],
        gated[...],
        *gain_columns(gains, 1, square),
        ws[: 3 * PART, :],
        ws[3 * PART :, :],
    )
    term = term + gn_r[...].astype(F32)
    branch = branch + br_r[...].astype(F32)
    gn0[...] = term[:OWN]
    gn1[...] = term[OWN:].astype(BF16)
    op0[...] = branch[:OWN]
    op1[...] = branch[OWN:].astype(BF16)


def temporal_finish(tc0, gn0, gn1, op0, op1, mod, out_o):
    stream = tc0[:, :WIDE].astype(F32)
    mean = jnp.sum(stream, axis=1, keepdims=True) * (1.0 / WIDE)
    shifted = stream - mean
    inverse = lax.rsqrt(jnp.sum(shifted * shifted, axis=1, keepdims=True) * (1.0 / WIDE) + EPS)
    centred = shifted * inverse
    scaled = (gn0[...] + gn1[...].astype(F32)) * (1.0 + mod[1, 1:2, :])
    first = jnp.sum(scaled, axis=1, keepdims=True) * (1.0 / WIDE)
    second = jnp.sum(scaled * centred, axis=1, keepdims=True) * (1.0 / WIDE)
    out_o[:, :WIDE] = (tc0[:, WIDE:].astype(F32) + inverse * (scaled - first - centred * second)).astype(BF16)
    out_o[:, WIDE:] = (stream + mod[2, 1:2, :] * (op0[...] + op1[...].astype(F32))).astype(BF16)


def backward_half(queries, grad_att, k_r, v_r):
    gq, gk, gv = [], [], []

    def start(rows):
        return dot(k_r[rows, :], queries[rows], (0, 0)), dot(v_r[rows, :], grad_att[rows], (0, 0))

    for rows, (scores, grad_probs) in one_ahead(start):
        q, k, da = queries[rows], k_r[rows, :], grad_att[rows]
        unnormed = jnp.exp2(scores * (SCALE * LOG2E))
        probs = unnormed * (1.0 / jnp.sum(unnormed, axis=0, keepdims=True))
        rounded = probs.astype(BF16)
        inner = jnp.sum(grad_probs * probs, axis=0, keepdims=True)
        grad_scores = (probs * (grad_probs - inner)).astype(BF16)
        gv.append(dot(da, rounded, (1, 1)))
        gk.append(dot(q, grad_scores, (1, 1)))
        gq.append(dot(k, grad_scores, (1, 0)) * SCALE)
    return [jnp.concatenate(g, axis=0) for g in (gq, gk, gv)]


def gated_half(me, d, ga, gb, mod, rows):
    rows[core_of(me, d), :] = (mod[2, 0:1, :] * ga[...].astype(F32)).astype(BF16)
    rows[core_of(me, d ^ 1), :] = (mod[2, 0:1, :] * gb[...].astype(F32)).astype(BF16)
    return rows[...]


def spatial_backward_own(
    me_ref, g0, g1, q_r, k_r, v_r, mod, wo, gq_o, gk_o, gv_o, rows
):
    me = me_ref[0]
    gated = gated_half(me, 0, g0, g1, mod, rows)
    grad_att = dot(wo[...], gated, (1, 1)).astype(BF16)
    gq, gk, gv = backward_half(q_r[:, half_of(me, 0)], grad_att, k_r, v_r)
    gq_o[...] = gq.astype(BF16)
    gk_o[...] = gk
    gv_o[...] = gv


def norm_sums(part, normed, inverse, gains, uw, start):
    n = part.shape[1]
    grad = part.astype(F32)
    before = normed.astype(F32)
    if inverse is not None:
        before = (before * (1.0 / gains)).reshape(PER, HEAD, n) * (1.0 / inverse)
        before = before.reshape(PART, n)
    shift, scale = uw[start : start + PART, 0:1], uw[start : start + PART, 3:4]
    first = jnp.sum(grad * scale, axis=0, keepdims=True)
    return first, jnp.sum(grad * (before - shift), axis=0, keepdims=True)


def spatial_backward_far(
    me_ref, g2, g3, q_r, k_r, v_r, st, gq_r, gk_r, gv_r, mod, gains, uw_r, wo, wn,
    p2, p3, stacked_o, rs_o, rows, gq_s, square,
):
    me = me_ref[0]
    gated = gated_half(me, 2, g2, g3, mod, rows)
    grad_att = dot(wo[...], gated, (1, 1)).astype(BF16)
    gq, gk, gv = backward_half(q_r[:, half_of(me, 1)], grad_att, k_r, v_r)
    gain_q, gain_k = gain_columns(gains, 0, square)
    gq_s[:, half_of(me, 0)] = gq_r[...]
    gq_s[:, half_of(me, 1)] = gq.astype(BF16)
    gk = ((gk + gk_r[...]) * SCALE).astype(BF16)
    inv_q = st[0:4, :].reshape(PER, 1, ROWS)
    inv_k = st[4:8, :].reshape(PER, 1, ROWS)
    stacked_o[:PART, :] = head_back_t(gq_s[...], q_r[...], inv_q, gain_q)
    stacked_o[PART : 2 * PART, :] = head_back_t(gk, k_r[...], inv_k, gain_k)
    stacked_o[2 * PART :, :] = (gv + gv_r[...]).astype(BF16)
    stacked = stacked_o[...]
    turned = wn
    for d, partial in ((3, p3), (2, p2)):
        partial[:PART, :] = dot(turned[part_of(me, d), :], stacked, (1, 0)).astype(BF16)
    uw = uw_r[...].T
    sums = [
        norm_sums(stacked[:PART], q_r[...], inv_q, gain_q, uw, 0),
        norm_sums(stacked[PART : 2 * PART], k_r[...], inv_k, gain_k, uw, PART),
        norm_sums(stacked[2 * PART :], v_r[...], None, None, uw, 2 * PART),
    ]
    both = [sum(s[i] for s in sums) for i in range(2)]
    rs_o[...] = jnp.concatenate([*both, jnp.zeros((6, ROWS), F32)], axis=0)
    tail = jnp.concatenate([*both, jnp.zeros((14, ROWS), F32)], axis=0).astype(BF16)
    p2[PART:, :] = tail
    p3[PART:, :] = tail


def spatial_backward_last(me_ref, stacked_r, g0, g1, g2, g3, wn, p0, p1a, p1b, gown, rows):
    me = me_ref[0]
    stacked = stacked_r[...]
    turned = wn
    part = dot(turned[part_of(me, 1), :], stacked, (1, 0)).astype(BF16)
    p1a[...] = part[: PART // 2]
    p1b[...] = part[PART // 2 :]
    p0[...] = dot(turned[part_of(me, 0), :], stacked, (1, 0)).astype(BF16)
    for d, g in enumerate((g0, g1, g2, g3)):
        rows[...] = g[...].astype(F32).T
        gown[:, own_of(me, d)] = rows[part_of(me, 0), :].astype(BF16)


def spatial_finish(me_ref, p0, m1a, m1b, o2, m3, rs, st, x0, gown, mod, out_o, lines, modc):
    modc[...] = turned_lines(mod, lines)
    m1 = jnp.concatenate([m1a[...], m1b[...]], axis=0)
    grad = p0[...].astype(F32) + m1.astype(F32) + o2[:PART, :].astype(F32)
    inverse = st[9:10, :]
    scaled = grad * (1.0 + modc[part_of(me_ref[0], 0), 1:2])
    centred = (x0[...].astype(F32) - st[8:9, :]) * inverse
    tails = o2[PART:, :].astype(F32) + m3[PART:, :].astype(F32)
    first = (rs[0:1, :] + tails[0:1]) * (1.0 / WIDE)
    second = (rs[1:2, :] + tails[1:2]) * (1.0 / WIDE)
    out_o[...] = (gown[...].astype(F32) + inverse * (scaled - first - centred * second)).astype(BF16)


def split_columns(me_ref, columns, c0, c1, c23):
    me = me_ref[0]
    c0[...] = columns[:, own_of(me, 0)]
    c1[...] = columns[:, own_of(me, 1)]
    c23[:PART, :] = columns[:, own_of(me, 2)]
    c23[PART:, :] = columns[:, own_of(me, 3)]


def place_columns(me_ref, c0, c1, c2, c3, out_o):
    me = me_ref[0]
    for d, c in enumerate((c0[...], c1[...], c2[:PART, :], c3[PART:, :])):
        out_o[:, own_of(me, d)] = c


def gather_rows(me_ref, c0, c1, c2, c3, wt, mod, rows_o, wn_o, uw_o, cs, lines):
    me = me_ref[0]
    weights = wt[...].reshape(3 * PART, WIDE)
    wn_o[...] = weights.T
    uw_o[...] = dot(weights, turned_lines(mod, lines).astype(BF16), (1, 0)).T
    for d, c in enumerate((c0[...], c1[...], c2[:PART, :], c3[PART:, :])):
        cs[part_of(me, d), :] = c.astype(F32)
    rows_o[...] = cs[...].T.astype(BF16)


def split_rows(me_ref, rows, c0, c1, c23, cs):
    me = me_ref[0]
    cs[...] = rows[:, WIDE:].astype(F32).T
    c0[...] = cs[part_of(me, 0), :].astype(BF16)
    c1[...] = cs[part_of(me, 1), :].astype(BF16)
    c23[:PART, :] = cs[part_of(me, 2), :].astype(BF16)
    c23[PART:, :] = cs[part_of(me, 3), :].astype(BF16)


def swap(values, d):
    return lax.ppermute(values, "head", [(i, i ^ d) for i in range(4)])


def exchange(parts):
    mine, mate, both = parts
    far = swap(both, 2)
    return [mine, swap(mate, 1), far, swap(far, 1)]


def across_seq(rows):
    rows = rows.reshape(64, 2, 2 * WIDE)
    moved = lax.all_to_all(rows, "seq", split_axis=0, concat_axis=0, tiled=True)
    return moved.reshape(OWN, 2 * WIDE)


def from_neighbour(chunk):
    index = [(s, h) for s in range(64) for h in range(4)]
    near = [(s * 4 + h, (s ^ 4) * 4 + (h ^ 2)) for s, h in index]
    return lax.ppermute(chunk, ("seq", "head"), near)


def round_x(chunk, d):
    return lax.ppermute(chunk, "seq", [(s // 4 * 4 + (s + d) % 4, s) for s in range(64)])


def on_device(tokens, cotangent, qkv_weight, out_weight, modulation, head_gains):
    me = lax.axis_index("head")
    mine = me.astype(jnp.int32).reshape(1)
    at = (lax.axis_index("seq") & 3).astype(jnp.int32)
    wt = jnp.transpose(qkv_weight, (0, 2, 3, 1))
    mod = jnp.transpose(modulation, (1, 0, 2))
    row = out((OWN, WIDE))
    col = out((PART, ROWS))
    piece = out((PART, OWN))
    square = pltpu.VMEM((8, 128), F32)

    x0 = tokens.T
    x2 = swap(x0, 2)
    x1 = swap(x0, 1)
    pieces = [piece, piece, out((2 * PART, OWN))]
    parts = list(call(split_columns, pieces, [mine, cotangent.T], smem=1))
    weights = [wt[0], wt[1], out_weight[0], out_weight[1]]
    chunk = lax.select_n(at, wt[1, 0], wt[1, 1], wt[1, 2], out_weight[1])
    x2, weights, parts[0] = lax.optimization_barrier((x2, weights, parts[0]))
    wt_s, wt_t, wo_s, wo_t = weights
    x3 = swap(x2, 1)
    parts = exchange(parts)
    near = from_neighbour(chunk)

    query, key, value, stats, p0, p1, p2, p3, xrow = call(
        spatial_forward,
        [col] * 3 + [out((16, ROWS), F32)] + [row] * 5,
        [mine, x0, x1, x2, x3, mod, head_gains, wt_s, wo_s],
        [pltpu.VMEM((WIDE, 8), F32), pltpu.VMEM((WIDE, ROWS), BF16),
         pltpu.VMEM((ROWS, WIDE), BF16), pltpu.VMEM((8, WIDE), F32), square],
        smem=1,
    )
    m3, near, parts[2], parts[3] = lax.optimization_barrier(
        (swap(p3, 1), near, parts[2], parts[3])
    )
    m1 = swap(p1, 1)
    chip = (p2.astype(F32) + m3.astype(F32)).astype(BF16)
    far = swap(chip, 2)
    cot0, wn, uw = call(
        gather_rows, [row, out((WIDE, 3 * PART)), out((8, 3 * PART), F32)],
        [mine, *parts, wt_s, mod],
        [pltpu.VMEM((WIDE, OWN), F32), pltpu.VMEM((8, WIDE), F32)], smem=1, behind=[chip],
    )

    chunk = lax.select_n(at ^ 2, wt[1, 0], wt[1, 1], wt[1, 2], out_weight[1])
    chunk, far = lax.optimization_barrier((chunk, far))
    second = from_neighbour(chunk)
    others = [near, round_x(near, 1), second, round_x(near, 3)]

    branch = p0.astype(F32) + m1.astype(F32) + far.astype(F32)
    middle = (xrow.astype(F32) + modulation[0, 2][None] * branch).astype(BF16)

    tc0 = across_seq(jnp.concatenate([middle, cot0], axis=1))
    tc1 = swap(tc0, 1)
    gn, br, normed, gated = call(
        temporal_own, [out((2 * OWN, WIDE))] * 4,
        [tc0, tc1, mod, head_gains, wt_t, wo_t],
        [square],
    )
    gn0, gn1, op0, op1 = call(
        temporal_far,
        [out((OWN, WIDE), F32), row, out((OWN, WIDE), F32), row],
        [at.reshape(1), normed, gated, gn, br, head_gains, *others],
        [pltpu.VMEM((4 * PART, WIDE), BF16), square],
        smem=1,
    )
    gn1, op1 = swap(gn1, 1), swap(op1, 1)
    (rows,) = call(
        temporal_finish, [out((OWN, 2 * WIDE))], [tc0, gn0, gn1, op0, op1, mod]
    )

    moved = across_seq(rows)
    g0 = moved[:, :WIDE]
    g2 = swap(g0, 2)
    g1 = swap(g0, 1)
    gq, gk, gv = call(
        spatial_backward_own,
        [out((PART, 2 * OWN)), out((PART, ROWS), F32), out((PART, ROWS), F32)],
        [mine, g0, g1, query, key, value, mod, wo_s],
        [pltpu.VMEM((2 * OWN, WIDE), BF16)],
        smem=1,
    )
    parts = call(split_rows, pieces, [mine, moved], [pltpu.VMEM((WIDE, OWN), F32)], smem=1)
    parts = list(parts)
    g2, gq, parts[0] = lax.optimization_barrier((g2, gq, parts[0]))
    g3 = swap(g2, 1)
    parts = exchange(parts)
    p2, p3, stacked, sums = call(
        spatial_backward_far,
        [out((PART + 16, ROWS))] * 2 + [out((3 * PART, ROWS)), out((8, ROWS), F32)],
        [mine, g2, g3, query, key, value, stats, gq, gk, gv, mod, head_gains, uw, wo_s,
         wn],
        [pltpu.VMEM((2 * OWN, WIDE), BF16), pltpu.VMEM((PART, ROWS), BF16), square],
        smem=1,
    )
    m3, parts[2], parts[3] = lax.optimization_barrier((swap(p3, 1), parts[2], parts[3]))
    chip = (p2.astype(F32) + m3.astype(F32)).astype(BF16)
    far = swap(chip, 2)
    p0, p1a, p1b, gown = call(
        spatial_backward_last,
        [col, out((PART // 2, ROWS)), out((PART // 2, ROWS)), col],
        [mine, stacked, g0, g1, g2, g3, wn],
        [pltpu.VMEM((WIDE, OWN), F32)],
        smem=1,
        behind=[chip],
    )
    m1a, m1b = swap(p1a, 1), swap(p1b, 1)

    (mixed,) = call(place_columns, [col], [mine, *parts], smem=1, behind=[p0])

    (grad,) = call(
        spatial_finish, [col], [mine, p0, m1a, m1b, far, m3, sums, stats, x0, gown, mod],
        [pltpu.VMEM((8, WIDE), F32), pltpu.VMEM((WIDE, 8), F32)],
        smem=1,
    )
    return (mixed.T, grad.T)


def solution(mesh):
    in_specs = (
        P("seq", "head"),
        P("seq", "head"),
        P(None, None, None, "head"),
        P(None, "head", None),
        P(),
        P(),
    )
    out_specs = (P("seq", "head"), P("seq", "head"))
    return jax.shard_map(
        on_device, mesh=mesh, in_specs=in_specs, out_specs=out_specs, check_vma=False
    )
```

```python
import jax
import jax.numpy as jnp
from jax import lax
from jax.experimental import pallas as pl
from jax.experimental.pallas import tpu as pltpu
from jax.sharding import PartitionSpec as P

EPS = 1e-06
HEAD = 72
PER = 4
WIDE = 1152
PART = 288
ROWS = 512
OWN = 128
LOG2E = 1.4426950408889634
SCALE = HEAD**-0.5
F32 = jnp.float32
BF16 = jnp.bfloat16
VMEM_LIMIT = 56 * 1024 * 1024


def dot(a, b, over):
    return lax.dot_general(a, b, (((over[0],), (over[1],)), ((), ())), preferred_element_type=F32)


def call(body, outs, operands, scratch=(), smem=0, behind=()):
    n, skip = len(operands), len(behind)
    specs = [
        pl.BlockSpec(memory_space=pltpu.SMEM if i < smem else pltpu.VMEM) for i in range(n)
    ] + [pl.BlockSpec(memory_space=pl.ANY)] * skip

    def run(*refs):
        body(*refs[:n], *refs[n + skip :])

    return pl.pallas_call(
        run,
        out_shape=list(outs),
        in_specs=specs,
        out_specs=[pl.BlockSpec(memory_space=pltpu.VMEM)] * len(outs),
        scratch_shapes=list(scratch),
        compiler_params=pltpu.CompilerParams(vmem_limit_bytes=VMEM_LIMIT),
        cost_estimate=pl.CostEstimate(flops=1, bytes_accessed=1, transcendentals=0),
    )(*operands, *behind)


def out(shape, dtype=BF16):
    return jax.ShapeDtypeStruct(shape, dtype)


def head_norm_t(part, gains):
    n = part.shape[1]
    cube = part.reshape(PER, HEAD, n)
    inverse = lax.rsqrt(jnp.sum(cube * cube, axis=1, keepdims=True) * (1.0 / HEAD) + EPS)
    return (cube * inverse * gains.reshape(PER, HEAD, 1)).reshape(PART, n).astype(BF16), inverse


def head_back_t(incoming, normed, inverse, gains):
    n = incoming.shape[1]
    grad = incoming.astype(F32).reshape(PER, HEAD, n)
    norm = normed.astype(F32).reshape(PER, HEAD, n)
    gain = gains.reshape(PER, HEAD, 1)
    inner = jnp.sum(norm * grad, axis=1, keepdims=True) * (1.0 / HEAD)
    return (inverse * (gain * grad - norm * (1.0 / gain) * inner)).reshape(PART, n).astype(BF16)


def turned_lines(mod, lines):
    lines[...] = jnp.zeros_like(lines)
    for i in range(3):
        lines[i : i + 1, :] = mod[i, 0:1, :]
    lines[3:4, :] = 1.0 + mod[1, 0:1, :]
    return lines[...].T


def gain_columns(gains, block, square):
    square[...] = jnp.zeros_like(square)
    square[0:2, 0:HEAD] = gains[block]
    turned = square[...].T
    return [jnp.concatenate([turned[:HEAD, i : i + 1]] * PER, axis=0) for i in range(2)]


def one_ahead(start, depth=2):
    heads = [slice(h * HEAD, (h + 1) * HEAD) for h in range(PER)]
    ahead = [start(rows) for rows in heads[:depth]]
    for h, rows in enumerate(heads):
        if h + depth < PER:
            ahead.append(start(heads[h + depth]))
        yield rows, ahead.pop(0)


def softmax_pieces(query, key, value):
    pieces = []
    for rows, scores in one_ahead(lambda rows: dot(key[rows], query[rows], (0, 0))):
        unnormed = jnp.exp2(scores * (SCALE * LOG2E))
        total = jnp.sum(unnormed, axis=0, keepdims=True)
        pieces.append(dot(value[rows], unnormed.astype(BF16), (1, 0)) * (1.0 / total))
    return jnp.concatenate(pieces, axis=0).astype(BF16)


def half_of(me, other):
    return pl.ds(pl.multiple_of(((me // 2) ^ other) * 2 * OWN, 2 * OWN), 2 * OWN)


def core_of(me, d):
    return pl.ds(pl.multiple_of(((me ^ d) & 1) * OWN, OWN), OWN)


def part_of(me, d):
    return pl.ds(pl.multiple_of((me ^ d) * PART, 32), PART)


def own_of(me, d):
    return pl.ds(pl.multiple_of((me ^ d) * OWN, OWN), OWN)


def spatial_forward(
    me_ref, x0, x1, x2, x3, mod, gains, wt, wo, q_o, k_o, v_o, st_o, p0, p1, p2, p3, xrow,
    modc, xs, both, lines, square,
):
    me = me_ref[0]
    gain_q, gain_k = gain_columns(gains, 0, square)
    modc[...] = turned_lines(mod, lines)
    for d, x in enumerate((x0, x1, x2, x3)):
        xs[part_of(me, d), :] = x[...]
    stream = xs[...].astype(F32)
    mean = jnp.sum(stream, axis=0, keepdims=True) * (1.0 / WIDE)
    centred = stream - mean
    inverse = lax.rsqrt(jnp.sum(centred * centred, axis=0, keepdims=True) * (1.0 / WIDE) + EPS)
    normed = (centred * inverse * (1.0 + modc[:, 1:2]) + modc[:, 0:1]).astype(BF16)
    weights = wt[...].reshape(3 * PART, WIDE)
    projected = dot(weights, normed, (1, 0))
    query, inv_q = head_norm_t(projected[:PART], gain_q)
    key, inv_k = head_norm_t(projected[PART : 2 * PART], gain_k)
    q_o[...] = query
    k_o[...] = key
    v_o[...] = projected[2 * PART :].astype(BF16)
    st_o[0:4, :] = inv_q.reshape(PER, ROWS)
    st_o[4:8, :] = inv_k.reshape(PER, ROWS)
    st_o[8:9, :] = mean
    st_o[9:10, :] = inverse
    attended = softmax_pieces(query, key, v_o[...])
    branch = dot(attended, wo[...], (0, 0)).astype(BF16)
    both[...] = branch
    for d, partial in enumerate((p0, p1, p2, p3)):
        partial[...] = both[own_of(me, d), :]
    xrow[...] = xs[:, own_of(me, 0)].astype(F32).T.astype(BF16)


def temporal_group(normed, gated, gain_q, gain_k, weights, wo):
    n = normed.shape[0]
    left = lax.broadcasted_iota(jnp.int32, (n, n), 0)
    right = lax.broadcasted_iota(jnp.int32, (n, n), 1)
    mask = ((left & 1) == (right & 1)) & ((left // OWN) == (right // OWN))
    projected = dot(weights, normed, (1, 1))
    query, inv_q = head_norm_t(projected[:PART], gain_q)
    key, inv_k = head_norm_t(projected[PART : 2 * PART], gain_k)
    value = projected[2 * PART :].astype(BF16)
    grad_att = dot(wo, gated, (1, 1)).astype(BF16)
    attended, gq, gk, gv = [], [], [], []

    def start(rows):
        return dot(key[rows], query[rows], (0, 0)), dot(value[rows], grad_att[rows], (0, 0))

    for rows, (scores, grad_probs) in one_ahead(start):
        q, k, v, da = query[rows], key[rows], value[rows], grad_att[rows]
        unnormed = jnp.where(mask, jnp.exp2(scores * (SCALE * LOG2E)), 0.0)
        probs = unnormed * (1.0 / jnp.sum(unnormed, axis=0, keepdims=True))
        rounded = probs.astype(BF16)
        attended.append(dot(v, rounded, (1, 0)))
        inner = jnp.sum(grad_probs * probs, axis=0, keepdims=True)
        grad_scores = (probs * (grad_probs - inner)).astype(BF16)
        gv.append(dot(da, rounded, (1, 1)))
        gq.append(dot(k, grad_scores, (1, 0)) * SCALE)
        gk.append(dot(q, grad_scores, (1, 1)) * SCALE)
    attended = jnp.concatenate(attended, axis=0).astype(BF16)
    gq = jnp.concatenate(gq, axis=0).astype(BF16)
    gk = jnp.concatenate(gk, axis=0).astype(BF16)
    gv = jnp.concatenate(gv, axis=0).astype(BF16)
    dq = head_back_t(gq, query, inv_q, gain_q)
    dk = head_back_t(gk, key, inv_k, gain_k)
    stacked = jnp.concatenate([dq, dk, gv], axis=0)
    return dot(stacked, weights, (0, 0)), dot(attended, wo, (0, 0))


def temporal_own(tc0, tc1, mod, gains, wt, wo, gn_o, br_o, normed_o, gated_o, square):
    both = jnp.concatenate([tc0[...], tc1[...]], axis=0)
    stream, incoming = both[:, :WIDE].astype(F32), both[:, WIDE:].astype(F32)
    mean = jnp.sum(stream, axis=1, keepdims=True) * (1.0 / WIDE)
    centred = stream - mean
    inverse = lax.rsqrt(jnp.sum(centred * centred, axis=1, keepdims=True) * (1.0 / WIDE) + EPS)
    normed = (centred * inverse * (1.0 + mod[1, 1:2, :]) + mod[0, 1:2, :]).astype(BF16)
    gated = (mod[2, 1:2, :] * incoming).astype(BF16)
    normed_o[...] = normed
    gated_o[...] = gated
    term, branch = temporal_group(
        normed, gated, *gain_columns(gains, 1, square), wt[...].reshape(3 * PART, WIDE), wo[...]
    )
    gn_o[...] = term.astype(BF16)
    br_o[...] = branch.astype(BF16)


def temporal_far(
    at_ref, normed, gated, gn_r, br_r, gains, w0, w1, w2, w3, gn0, gn1, op0, op1, ws, square
):
    for d, w in enumerate((w0, w1, w2, w3)):
        ws[pl.ds(pl.multiple_of(((at_ref[0] + d) & 3) * PART, 32), PART), :] = w[...]
    term, branch = temporal_group(
        normed[...],
        gated[...],
        *gain_columns(gains, 1, square),
        ws[: 3 * PART, :],
        ws[3 * PART :, :],
    )
    term = term + gn_r[...].astype(F32)
    branch = branch + br_r[...].astype(F32)
    gn0[...] = term[:OWN]
    gn1[...] = term[OWN:].astype(BF16)
    op0[...] = branch[:OWN]
    op1[...] = branch[OWN:].astype(BF16)


def temporal_finish(tc0, gn0, gn1, op0, op1, mod, gm_o, mixed_o):
    stream = tc0[:, :WIDE].astype(F32)
    mean = jnp.sum(stream, axis=1, keepdims=True) * (1.0 / WIDE)
    shifted = stream - mean
    inverse = lax.rsqrt(jnp.sum(shifted * shifted, axis=1, keepdims=True) * (1.0 / WIDE) + EPS)
    centred = shifted * inverse
    scaled = (gn0[...] + gn1[...].astype(F32)) * (1.0 + mod[1, 1:2, :])
    first = jnp.sum(scaled, axis=1, keepdims=True) * (1.0 / WIDE)
    second = jnp.sum(scaled * centred, axis=1, keepdims=True) * (1.0 / WIDE)
    gm_o[...] = (tc0[:, WIDE:].astype(F32) + inverse * (scaled - first - centred * second)).astype(BF16)
    mixed_o[...] = (stream + mod[2, 1:2, :] * (op0[...] + op1[...].astype(F32))).astype(BF16)


def backward_half(queries, grad_att, k_r, v_r):
    gq, gk, gv = [], [], []

    def start(rows):
        return dot(k_r[rows, :], queries[rows], (0, 0)), dot(v_r[rows, :], grad_att[rows], (0, 0))

    for rows, (scores, grad_probs) in one_ahead(start):
        q, k, da = queries[rows], k_r[rows, :], grad_att[rows]
        unnormed = jnp.exp2(scores * (SCALE * LOG2E))
        probs = unnormed * (1.0 / jnp.sum(unnormed, axis=0, keepdims=True))
        rounded = probs.astype(BF16)
        inner = jnp.sum(grad_probs * probs, axis=0, keepdims=True)
        grad_scores = (probs * (grad_probs - inner)).astype(BF16)
        gv.append(dot(da, rounded, (1, 1)))
        gk.append(dot(q, grad_scores, (1, 1)))
        gq.append(dot(k, grad_scores, (1, 0)) * SCALE)
    return [jnp.concatenate(g, axis=0) for g in (gq, gk, gv)]


def gated_half(me, d, ga, gb, mod, rows):
    rows[core_of(me, d), :] = (mod[2, 0:1, :] * ga[...].astype(F32)).astype(BF16)
    rows[core_of(me, d ^ 1), :] = (mod[2, 0:1, :] * gb[...].astype(F32)).astype(BF16)
    return rows[...]


def spatial_backward_own(
    me_ref, g0, g1, q_r, k_r, v_r, mod, wo, gq_o, gk_o, gv_o, rows
):
    me = me_ref[0]
    gated = gated_half(me, 0, g0, g1, mod, rows)
    grad_att = dot(wo[...], gated, (1, 1)).astype(BF16)
    gq, gk, gv = backward_half(q_r[:, half_of(me, 0)], grad_att, k_r, v_r)
    gq_o[...] = gq.astype(BF16)
    gk_o[...] = gk
    gv_o[...] = gv


def norm_sums(part, normed, inverse, gains, uw, start):
    n = part.shape[1]
    grad = part.astype(F32)
    before = normed.astype(F32)
    if inverse is not None:
        before = (before * (1.0 / gains)).reshape(PER, HEAD, n) * (1.0 / inverse)
        before = before.reshape(PART, n)
    shift, scale = uw[start : start + PART, 0:1], uw[start : start + PART, 3:4]
    first = jnp.sum(grad * scale, axis=0, keepdims=True)
    return first, jnp.sum(grad * (before - shift), axis=0, keepdims=True)


def spatial_backward_far(
    me_ref, g2, g3, q_r, k_r, v_r, st, gq_r, gk_r, gv_r, mod, gains, uw_r, wo, wn,
    p2, p3, stacked_o, rs_o, rows, gq_s, square,
):
    me = me_ref[0]
    gated = gated_half(me, 2, g2, g3, mod, rows)
    grad_att = dot(wo[...], gated, (1, 1)).astype(BF16)
    gq, gk, gv = backward_half(q_r[:, half_of(me, 1)], grad_att, k_r, v_r)
    gain_q, gain_k = gain_columns(gains, 0, square)
    gq_s[:, half_of(me, 0)] = gq_r[...]
    gq_s[:, half_of(me, 1)] = gq.astype(BF16)
    gk = ((gk + gk_r[...]) * SCALE).astype(BF16)
    inv_q = st[0:4, :].reshape(PER, 1, ROWS)
    inv_k = st[4:8, :].reshape(PER, 1, ROWS)
    stacked_o[:PART, :] = head_back_t(gq_s[...], q_r[...], inv_q, gain_q)
    stacked_o[PART : 2 * PART, :] = head_back_t(gk, k_r[...], inv_k, gain_k)
    stacked_o[2 * PART :, :] = (gv + gv_r[...]).astype(BF16)
    stacked = stacked_o[...]
    turned = wn
    for d, partial in ((3, p3), (2, p2)):
        partial[...] = dot(turned[part_of(me, d), :], stacked, (1, 0)).astype(BF16)
    uw = uw_r[...].T
    sums = [
        norm_sums(stacked[:PART], q_r[...], inv_q, gain_q, uw, 0),
        norm_sums(stacked[PART : 2 * PART], k_r[...], inv_k, gain_k, uw, PART),
        norm_sums(stacked[2 * PART :], v_r[...], None, None, uw, 2 * PART),
    ]
    rs_o[...] = jnp.zeros_like(rs_o)
    rs_o[0:1, :] = sums[0][0] + sums[1][0] + sums[2][0]
    rs_o[1:2, :] = sums[0][1] + sums[1][1] + sums[2][1]


def spatial_backward_last(me_ref, stacked_r, g0, g1, g2, g3, wn, p0, p1a, p1b, gown, rows):
    me = me_ref[0]
    stacked = stacked_r[...]
    turned = wn
    part = dot(turned[part_of(me, 1), :], stacked, (1, 0)).astype(BF16)
    p1a[...] = part[: PART // 2]
    p1b[...] = part[PART // 2 :]
    p0[...] = dot(turned[part_of(me, 0), :], stacked, (1, 0)).astype(BF16)
    for d, g in enumerate((g0, g1, g2, g3)):
        rows[...] = g[...].astype(F32).T
        gown[:, own_of(me, d)] = rows[part_of(me, 0), :].astype(BF16)


def spatial_finish(me_ref, p0, m1a, m1b, o2, rs, more, st, x0, gown, mod, out_o, lines, modc):
    modc[...] = turned_lines(mod, lines)
    m1 = jnp.concatenate([m1a[...], m1b[...]], axis=0)
    grad = p0[...].astype(F32) + m1.astype(F32) + o2[...].astype(F32)
    inverse = st[9:10, :]
    scaled = grad * (1.0 + modc[part_of(me_ref[0], 0), 1:2])
    centred = (x0[...].astype(F32) - st[8:9, :]) * inverse
    first = (rs[0:1, :] + more[0:1, :]) * (1.0 / WIDE)
    second = (rs[1:2, :] + more[1:2, :]) * (1.0 / WIDE)
    out_o[...] = (gown[...].astype(F32) + inverse * (scaled - first - centred * second)).astype(BF16)


def split_columns(me_ref, columns, c0, c1, c23):
    me = me_ref[0]
    c0[...] = columns[:, own_of(me, 0)]
    c1[...] = columns[:, own_of(me, 1)]
    c23[:PART, :] = columns[:, own_of(me, 2)]
    c23[PART:, :] = columns[:, own_of(me, 3)]


def place_columns(me_ref, c0, c1, c2, c3, out_o):
    me = me_ref[0]
    for d, c in enumerate((c0[...], c1[...], c2[:PART, :], c3[PART:, :])):
        out_o[:, own_of(me, d)] = c


def gather_rows(me_ref, c0, c1, c2, c3, wt, mod, rows_o, wn_o, uw_o, cs, lines):
    me = me_ref[0]
    weights = wt[...].reshape(3 * PART, WIDE)
    wn_o[...] = weights.T
    uw_o[...] = dot(weights, turned_lines(mod, lines).astype(BF16), (1, 0)).T
    for d, c in enumerate((c0[...], c1[...], c2[:PART, :], c3[PART:, :])):
        cs[part_of(me, d), :] = c.astype(F32)
    rows_o[...] = cs[...].T.astype(BF16)


def split_rows(me_ref, rows, c0, c1, c23, cs):
    me = me_ref[0]
    cs[...] = rows[:, WIDE:].astype(F32).T
    c0[...] = cs[part_of(me, 0), :].astype(BF16)
    c1[...] = cs[part_of(me, 1), :].astype(BF16)
    c23[:PART, :] = cs[part_of(me, 2), :].astype(BF16)
    c23[PART:, :] = cs[part_of(me, 3), :].astype(BF16)


def swap(values, d):
    return lax.ppermute(values, "head", [(i, i ^ d) for i in range(4)])


def exchange(parts):
    mine, mate, both = parts
    far = swap(both, 2)
    return [mine, swap(mate, 1), far, swap(far, 1)]


def across_seq(one, two):
    rows = jnp.concatenate([one, two], axis=1).reshape(64, 2, 2 * WIDE)
    moved = lax.all_to_all(rows, "seq", split_axis=0, concat_axis=0, tiled=True)
    return moved.reshape(OWN, 2 * WIDE)


def from_neighbour(chunk, d):
    index = [(s, h) for s in range(64) for h in range(4)]
    near = [(s * 4 + h, (s ^ 4) * 4 + (h ^ d)) for s, h in index]
    return lax.ppermute(chunk, ("seq", "head"), near)


def round_x(chunk, d):
    return lax.ppermute(chunk, "seq", [(s // 4 * 4 + (s + d) % 4, s) for s in range(64)])


def on_device(tokens, cotangent, qkv_weight, out_weight, modulation, head_gains):
    me = lax.axis_index("head")
    mine = me.astype(jnp.int32).reshape(1)
    at = (lax.axis_index("seq") & 3).astype(jnp.int32)
    wt = jnp.transpose(qkv_weight, (0, 2, 3, 1))
    mod = jnp.transpose(modulation, (1, 0, 2))
    row = out((OWN, WIDE))
    col = out((PART, ROWS))
    piece = out((PART, OWN))
    square = pltpu.VMEM((8, 128), F32)

    x0 = tokens.T
    x2 = swap(x0, 2)
    x1 = swap(x0, 1)
    pieces = [piece, piece, out((2 * PART, OWN))]
    parts = list(call(split_columns, pieces, [mine, cotangent.T], smem=1))
    weights = [wt[0], wt[1], out_weight[0], out_weight[1]]
    x2, weights, parts[0] = lax.optimization_barrier((x2, weights, parts[0]))
    wt_s, wt_t, wo_s, wo_t = weights
    x3 = swap(x2, 1)
    parts = exchange(parts)
    query, key, value, stats, p0, p1, p2, p3, xrow = call(
        spatial_forward,
        [col] * 3 + [out((16, ROWS), F32)] + [row] * 5,
        [mine, x0, x1, x2, x3, mod, head_gains, wt_s, wo_s],
        [pltpu.VMEM((WIDE, 8), F32), pltpu.VMEM((WIDE, ROWS), BF16),
         pltpu.VMEM((ROWS, WIDE), BF16), pltpu.VMEM((8, WIDE), F32), square],
        smem=1,
    )
    m3, parts[2], parts[3] = lax.optimization_barrier((swap(p3, 1), parts[2], parts[3]))
    m1 = swap(p1, 1)
    chip = (p2.astype(F32) + m3.astype(F32)).astype(BF16)
    far = swap(chip, 2)
    cot0, wn, uw = call(
        gather_rows, [row, out((WIDE, 3 * PART)), out((8, 3 * PART), F32)],
        [mine, *parts, wt_s, mod],
        [pltpu.VMEM((WIDE, OWN), F32), pltpu.VMEM((8, WIDE), F32)], smem=1, behind=[chip],
    )

    chunks = [lax.select_n(at ^ d, wt_t[0], wt_t[1], wt_t[2], wo_t) for d in (0, 2)]
    chunks, far = lax.optimization_barrier((chunks, far))
    near = swap(from_neighbour(chunks[0], 3), 1)
    others = [near, round_x(near, 1), from_neighbour(chunks[1], 2), round_x(near, 3)]

    branch = p0.astype(F32) + m1.astype(F32) + far.astype(F32)
    middle = (xrow.astype(F32) + modulation[0, 2][None] * branch).astype(BF16)

    tc0 = across_seq(middle, cot0)
    tc1 = swap(tc0, 1)
    gn, br, normed, gated = call(
        temporal_own, [out((2 * OWN, WIDE))] * 4,
        [tc0, tc1, mod, head_gains, wt_t, wo_t],
        [square],
    )
    gn0, gn1, op0, op1 = call(
        temporal_far,
        [out((OWN, WIDE), F32), row, out((OWN, WIDE), F32), row],
        [at.reshape(1), normed, gated, gn, br, head_gains, *others],
        [pltpu.VMEM((4 * PART, WIDE), BF16), square],
        smem=1,
    )
    gn1, op1 = swap(gn1, 1), swap(op1, 1)
    grad_middle, mixed_rows = call(
        temporal_finish, [row] * 2, [tc0, gn0, gn1, op0, op1, mod]
    )

    moved = across_seq(grad_middle, mixed_rows)
    g0 = moved[:, :WIDE]
    g2 = swap(g0, 2)
    g1 = swap(g0, 1)
    gq, gk, gv = call(
        spatial_backward_own,
        [out((PART, 2 * OWN)), out((PART, ROWS), F32), out((PART, ROWS), F32)],
        [mine, g0, g1, query, key, value, mod, wo_s],
        [pltpu.VMEM((2 * OWN, WIDE), BF16)],
        smem=1,
    )
    parts = call(split_rows, pieces, [mine, moved], [pltpu.VMEM((WIDE, OWN), F32)], smem=1)
    g2, gq, *parts = lax.optimization_barrier((g2, gq, *parts))
    g3 = swap(g2, 1)
    parts = exchange(parts)
    p2, p3, stacked, sums = call(
        spatial_backward_far,
        [col, col, out((3 * PART, ROWS)), out((8, ROWS), F32)],
        [mine, g2, g3, query, key, value, stats, gq, gk, gv, mod, head_gains, uw, wo_s,
         wn],
        [pltpu.VMEM((2 * OWN, WIDE), BF16), pltpu.VMEM((PART, ROWS), BF16), square],
        smem=1,
    )
    m3, other, parts[2], parts[3] = lax.optimization_barrier(
        (swap(p3, 1), swap(sums, 1), parts[2], parts[3])
    )
    chip = (p2.astype(F32) + m3.astype(F32)).astype(BF16)
    far = swap(chip, 2)
    sums = sums + other
    more = swap(sums, 2)
    p0, p1a, p1b, gown = call(
        spatial_backward_last,
        [col, out((PART // 2, ROWS)), out((PART // 2, ROWS)), col],
        [mine, stacked, g0, g1, g2, g3, wn],
        [pltpu.VMEM((WIDE, OWN), F32)],
        smem=1,
        behind=[chip],
    )
    m1a, m1b = swap(p1a, 1), swap(p1b, 1)

    (mixed,) = call(place_columns, [col], [mine, *parts], smem=1, behind=[p0])

    (grad,) = call(
        spatial_finish, [col], [mine, p0, m1a, m1b, far, sums, more, stats, x0, gown, mod],
        [pltpu.VMEM((8, WIDE), F32), pltpu.VMEM((WIDE, 8), F32)],
        smem=1,
    )
    return (mixed.T, grad.T)


def solution(mesh):
    in_specs = (
        P("seq", "head"),
        P("seq", "head"),
        P(None, None, None, "head"),
        P(None, "head", None),
        P(),
        P(),
    )
    out_specs = (P("seq", "head"), P("seq", "head"))
    return jax.shard_map(
        on_device, mesh=mesh, in_specs=in_specs, out_specs=out_specs, check_vma=False
    )
```

```python
import jax
import jax.numpy as jnp
from jax import lax
from jax.experimental import pallas as pl
from jax.experimental.pallas import tpu as pltpu
from jax.sharding import PartitionSpec as P

EPS = 1e-06
HEAD = 72
PER = 4
WIDE = 1152
PART = 288
ROWS = 512
OWN = 128
LOG2E = 1.4426950408889634
SCALE = HEAD**-0.5
F32 = jnp.float32
BF16 = jnp.bfloat16
VMEM_LIMIT = 24 * 1024 * 1024


def dot(a, b, over):
    return lax.dot_general(a, b, (((over[0],), (over[1],)), ((), ())), preferred_element_type=F32)


def call(body, outs, operands, scratch=(), smem=0, behind=()):
    n, skip = len(operands), len(behind)
    specs = [
        pl.BlockSpec(memory_space=pltpu.SMEM if i < smem else pltpu.VMEM) for i in range(n)
    ] + [pl.BlockSpec(memory_space=pl.ANY)] * skip

    def run(*refs):
        body(*refs[:n], *refs[n + skip :])

    return pl.pallas_call(
        run,
        out_shape=list(outs),
        in_specs=specs,
        out_specs=[pl.BlockSpec(memory_space=pltpu.VMEM)] * len(outs),
        scratch_shapes=list(scratch),
        compiler_params=pltpu.CompilerParams(vmem_limit_bytes=VMEM_LIMIT),
        cost_estimate=pl.CostEstimate(flops=1, bytes_accessed=1, transcendentals=0),
    )(*operands, *behind)


def out(shape, dtype=BF16):
    return jax.ShapeDtypeStruct(shape, dtype)


def head_norm_t(part, gains):
    n = part.shape[1]
    cube = part.reshape(PER, HEAD, n)
    inverse = lax.rsqrt(jnp.sum(cube * cube, axis=1, keepdims=True) * (1.0 / HEAD) + EPS)
    return (cube * inverse * gains.reshape(PER, HEAD, 1)).reshape(PART, n).astype(BF16), inverse


def head_back_t(incoming, normed, inverse, gains):
    n = incoming.shape[1]
    grad = incoming.astype(F32).reshape(PER, HEAD, n)
    norm = normed.astype(F32).reshape(PER, HEAD, n)
    gain = gains.reshape(PER, HEAD, 1)
    inner = jnp.sum(norm * grad, axis=1, keepdims=True) * (1.0 / HEAD)
    return (inverse * (gain * grad - norm * (1.0 / gain) * inner)).reshape(PART, n).astype(BF16)


def turned_lines(mod, lines):
    lines[...] = jnp.zeros_like(lines)
    for i in range(3):
        lines[i : i + 1, :] = mod[i, 0:1, :]
    lines[3:4, :] = 1.0 + mod[1, 0:1, :]
    return lines[...].T


def gain_columns(gains, block, square):
    square[...] = jnp.zeros_like(square)
    square[0:2, 0:HEAD] = gains[block]
    turned = square[...].T
    return [jnp.concatenate([turned[:HEAD, i : i + 1]] * PER, axis=0) for i in range(2)]


def one_ahead(start, depth=2):
    heads = [slice(h * HEAD, (h + 1) * HEAD) for h in range(PER)]
    ahead = [start(rows) for rows in heads[:depth]]
    for h, rows in enumerate(heads):
        if h + depth < PER:
            ahead.append(start(heads[h + depth]))
        yield rows, ahead.pop(0)


def softmax_pieces(query, key, value):
    pieces = []
    for rows, scores in one_ahead(lambda rows: dot(key[rows], query[rows], (0, 0))):
        unnormed = jnp.exp2(scores * (SCALE * LOG2E))
        total = jnp.sum(unnormed, axis=0, keepdims=True)
        pieces.append(dot(value[rows], unnormed.astype(BF16), (1, 0)) * (1.0 / total))
    return jnp.concatenate(pieces, axis=0).astype(BF16)


def half_of(me, other):
    return pl.ds(pl.multiple_of(((me // 2) ^ other) * 2 * OWN, 2 * OWN), 2 * OWN)


def core_of(me, d):
    return pl.ds(pl.multiple_of(((me ^ d) & 1) * OWN, OWN), OWN)


def part_of(me, d):
    return pl.ds(pl.multiple_of((me ^ d) * PART, 32), PART)


def own_of(me, d):
    return pl.ds(pl.multiple_of((me ^ d) * OWN, OWN), OWN)


def spatial_forward(
    me_ref, x0, x1, x2, x3, mod, gains, wt, wo, q_o, k_o, v_o, st_o, p0, p1, p2, p3, xrow,
    modc, xs, both, lines, square,
):
    me = me_ref[0]
    gain_q, gain_k = gain_columns(gains, 0, square)
    modc[...] = turned_lines(mod, lines)
    for d, x in enumerate((x0, x1, x2, x3)):
        xs[part_of(me, d), :] = x[...]
    stream = xs[...].astype(F32)
    mean = jnp.sum(stream, axis=0, keepdims=True) * (1.0 / WIDE)
    centred = stream - mean
    inverse = lax.rsqrt(jnp.sum(centred * centred, axis=0, keepdims=True) * (1.0 / WIDE) + EPS)
    normed = (centred * inverse * (1.0 + modc[:, 1:2]) + modc[:, 0:1]).astype(BF16)
    weights = wt[...].reshape(3 * PART, WIDE)
    projected = dot(weights, normed, (1, 0))
    query, inv_q = head_norm_t(projected[:PART], gain_q)
    key, inv_k = head_norm_t(projected[PART : 2 * PART], gain_k)
    q_o[...] = query
    k_o[...] = key
    v_o[...] = projected[2 * PART :].astype(BF16)
    st_o[0:4, :] = inv_q.reshape(PER, ROWS)
    st_o[4:8, :] = inv_k.reshape(PER, ROWS)
    st_o[8:9, :] = mean
    st_o[9:10, :] = inverse
    attended = softmax_pieces(query, key, v_o[...])
    branch = dot(attended, wo[...], (0, 0)).astype(BF16)
    both[...] = branch
    for d, partial in enumerate((p0, p1, p2, p3)):
        partial[...] = both[own_of(me, d), :]
    xrow[...] = xs[:, own_of(me, 0)].astype(F32).T.astype(BF16)


def temporal_group(normed, gated, gain_q, gain_k, weights, wo):
    n = normed.shape[0]
    left = lax.broadcasted_iota(jnp.int32, (n, n), 0)
    right = lax.broadcasted_iota(jnp.int32, (n, n), 1)
    mask = ((left & 1) == (right & 1)) & ((left // OWN) == (right // OWN))
    projected = dot(weights, normed, (1, 1))
    query, inv_q = head_norm_t(projected[:PART], gain_q)
    key, inv_k = head_norm_t(projected[PART : 2 * PART], gain_k)
    value = projected[2 * PART :].astype(BF16)
    grad_att = dot(wo, gated, (1, 1)).astype(BF16)
    attended, gq, gk, gv = [], [], [], []

    def start(rows):
        return dot(key[rows], query[rows], (0, 0)), dot(value[rows], grad_att[rows], (0, 0))

    for rows, (scores, grad_probs) in one_ahead(start):
        q, k, v, da = query[rows], key[rows], value[rows], grad_att[rows]
        unnormed = jnp.where(mask, jnp.exp2(scores * (SCALE * LOG2E)), 0.0)
        probs = unnormed * (1.0 / jnp.sum(unnormed, axis=0, keepdims=True))
        rounded = probs.astype(BF16)
        attended.append(dot(v, rounded, (1, 0)))
        inner = jnp.sum(grad_probs * probs, axis=0, keepdims=True)
        grad_scores = (probs * (grad_probs - inner)).astype(BF16)
        gv.append(dot(da, rounded, (1, 1)))
        gq.append(dot(k, grad_scores, (1, 0)) * SCALE)
        gk.append(dot(q, grad_scores, (1, 1)) * SCALE)
    attended = jnp.concatenate(attended, axis=0).astype(BF16)
    gq = jnp.concatenate(gq, axis=0).astype(BF16)
    gk = jnp.concatenate(gk, axis=0).astype(BF16)
    gv = jnp.concatenate(gv, axis=0).astype(BF16)
    dq = head_back_t(gq, query, inv_q, gain_q)
    dk = head_back_t(gk, key, inv_k, gain_k)
    stacked = jnp.concatenate([dq, dk, gv], axis=0)
    return dot(stacked, weights, (0, 0)), dot(attended, wo, (0, 0))


def temporal_own(tc0, tc1, mod, gains, wt, wo, gn_o, br_o, normed_o, gated_o, square):
    both = jnp.concatenate([tc0[...], tc1[...]], axis=0)
    stream, incoming = both[:, :WIDE].astype(F32), both[:, WIDE:].astype(F32)
    mean = jnp.sum(stream, axis=1, keepdims=True) * (1.0 / WIDE)
    centred = stream - mean
    inverse = lax.rsqrt(jnp.sum(centred * centred, axis=1, keepdims=True) * (1.0 / WIDE) + EPS)
    normed = (centred * inverse * (1.0 + mod[1, 1:2, :]) + mod[0, 1:2, :]).astype(BF16)
    gated = (mod[2, 1:2, :] * incoming).astype(BF16)
    normed_o[...] = normed
    gated_o[...] = gated
    term, branch = temporal_group(
        normed, gated, *gain_columns(gains, 1, square), wt[...].reshape(3 * PART, WIDE), wo[...]
    )
    gn_o[...] = term.astype(BF16)
    br_o[...] = branch.astype(BF16)


def temporal_far(
    at_ref, normed, gated, gn_r, br_r, gains, w0, w1, w2, w3, gn0, gn1, op0, op1, ws, square
):
    for d, w in enumerate((w0, w1, w2, w3)):
        ws[pl.ds(pl.multiple_of(((at_ref[0] + d) & 3) * PART, 32), PART), :] = w[...]
    term, branch = temporal_group(
        normed[...],
        gated[...],
        *gain_columns(gains, 1, square),
        ws[: 3 * PART, :],
        ws[3 * PART :, :],
    )
    term = term + gn_r[...].astype(F32)
    branch = branch + br_r[...].astype(F32)
    gn0[...] = term[:OWN]
    gn1[...] = term[OWN:].astype(BF16)
    op0[...] = branch[:OWN]
    op1[...] = branch[OWN:].astype(BF16)


def temporal_finish(tc0, gn0, gn1, op0, op1, mod, gm_o, mixed_o):
    stream = tc0[:, :WIDE].astype(F32)
    mean = jnp.sum(stream, axis=1, keepdims=True) * (1.0 / WIDE)
    shifted = stream - mean
    inverse = lax.rsqrt(jnp.sum(shifted * shifted, axis=1, keepdims=True) * (1.0 / WIDE) + EPS)
    centred = shifted * inverse
    scaled = (gn0[...] + gn1[...].astype(F32)) * (1.0 + mod[1, 1:2, :])
    first = jnp.sum(scaled, axis=1, keepdims=True) * (1.0 / WIDE)
    second = jnp.sum(scaled * centred, axis=1, keepdims=True) * (1.0 / WIDE)
    gm_o[...] = (tc0[:, WIDE:].astype(F32) + inverse * (scaled - first - centred * second)).astype(BF16)
    mixed_o[...] = (stream + mod[2, 1:2, :] * (op0[...] + op1[...].astype(F32))).astype(BF16)


def backward_half(queries, grad_att, k_r, v_r):
    gq, gk, gv = [], [], []

    def start(rows):
        return dot(k_r[rows, :], queries[rows], (0, 0)), dot(v_r[rows, :], grad_att[rows], (0, 0))

    for rows, (scores, grad_probs) in one_ahead(start):
        q, k, da = queries[rows], k_r[rows, :], grad_att[rows]
        unnormed = jnp.exp2(scores * (SCALE * LOG2E))
        probs = unnormed * (1.0 / jnp.sum(unnormed, axis=0, keepdims=True))
        rounded = probs.astype(BF16)
        inner = jnp.sum(grad_probs * probs, axis=0, keepdims=True)
        grad_scores = (probs * (grad_probs - inner)).astype(BF16)
        gv.append(dot(da, rounded, (1, 1)))
        gk.append(dot(q, grad_scores, (1, 1)))
        gq.append(dot(k, grad_scores, (1, 0)) * SCALE)
    return [jnp.concatenate(g, axis=0) for g in (gq, gk, gv)]


def gated_half(me, d, ga, gb, mod, rows):
    rows[core_of(me, d), :] = (mod[2, 0:1, :] * ga[...].astype(F32)).astype(BF16)
    rows[core_of(me, d ^ 1), :] = (mod[2, 0:1, :] * gb[...].astype(F32)).astype(BF16)
    return rows[...]


def spatial_backward_own(
    me_ref, g0, g1, q_r, k_r, v_r, mod, wo, gq_o, gk_o, gv_o, rows
):
    me = me_ref[0]
    gated = gated_half(me, 0, g0, g1, mod, rows)
    grad_att = dot(wo[...], gated, (1, 1)).astype(BF16)
    gq, gk, gv = backward_half(q_r[:, half_of(me, 0)], grad_att, k_r, v_r)
    gq_o[...] = gq.astype(BF16)
    gk_o[...] = gk
    gv_o[...] = gv


def norm_sums(part, normed, inverse, gains, uw, start):
    n = part.shape[1]
    grad = part.astype(F32)
    before = normed.astype(F32)
    if inverse is not None:
        before = (before * (1.0 / gains)).reshape(PER, HEAD, n) * (1.0 / inverse)
        before = before.reshape(PART, n)
    shift, scale = uw[start : start + PART, 0:1], uw[start : start + PART, 3:4]
    first = jnp.sum(grad * scale, axis=0, keepdims=True)
    return first, jnp.sum(grad * (before - shift), axis=0, keepdims=True)


def spatial_backward_far(
    me_ref, g2, g3, q_r, k_r, v_r, st, gq_r, gk_r, gv_r, mod, gains, uw_r, wo, wn,
    p2, p3, stacked_o, rs_o, rows, gq_s, square,
):
    me = me_ref[0]
    gated = gated_half(me, 2, g2, g3, mod, rows)
    grad_att = dot(wo[...], gated, (1, 1)).astype(BF16)
    gq, gk, gv = backward_half(q_r[:, half_of(me, 1)], grad_att, k_r, v_r)
    gain_q, gain_k = gain_columns(gains, 0, square)
    gq_s[:, half_of(me, 0)] = gq_r[...]
    gq_s[:, half_of(me, 1)] = gq.astype(BF16)
    gk = ((gk + gk_r[...]) * SCALE).astype(BF16)
    inv_q = st[0:4, :].reshape(PER, 1, ROWS)
    inv_k = st[4:8, :].reshape(PER, 1, ROWS)
    stacked_o[:PART, :] = head_back_t(gq_s[...], q_r[...], inv_q, gain_q)
    stacked_o[PART : 2 * PART, :] = head_back_t(gk, k_r[...], inv_k, gain_k)
    stacked_o[2 * PART :, :] = (gv + gv_r[...]).astype(BF16)
    stacked = stacked_o[...]
    turned = wn
    for d, partial in ((3, p3), (2, p2)):
        partial[...] = dot(turned[part_of(me, d), :], stacked, (1, 0)).astype(BF16)
    uw = uw_r[...].T
    sums = [
        norm_sums(stacked[:PART], q_r[...], inv_q, gain_q, uw, 0),
        norm_sums(stacked[PART : 2 * PART], k_r[...], inv_k, gain_k, uw, PART),
        norm_sums(stacked[2 * PART :], v_r[...], None, None, uw, 2 * PART),
    ]
    rs_o[...] = jnp.zeros_like(rs_o)
    rs_o[0:1, :] = sums[0][0] + sums[1][0] + sums[2][0]
    rs_o[1:2, :] = sums[0][1] + sums[1][1] + sums[2][1]


def spatial_backward_last(me_ref, stacked_r, g0, g1, g2, g3, wn, p0, p1a, p1b, gown, rows):
    me = me_ref[0]
    stacked = stacked_r[...]
    turned = wn
    part = dot(turned[part_of(me, 1), :], stacked, (1, 0)).astype(BF16)
    p1a[...] = part[: PART // 2]
    p1b[...] = part[PART // 2 :]
    p0[...] = dot(turned[part_of(me, 0), :], stacked, (1, 0)).astype(BF16)
    for d, g in enumerate((g0, g1, g2, g3)):
        rows[...] = g[...].astype(F32).T
        gown[:, own_of(me, d)] = rows[part_of(me, 0), :].astype(BF16)


def spatial_finish(me_ref, p0, m1a, m1b, o2, rs, more, st, x0, gown, mod, out_o, lines, modc):
    modc[...] = turned_lines(mod, lines)
    m1 = jnp.concatenate([m1a[...], m1b[...]], axis=0)
    grad = p0[...].astype(F32) + m1.astype(F32) + o2[...].astype(F32)
    inverse = st[9:10, :]
    scaled = grad * (1.0 + modc[part_of(me_ref[0], 0), 1:2])
    centred = (x0[...].astype(F32) - st[8:9, :]) * inverse
    first = (rs[0:1, :] + more[0:1, :]) * (1.0 / WIDE)
    second = (rs[1:2, :] + more[1:2, :]) * (1.0 / WIDE)
    out_o[...] = (gown[...].astype(F32) + inverse * (scaled - first - centred * second)).astype(BF16)


def split_columns(me_ref, columns, c0, c1, c23):
    me = me_ref[0]
    c0[...] = columns[:, own_of(me, 0)]
    c1[...] = columns[:, own_of(me, 1)]
    c23[:PART, :] = columns[:, own_of(me, 2)]
    c23[PART:, :] = columns[:, own_of(me, 3)]


def place_columns(me_ref, c0, c1, c2, c3, out_o):
    me = me_ref[0]
    for d, c in enumerate((c0[...], c1[...], c2[:PART, :], c3[PART:, :])):
        out_o[:, own_of(me, d)] = c


def gather_rows(me_ref, c0, c1, c2, c3, wt, mod, rows_o, wn_o, uw_o, cs, lines):
    me = me_ref[0]
    weights = wt[...].reshape(3 * PART, WIDE)
    wn_o[...] = weights.T
    uw_o[...] = dot(weights, turned_lines(mod, lines).astype(BF16), (1, 0)).T
    for d, c in enumerate((c0[...], c1[...], c2[:PART, :], c3[PART:, :])):
        cs[part_of(me, d), :] = c.astype(F32)
    rows_o[...] = cs[...].T.astype(BF16)


def split_rows(me_ref, rows, c0, c1, c23, cs):
    me = me_ref[0]
    cs[...] = rows[:, WIDE:].astype(F32).T
    c0[...] = cs[part_of(me, 0), :].astype(BF16)
    c1[...] = cs[part_of(me, 1), :].astype(BF16)
    c23[:PART, :] = cs[part_of(me, 2), :].astype(BF16)
    c23[PART:, :] = cs[part_of(me, 3), :].astype(BF16)


def swap(values, d):
    return lax.ppermute(values, "head", [(i, i ^ d) for i in range(4)])


def exchange(parts):
    mine, mate, both = parts
    far = swap(both, 2)
    return [mine, swap(mate, 1), far, swap(far, 1)]


def across_seq(one, two):
    rows = jnp.concatenate([one, two], axis=1).reshape(64, 2, 2 * WIDE)
    moved = lax.all_to_all(rows, "seq", split_axis=0, concat_axis=0, tiled=True)
    return moved.reshape(OWN, 2 * WIDE)


def from_neighbour(chunk, d):
    index = [(s, h) for s in range(64) for h in range(4)]
    near = [(s * 4 + h, (s ^ 4) * 4 + (h ^ d)) for s, h in index]
    return lax.ppermute(chunk, ("seq", "head"), near)


def round_x(chunk, d):
    return lax.ppermute(chunk, "seq", [(s // 4 * 4 + (s + d) % 4, s) for s in range(64)])


def on_device(tokens, cotangent, qkv_weight, out_weight, modulation, head_gains):
    me = lax.axis_index("head")
    mine = me.astype(jnp.int32).reshape(1)
    at = (lax.axis_index("seq") & 3).astype(jnp.int32)
    wt = jnp.transpose(qkv_weight, (0, 2, 3, 1))
    mod = jnp.transpose(modulation, (1, 0, 2))
    row = out((OWN, WIDE))
    col = out((PART, ROWS))
    piece = out((PART, OWN))
    square = pltpu.VMEM((8, 128), F32)

    x0 = tokens.T
    x2 = swap(x0, 2)
    x1 = swap(x0, 1)
    pieces = [piece, piece, out((2 * PART, OWN))]
    parts = list(call(split_columns, pieces, [mine, cotangent.T], smem=1))
    weights = [wt[0], wt[1], out_weight[0], out_weight[1]]
    x2, weights, parts[0] = lax.optimization_barrier((x2, weights, parts[0]))
    wt_s, wt_t, wo_s, wo_t = weights
    x3 = swap(x2, 1)
    parts = exchange(parts)
    query, key, value, stats, p0, p1, p2, p3, xrow = call(
        spatial_forward,
        [col] * 3 + [out((16, ROWS), F32)] + [row] * 5,
        [mine, x0, x1, x2, x3, mod, head_gains, wt_s, wo_s],
        [pltpu.VMEM((WIDE, 8), F32), pltpu.VMEM((WIDE, ROWS), BF16),
         pltpu.VMEM((ROWS, WIDE), BF16), pltpu.VMEM((8, WIDE), F32), square],
        smem=1,
    )
    m3, parts[2], parts[3] = lax.optimization_barrier((swap(p3, 1), parts[2], parts[3]))
    m1 = swap(p1, 1)
    chip = (p2.astype(F32) + m3.astype(F32)).astype(BF16)
    far = swap(chip, 2)
    cot0, wn, uw = call(
        gather_rows, [row, out((WIDE, 3 * PART)), out((8, 3 * PART), F32)],
        [mine, *parts, wt_s, mod],
        [pltpu.VMEM((WIDE, OWN), F32), pltpu.VMEM((8, WIDE), F32)], smem=1, behind=[chip],
    )

    chunks = [lax.select_n(at ^ d, wt_t[0], wt_t[1], wt_t[2], wo_t) for d in (0, 2)]
    chunks, far = lax.optimization_barrier((chunks, far))
    near = swap(from_neighbour(chunks[0], 3), 1)
    others = [near, round_x(near, 1), from_neighbour(chunks[1], 2), round_x(near, 3)]

    branch = p0.astype(F32) + m1.astype(F32) + far.astype(F32)
    middle = (xrow.astype(F32) + modulation[0, 2][None] * branch).astype(BF16)

    tc0 = across_seq(middle, cot0)
    tc1 = swap(tc0, 1)
    gn, br, normed, gated = call(
        temporal_own, [out((2 * OWN, WIDE))] * 4,
        [tc0, tc1, mod, head_gains, wt_t, wo_t],
        [square],
    )
    gn0, gn1, op0, op1 = call(
        temporal_far,
        [out((OWN, WIDE), F32), row, out((OWN, WIDE), F32), row],
        [at.reshape(1), normed, gated, gn, br, head_gains, *others],
        [pltpu.VMEM((4 * PART, WIDE), BF16), square],
        smem=1,
    )
    gn1, op1 = swap(gn1, 1), swap(op1, 1)
    grad_middle, mixed_rows = call(
        temporal_finish, [row] * 2, [tc0, gn0, gn1, op0, op1, mod]
    )

    moved = across_seq(grad_middle, mixed_rows)
    g0 = moved[:, :WIDE]
    g2 = swap(g0, 2)
    g1 = swap(g0, 1)
    gq, gk, gv = call(
        spatial_backward_own,
        [out((PART, 2 * OWN)), out((PART, ROWS), F32), out((PART, ROWS), F32)],
        [mine, g0, g1, query, key, value, mod, wo_s],
        [pltpu.VMEM((2 * OWN, WIDE), BF16)],
        smem=1,
    )
    parts = call(split_rows, pieces, [mine, moved], [pltpu.VMEM((WIDE, OWN), F32)], smem=1)
    g2, gq, *parts = lax.optimization_barrier((g2, gq, *parts))
    g3 = swap(g2, 1)
    parts = exchange(parts)
    p2, p3, stacked, sums = call(
        spatial_backward_far,
        [col, col, out((3 * PART, ROWS)), out((8, ROWS), F32)],
        [mine, g2, g3, query, key, value, stats, gq, gk, gv, mod, head_gains, uw, wo_s,
         wn],
        [pltpu.VMEM((2 * OWN, WIDE), BF16), pltpu.VMEM((PART, ROWS), BF16), square],
        smem=1,
    )
    m3, other, parts[2], parts[3] = lax.optimization_barrier(
        (swap(p3, 1), swap(sums, 1), parts[2], parts[3])
    )
    chip = (p2.astype(F32) + m3.astype(F32)).astype(BF16)
    far = swap(chip, 2)
    sums = sums + other
    more = swap(sums, 2)
    p0, p1a, p1b, gown = call(
        spatial_backward_last,
        [col, out((PART // 2, ROWS)), out((PART // 2, ROWS)), col],
        [mine, stacked, g0, g1, g2, g3, wn],
        [pltpu.VMEM((WIDE, OWN), F32)],
        smem=1,
        behind=[chip],
    )
    m1a, m1b = swap(p1a, 1), swap(p1b, 1)

    (mixed,) = call(place_columns, [col], [mine, *parts], smem=1, behind=[p0])

    (grad,) = call(
        spatial_finish, [col], [mine, p0, m1a, m1b, far, sums, more, stats, x0, gown, mod],
        [pltpu.VMEM((8, WIDE), F32), pltpu.VMEM((WIDE, 8), F32)],
        smem=1,
    )
    return (mixed.T, grad.T)


def solution(mesh):
    in_specs = (
        P("seq", "head"),
        P("seq", "head"),
        P(None, None, None, "head"),
        P(None, "head", None),
        P(),
        P(),
    )
    out_specs = (P("seq", "head"), P("seq", "head"))
    return jax.shard_map(
        on_device, mesh=mesh, in_specs=in_specs, out_specs=out_specs, check_vma=False
    )
```

```python
import jax
import jax.numpy as jnp
from jax import lax
from jax.experimental import pallas as pl
from jax.experimental.pallas import tpu as pltpu
from jax.sharding import PartitionSpec as P

EPS = 1e-06
HEAD = 72
PER = 4
WIDE = 1152
PART = 288
ROWS = 512
OWN = 128
LOG2E = 1.4426950408889634
SCALE = HEAD**-0.5
F32 = jnp.float32
BF16 = jnp.bfloat16
VMEM_MIB = 24
VMEM_WIDE_MIB = 56


def dot(a, b, over):
    return lax.dot_general(a, b, (((over[0],), (over[1],)), ((), ())), preferred_element_type=F32)


def call(body, outs, operands, scratch=(), smem=0, behind=(), wide=False):
    n, skip = len(operands), len(behind)
    specs = [
        pl.BlockSpec(memory_space=pltpu.SMEM if i < smem else pltpu.VMEM) for i in range(n)
    ] + [pl.BlockSpec(memory_space=pl.ANY)] * skip

    def run(*refs):
        body(*refs[:n], *refs[n + skip :])

    return pl.pallas_call(
        run,
        out_shape=list(outs),
        in_specs=specs,
        out_specs=[pl.BlockSpec(memory_space=pltpu.VMEM)] * len(outs),
        scratch_shapes=list(scratch),
        compiler_params=pltpu.CompilerParams(vmem_limit_bytes=(VMEM_WIDE_MIB if wide else VMEM_MIB) * 2**20),
        cost_estimate=pl.CostEstimate(flops=1, bytes_accessed=1, transcendentals=0),
    )(*operands, *behind)


def out(shape, dtype=BF16):
    return jax.ShapeDtypeStruct(shape, dtype)


def head_norm_t(part, gains):
    n = part.shape[1]
    cube = part.reshape(PER, HEAD, n)
    inverse = lax.rsqrt(jnp.sum(cube * cube, axis=1, keepdims=True) * (1.0 / HEAD) + EPS)
    return (cube * inverse * gains.reshape(PER, HEAD, 1)).reshape(PART, n).astype(BF16), inverse


def head_back_t(incoming, normed, inverse, gains):
    n = incoming.shape[1]
    grad = incoming.astype(F32).reshape(PER, HEAD, n)
    norm = normed.astype(F32).reshape(PER, HEAD, n)
    gain = gains.reshape(PER, HEAD, 1)
    inner = jnp.sum(norm * grad, axis=1, keepdims=True) * (1.0 / HEAD)
    return (inverse * (gain * grad - norm * (1.0 / gain) * inner)).reshape(PART, n).astype(BF16)


def turned_lines(mod, lines):
    lines[...] = jnp.zeros_like(lines)
    for i in range(3):
        lines[i : i + 1, :] = mod[i, 0:1, :]
    lines[3:4, :] = 1.0 + mod[1, 0:1, :]
    return lines[...].T


def gain_columns(gains, block, square):
    square[...] = jnp.zeros_like(square)
    square[0:2, 0:HEAD] = gains[block]
    turned = square[...].T
    return [jnp.concatenate([turned[:HEAD, i : i + 1]] * PER, axis=0) for i in range(2)]


def one_ahead(start, depth=2):
    heads = [slice(h * HEAD, (h + 1) * HEAD) for h in range(PER)]
    ahead = [start(rows) for rows in heads[:depth]]
    for h, rows in enumerate(heads):
        if h + depth < PER:
            ahead.append(start(heads[h + depth]))
        yield rows, ahead.pop(0)


def softmax_pieces(query, key, value):
    pieces = []
    for rows, scores in one_ahead(lambda rows: dot(key[rows], query[rows], (0, 0))):
        unnormed = jnp.exp2(scores * (SCALE * LOG2E))
        total = jnp.sum(unnormed, axis=0, keepdims=True)
        pieces.append(dot(value[rows], unnormed.astype(BF16), (1, 0)) * (1.0 / total))
    return jnp.concatenate(pieces, axis=0).astype(BF16)


def half_of(me, other):
    return pl.ds(pl.multiple_of(((me // 2) ^ other) * 2 * OWN, 2 * OWN), 2 * OWN)


def core_of(me, d):
    return pl.ds(pl.multiple_of(((me ^ d) & 1) * OWN, OWN), OWN)


def part_of(me, d):
    return pl.ds(pl.multiple_of((me ^ d) * PART, 32), PART)


def own_of(me, d):
    return pl.ds(pl.multiple_of((me ^ d) * OWN, OWN), OWN)


def spatial_forward(
    me_ref, x0, x1, x2, x3, mod, gains, wt, wo, q_o, k_o, v_o, st_o, p0, p1, p2, p3, xrow,
    modc, xs, both, lines, square,
):
    me = me_ref[0]
    gain_q, gain_k = gain_columns(gains, 0, square)
    modc[...] = turned_lines(mod, lines)
    for d, x in enumerate((x0, x1, x2, x3)):
        xs[part_of(me, d), :] = x[...]
    stream = xs[...].astype(F32)
    mean = jnp.sum(stream, axis=0, keepdims=True) * (1.0 / WIDE)
    centred = stream - mean
    inverse = lax.rsqrt(jnp.sum(centred * centred, axis=0, keepdims=True) * (1.0 / WIDE) + EPS)
    normed = (centred * inverse * (1.0 + modc[:, 1:2]) + modc[:, 0:1]).astype(BF16)
    weights = wt[...].reshape(3 * PART, WIDE)
    projected = dot(weights, normed, (1, 0))
    query, inv_q = head_norm_t(projected[:PART], gain_q)
    key, inv_k = head_norm_t(projected[PART : 2 * PART], gain_k)
    q_o[...] = query
    k_o[...] = key
    v_o[...] = projected[2 * PART :].astype(BF16)
    st_o[0:4, :] = inv_q.reshape(PER, ROWS)
    st_o[4:8, :] = inv_k.reshape(PER, ROWS)
    st_o[8:9, :] = mean
    st_o[9:10, :] = inverse
    attended = softmax_pieces(query, key, v_o[...])
    branch = dot(attended, wo[...], (0, 0)).astype(BF16)
    both[...] = branch
    for d, partial in enumerate((p0, p1, p2, p3)):
        partial[...] = both[own_of(me, d), :]
    xrow[...] = xs[:, own_of(me, 0)].astype(F32).T.astype(BF16)


def temporal_group(normed, gated, gain_q, gain_k, weights, wo):
    n = normed.shape[0]
    left = lax.broadcasted_iota(jnp.int32, (n, n), 0)
    right = lax.broadcasted_iota(jnp.int32, (n, n), 1)
    mask = ((left & 1) == (right & 1)) & ((left // OWN) == (right // OWN))
    projected = dot(weights, normed, (1, 1))
    query, inv_q = head_norm_t(projected[:PART], gain_q)
    key, inv_k = head_norm_t(projected[PART : 2 * PART], gain_k)
    value = projected[2 * PART :].astype(BF16)
    grad_att = dot(wo, gated, (1, 1)).astype(BF16)
    attended, gq, gk, gv = [], [], [], []

    def start(rows):
        return dot(key[rows], query[rows], (0, 0)), dot(value[rows], grad_att[rows], (0, 0))

    for rows, (scores, grad_probs) in one_ahead(start):
        q, k, v, da = query[rows], key[rows], value[rows], grad_att[rows]
        unnormed = jnp.where(mask, jnp.exp2(scores * (SCALE * LOG2E)), 0.0)
        probs = unnormed * (1.0 / jnp.sum(unnormed, axis=0, keepdims=True))
        rounded = probs.astype(BF16)
        attended.append(dot(v, rounded, (1, 0)))
        inner = jnp.sum(grad_probs * probs, axis=0, keepdims=True)
        grad_scores = (probs * (grad_probs - inner)).astype(BF16)
        gv.append(dot(da, rounded, (1, 1)))
        gq.append(dot(k, grad_scores, (1, 0)) * SCALE)
        gk.append(dot(q, grad_scores, (1, 1)) * SCALE)
    attended = jnp.concatenate(attended, axis=0).astype(BF16)
    gq = jnp.concatenate(gq, axis=0).astype(BF16)
    gk = jnp.concatenate(gk, axis=0).astype(BF16)
    gv = jnp.concatenate(gv, axis=0).astype(BF16)
    dq = head_back_t(gq, query, inv_q, gain_q)
    dk = head_back_t(gk, key, inv_k, gain_k)
    stacked = jnp.concatenate([dq, dk, gv], axis=0)
    return dot(stacked, weights, (0, 0)), dot(attended, wo, (0, 0))


def temporal_own(tc0, tc1, mod, gains, wt, wo, gn_o, br_o, normed_o, gated_o, square):
    both = jnp.concatenate([tc0[...], tc1[...]], axis=0)
    stream, incoming = both[:, :WIDE].astype(F32), both[:, WIDE:].astype(F32)
    mean = jnp.sum(stream, axis=1, keepdims=True) * (1.0 / WIDE)
    centred = stream - mean
    inverse = lax.rsqrt(jnp.sum(centred * centred, axis=1, keepdims=True) * (1.0 / WIDE) + EPS)
    normed = (centred * inverse * (1.0 + mod[1, 1:2, :]) + mod[0, 1:2, :]).astype(BF16)
    gated = (mod[2, 1:2, :] * incoming).astype(BF16)
    normed_o[...] = normed
    gated_o[...] = gated
    term, branch = temporal_group(
        normed, gated, *gain_columns(gains, 1, square), wt[...].reshape(3 * PART, WIDE), wo[...]
    )
    gn_o[...] = term.astype(BF16)
    br_o[...] = branch.astype(BF16)


def temporal_far(
    at_ref, normed, gated, gn_r, br_r, gains, w0, w1, w2, w3, gn0, gn1, op0, op1, ws, square
):
    for d, w in enumerate((w0, w1, w2, w3)):
        ws[pl.ds(pl.multiple_of(((at_ref[0] + d) & 3) * PART, 32), PART), :] = w[...]
    term, branch = temporal_group(
        normed[...],
        gated[...],
        *gain_columns(gains, 1, square),
        ws[: 3 * PART, :],
        ws[3 * PART :, :],
    )
    term = term + gn_r[...].astype(F32)
    branch = branch + br_r[...].astype(F32)
    gn0[...] = term[:OWN]
    gn1[...] = term[OWN:].astype(BF16)
    op0[...] = branch[:OWN]
    op1[...] = branch[OWN:].astype(BF16)


def temporal_finish(tc0, gn0, gn1, op0, op1, mod, gm_o, mixed_o):
    stream = tc0[:, :WIDE].astype(F32)
    mean = jnp.sum(stream, axis=1, keepdims=True) * (1.0 / WIDE)
    shifted = stream - mean
    inverse = lax.rsqrt(jnp.sum(shifted * shifted, axis=1, keepdims=True) * (1.0 / WIDE) + EPS)
    centred = shifted * inverse
    scaled = (gn0[...] + gn1[...].astype(F32)) * (1.0 + mod[1, 1:2, :])
    first = jnp.sum(scaled, axis=1, keepdims=True) * (1.0 / WIDE)
    second = jnp.sum(scaled * centred, axis=1, keepdims=True) * (1.0 / WIDE)
    gm_o[...] = (tc0[:, WIDE:].astype(F32) + inverse * (scaled - first - centred * second)).astype(BF16)
    mixed_o[...] = (stream + mod[2, 1:2, :] * (op0[...] + op1[...].astype(F32))).astype(BF16)


def backward_half(queries, grad_att, k_r, v_r):
    gq, gk, gv = [], [], []

    def start(rows):
        return dot(k_r[rows, :], queries[rows], (0, 0)), dot(v_r[rows, :], grad_att[rows], (0, 0))

    for rows, (scores, grad_probs) in one_ahead(start):
        q, k, da = queries[rows], k_r[rows, :], grad_att[rows]
        unnormed = jnp.exp2(scores * (SCALE * LOG2E))
        probs = unnormed * (1.0 / jnp.sum(unnormed, axis=0, keepdims=True))
        rounded = probs.astype(BF16)
        inner = jnp.sum(grad_probs * probs, axis=0, keepdims=True)
        grad_scores = (probs * (grad_probs - inner)).astype(BF16)
        gv.append(dot(da, rounded, (1, 1)))
        gk.append(dot(q, grad_scores, (1, 1)))
        gq.append(dot(k, grad_scores, (1, 0)) * SCALE)
    return [jnp.concatenate(g, axis=0) for g in (gq, gk, gv)]


def gated_half(me, d, ga, gb, mod, rows):
    rows[core_of(me, d), :] = (mod[2, 0:1, :] * ga[...].astype(F32)).astype(BF16)
    rows[core_of(me, d ^ 1), :] = (mod[2, 0:1, :] * gb[...].astype(F32)).astype(BF16)
    return rows[...]


def spatial_backward_own(
    me_ref, g0, g1, q_r, k_r, v_r, mod, wo, gq_o, gk_o, gv_o, rows
):
    me = me_ref[0]
    gated = gated_half(me, 0, g0, g1, mod, rows)
    grad_att = dot(wo[...], gated, (1, 1)).astype(BF16)
    gq, gk, gv = backward_half(q_r[:, half_of(me, 0)], grad_att, k_r, v_r)
    gq_o[...] = gq.astype(BF16)
    gk_o[...] = gk
    gv_o[...] = gv


def norm_sums(part, normed, inverse, gains, uw, start):
    n = part.shape[1]
    grad = part.astype(F32)
    before = normed.astype(F32)
    if inverse is not None:
        before = (before * (1.0 / gains)).reshape(PER, HEAD, n) * (1.0 / inverse)
        before = before.reshape(PART, n)
    shift, scale = uw[start : start + PART, 0:1], uw[start : start + PART, 3:4]
    first = jnp.sum(grad * scale, axis=0, keepdims=True)
    return first, jnp.sum(grad * (before - shift), axis=0, keepdims=True)


def spatial_backward_far(
    me_ref, g2, g3, q_r, k_r, v_r, st, gq_r, gk_r, gv_r, mod, gains, uw_r, wo, wn,
    p2, p3, stacked_o, rs_o, rows, gq_s, square,
):
    me = me_ref[0]
    gated = gated_half(me, 2, g2, g3, mod, rows)
    grad_att = dot(wo[...], gated, (1, 1)).astype(BF16)
    gq, gk, gv = backward_half(q_r[:, half_of(me, 1)], grad_att, k_r, v_r)
    gain_q, gain_k = gain_columns(gains, 0, square)
    gq_s[:, half_of(me, 0)] = gq_r[...]
    gq_s[:, half_of(me, 1)] = gq.astype(BF16)
    gk = ((gk + gk_r[...]) * SCALE).astype(BF16)
    inv_q = st[0:4, :].reshape(PER, 1, ROWS)
    inv_k = st[4:8, :].reshape(PER, 1, ROWS)
    stacked_o[:PART, :] = head_back_t(gq_s[...], q_r[...], inv_q, gain_q)
    stacked_o[PART : 2 * PART, :] = head_back_t(gk, k_r[...], inv_k, gain_k)
    stacked_o[2 * PART :, :] = (gv + gv_r[...]).astype(BF16)
    stacked = stacked_o[...]
    turned = wn
    for d, partial in ((3, p3), (2, p2)):
        partial[...] = dot(turned[part_of(me, d), :], stacked, (1, 0)).astype(BF16)
    uw = uw_r[...].T
    sums = [
        norm_sums(stacked[:PART], q_r[...], inv_q, gain_q, uw, 0),
        norm_sums(stacked[PART : 2 * PART], k_r[...], inv_k, gain_k, uw, PART),
        norm_sums(stacked[2 * PART :], v_r[...], None, None, uw, 2 * PART),
    ]
    rs_o[...] = jnp.zeros_like(rs_o)
    rs_o[0:1, :] = sums[0][0] + sums[1][0] + sums[2][0]
    rs_o[1:2, :] = sums[0][1] + sums[1][1] + sums[2][1]


def spatial_backward_last(me_ref, stacked_r, g0, g1, g2, g3, wn, p0, p1a, p1b, gown, rows):
    me = me_ref[0]
    stacked = stacked_r[...]
    turned = wn
    part = dot(turned[part_of(me, 1), :], stacked, (1, 0)).astype(BF16)
    p1a[...] = part[: PART // 2]
    p1b[...] = part[PART // 2 :]
    p0[...] = dot(turned[part_of(me, 0), :], stacked, (1, 0)).astype(BF16)
    for d, g in enumerate((g0, g1, g2, g3)):
        rows[...] = g[...].astype(F32).T
        gown[:, own_of(me, d)] = rows[part_of(me, 0), :].astype(BF16)


def spatial_finish(me_ref, p0, m1a, m1b, o2, rs, more, st, x0, gown, mod, out_o, lines, modc):
    modc[...] = turned_lines(mod, lines)
    m1 = jnp.concatenate([m1a[...], m1b[...]], axis=0)
    grad = p0[...].astype(F32) + m1.astype(F32) + o2[...].astype(F32)
    inverse = st[9:10, :]
    scaled = grad * (1.0 + modc[part_of(me_ref[0], 0), 1:2])
    centred = (x0[...].astype(F32) - st[8:9, :]) * inverse
    first = (rs[0:1, :] + more[0:1, :]) * (1.0 / WIDE)
    second = (rs[1:2, :] + more[1:2, :]) * (1.0 / WIDE)
    out_o[...] = (gown[...].astype(F32) + inverse * (scaled - first - centred * second)).astype(BF16)


def split_columns(me_ref, columns, c0, c1, c23):
    me = me_ref[0]
    c0[...] = columns[:, own_of(me, 0)]
    c1[...] = columns[:, own_of(me, 1)]
    c23[:PART, :] = columns[:, own_of(me, 2)]
    c23[PART:, :] = columns[:, own_of(me, 3)]


def place_columns(me_ref, c0, c1, c2, c3, out_o):
    me = me_ref[0]
    for d, c in enumerate((c0[...], c1[...], c2[:PART, :], c3[PART:, :])):
        out_o[:, own_of(me, d)] = c


def gather_rows(me_ref, c0, c1, c2, c3, wt, mod, rows_o, wn_o, uw_o, cs, lines):
    me = me_ref[0]
    weights = wt[...].reshape(3 * PART, WIDE)
    wn_o[...] = weights.T
    uw_o[...] = dot(weights, turned_lines(mod, lines).astype(BF16), (1, 0)).T
    for d, c in enumerate((c0[...], c1[...], c2[:PART, :], c3[PART:, :])):
        cs[part_of(me, d), :] = c.astype(F32)
    rows_o[...] = cs[...].T.astype(BF16)


def split_rows(me_ref, rows, c0, c1, c23, cs):
    me = me_ref[0]
    cs[...] = rows[:, WIDE:].astype(F32).T
    c0[...] = cs[part_of(me, 0), :].astype(BF16)
    c1[...] = cs[part_of(me, 1), :].astype(BF16)
    c23[:PART, :] = cs[part_of(me, 2), :].astype(BF16)
    c23[PART:, :] = cs[part_of(me, 3), :].astype(BF16)


def swap(values, d):
    return lax.ppermute(values, "head", [(i, i ^ d) for i in range(4)])


def exchange(parts):
    mine, mate, both = parts
    far = swap(both, 2)
    return [mine, swap(mate, 1), far, swap(far, 1)]


def across_seq(one, two):
    rows = jnp.concatenate([one, two], axis=1).reshape(64, 2, 2 * WIDE)
    moved = lax.all_to_all(rows, "seq", split_axis=0, concat_axis=0, tiled=True)
    return moved.reshape(OWN, 2 * WIDE)


def from_neighbour(chunk, d):
    index = [(s, h) for s in range(64) for h in range(4)]
    near = [(s * 4 + h, (s ^ 4) * 4 + (h ^ d)) for s, h in index]
    return lax.ppermute(chunk, ("seq", "head"), near)


def round_x(chunk, d):
    return lax.ppermute(chunk, "seq", [(s // 4 * 4 + (s + d) % 4, s) for s in range(64)])


def on_device(tokens, cotangent, qkv_weight, out_weight, modulation, head_gains):
    me = lax.axis_index("head")
    mine = me.astype(jnp.int32).reshape(1)
    at = (lax.axis_index("seq") & 3).astype(jnp.int32)
    wt = jnp.transpose(qkv_weight, (0, 2, 3, 1))
    mod = jnp.transpose(modulation, (1, 0, 2))
    row = out((OWN, WIDE))
    col = out((PART, ROWS))
    piece = out((PART, OWN))
    square = pltpu.VMEM((8, 128), F32)

    x0 = tokens.T
    x2 = swap(x0, 2)
    x1 = swap(x0, 1)
    pieces = [piece, piece, out((2 * PART, OWN))]
    parts = list(call(split_columns, pieces, [mine, cotangent.T], smem=1))
    weights = [wt[0], wt[1], out_weight[0], out_weight[1]]
    x2, weights, parts[0] = lax.optimization_barrier((x2, weights, parts[0]))
    wt_s, wt_t, wo_s, wo_t = weights
    x3 = swap(x2, 1)
    parts = exchange(parts)
    query, key, value, stats, p0, p1, p2, p3, xrow = call(
        spatial_forward,
        [col] * 3 + [out((16, ROWS), F32)] + [row] * 5,
        [mine, x0, x1, x2, x3, mod, head_gains, wt_s, wo_s],
        [pltpu.VMEM((WIDE, 8), F32), pltpu.VMEM((WIDE, ROWS), BF16),
         pltpu.VMEM((ROWS, WIDE), BF16), pltpu.VMEM((8, WIDE), F32), square],
        smem=1, wide=True,
    )
    m3, parts[2], parts[3] = lax.optimization_barrier((swap(p3, 1), parts[2], parts[3]))
    m1 = swap(p1, 1)
    chip = (p2.astype(F32) + m3.astype(F32)).astype(BF16)
    far = swap(chip, 2)
    cot0, wn, uw = call(
        gather_rows, [row, out((WIDE, 3 * PART)), out((8, 3 * PART), F32)],
        [mine, *parts, wt_s, mod],
        [pltpu.VMEM((WIDE, OWN), F32), pltpu.VMEM((8, WIDE), F32)], smem=1, wide=True, behind=[chip],
    )

    chunks = [lax.select_n(at ^ d, wt_t[0], wt_t[1], wt_t[2], wo_t) for d in (0, 2)]
    chunks, far = lax.optimization_barrier((chunks, far))
    near = swap(from_neighbour(chunks[0], 3), 1)
    others = [near, round_x(near, 1), from_neighbour(chunks[1], 2), round_x(near, 3)]

    branch = p0.astype(F32) + m1.astype(F32) + far.astype(F32)
    middle = (xrow.astype(F32) + modulation[0, 2][None] * branch).astype(BF16)

    tc0 = across_seq(middle, cot0)
    tc1 = swap(tc0, 1)
    gn, br, normed, gated = call(
        temporal_own, [out((2 * OWN, WIDE))] * 4,
        [tc0, tc1, mod, head_gains, wt_t, wo_t],
        [square],
    )
    gn0, gn1, op0, op1 = call(
        temporal_far,
        [out((OWN, WIDE), F32), row, out((OWN, WIDE), F32), row],
        [at.reshape(1), normed, gated, gn, br, head_gains, *others],
        [pltpu.VMEM((4 * PART, WIDE), BF16), square],
        smem=1,
    )
    gn1, op1 = swap(gn1, 1), swap(op1, 1)
    grad_middle, mixed_rows = call(
        temporal_finish, [row] * 2, [tc0, gn0, gn1, op0, op1, mod]
    )

    moved = across_seq(grad_middle, mixed_rows)
    g0 = moved[:, :WIDE]
    g2 = swap(g0, 2)
    g1 = swap(g0, 1)
    gq, gk, gv = call(
        spatial_backward_own,
        [out((PART, 2 * OWN)), out((PART, ROWS), F32), out((PART, ROWS), F32)],
        [mine, g0, g1, query, key, value, mod, wo_s],
        [pltpu.VMEM((2 * OWN, WIDE), BF16)],
        smem=1,
    )
    parts = call(split_rows, pieces, [mine, moved], [pltpu.VMEM((WIDE, OWN), F32)], smem=1)
    g2, gq, *parts = lax.optimization_barrier((g2, gq, *parts))
    g3 = swap(g2, 1)
    parts = exchange(parts)
    p2, p3, stacked, sums = call(
        spatial_backward_far,
        [col, col, out((3 * PART, ROWS)), out((8, ROWS), F32)],
        [mine, g2, g3, query, key, value, stats, gq, gk, gv, mod, head_gains, uw, wo_s,
         wn],
        [pltpu.VMEM((2 * OWN, WIDE), BF16), pltpu.VMEM((PART, ROWS), BF16), square],
        smem=1,
    )
    m3, other, parts[2], parts[3] = lax.optimization_barrier(
        (swap(p3, 1), swap(sums, 1), parts[2], parts[3])
    )
    chip = (p2.astype(F32) + m3.astype(F32)).astype(BF16)
    far = swap(chip, 2)
    sums = sums + other
    more = swap(sums, 2)
    p0, p1a, p1b, gown = call(
        spatial_backward_last,
        [col, out((PART // 2, ROWS)), out((PART // 2, ROWS)), col],
        [mine, stacked, g0, g1, g2, g3, wn],
        [pltpu.VMEM((WIDE, OWN), F32)],
        smem=1,
        behind=[chip],
    )
    m1a, m1b = swap(p1a, 1), swap(p1b, 1)

    (mixed,) = call(place_columns, [col], [mine, *parts], smem=1, behind=[p0])

    (grad,) = call(
        spatial_finish, [col], [mine, p0, m1a, m1b, far, sums, more, stats, x0, gown, mod],
        [pltpu.VMEM((8, WIDE), F32), pltpu.VMEM((WIDE, 8), F32)],
        smem=1,
    )
    return (mixed.T, grad.T)


def solution(mesh):
    in_specs = (
        P("seq", "head"),
        P("seq", "head"),
        P(None, None, None, "head"),
        P(None, "head", None),
        P(),
        P(),
    )
    out_specs = (P("seq", "head"), P("seq", "head"))
    return jax.shard_map(
        on_device, mesh=mesh, in_specs=in_specs, out_specs=out_specs, check_vma=False
    )
```

```python
import jax
import jax.numpy as jnp
from jax import lax
from jax.experimental import pallas as pl
from jax.experimental.pallas import tpu as pltpu
from jax.sharding import PartitionSpec as P

EPS = 1e-06
HEAD = 72
PER = 4
WIDE = 1152
PART = 288
ROWS = 512
OWN = 128
LOG2E = 1.4426950408889634
SCALE = HEAD**-0.5
F32 = jnp.float32
BF16 = jnp.bfloat16
VMEM_MIB = 24
VMEM_WIDE_MIB = 56


def dot(a, b, over):
    return lax.dot_general(a, b, (((over[0],), (over[1],)), ((), ())), preferred_element_type=F32)


def call(body, outs, operands, scratch=(), smem=0, behind=(), wide=False):
    n, skip = len(operands), len(behind)
    specs = [
        pl.BlockSpec(memory_space=pltpu.SMEM if i < smem else pltpu.VMEM) for i in range(n)
    ] + [pl.BlockSpec(memory_space=pl.ANY)] * skip

    def run(*refs):
        body(*refs[:n], *refs[n + skip :])

    return pl.pallas_call(
        run,
        out_shape=list(outs),
        in_specs=specs,
        out_specs=[pl.BlockSpec(memory_space=pltpu.VMEM)] * len(outs),
        scratch_shapes=list(scratch),
        compiler_params=pltpu.CompilerParams(vmem_limit_bytes=(VMEM_WIDE_MIB if wide else VMEM_MIB) * 2**20),
        cost_estimate=pl.CostEstimate(flops=1, bytes_accessed=1, transcendentals=0),
    )(*operands, *behind)


def out(shape, dtype=BF16):
    return jax.ShapeDtypeStruct(shape, dtype)


def head_norm_t(part, gains):
    n = part.shape[1]
    cube = part.reshape(PER, HEAD, n)
    inverse = lax.rsqrt(jnp.sum(cube * cube, axis=1, keepdims=True) * (1.0 / HEAD) + EPS)
    return (cube * inverse * gains.reshape(PER, HEAD, 1)).reshape(PART, n).astype(BF16), inverse


def head_back_t(incoming, normed, inverse, gains):
    n = incoming.shape[1]
    grad = incoming.astype(F32).reshape(PER, HEAD, n)
    norm = normed.astype(F32).reshape(PER, HEAD, n)
    gain = gains.reshape(PER, HEAD, 1)
    inner = jnp.sum(norm * grad, axis=1, keepdims=True) * (1.0 / HEAD)
    return (inverse * (gain * grad - norm * (1.0 / gain) * inner)).reshape(PART, n).astype(BF16)


def turned_lines(mod, lines):
    lines[...] = jnp.zeros_like(lines)
    for i in range(3):
        lines[i : i + 1, :] = mod[i, 0:1, :]
    lines[3:4, :] = 1.0 + mod[1, 0:1, :]
    return lines[...].T


def gain_columns(gains, block, square):
    square[...] = jnp.zeros_like(square)
    square[0:2, 0:HEAD] = gains[block]
    turned = square[...].T
    return [jnp.concatenate([turned[:HEAD, i : i + 1]] * PER, axis=0) for i in range(2)]


def one_ahead(start, depth=2):
    heads = [slice(h * HEAD, (h + 1) * HEAD) for h in range(PER)]
    ahead = [start(rows) for rows in heads[:depth]]
    for h, rows in enumerate(heads):
        if h + depth < PER:
            ahead.append(start(heads[h + depth]))
        yield rows, ahead.pop(0)


def softmax_pieces(query, key, value):
    pieces = []
    for rows, scores in one_ahead(lambda rows: dot(key[rows], query[rows], (0, 0))):
        unnormed = jnp.exp2(scores * (SCALE * LOG2E))
        total = jnp.sum(unnormed, axis=0, keepdims=True)
        pieces.append(dot(value[rows], unnormed.astype(BF16), (1, 0)) * (1.0 / total))
    return jnp.concatenate(pieces, axis=0).astype(BF16)


def half_of(me, other):
    return pl.ds(pl.multiple_of(((me // 2) ^ other) * 2 * OWN, 2 * OWN), 2 * OWN)


def core_of(me, d):
    return pl.ds(pl.multiple_of(((me ^ d) & 1) * OWN, OWN), OWN)


def part_of(me, d):
    return pl.ds(pl.multiple_of((me ^ d) * PART, 32), PART)


def own_of(me, d):
    return pl.ds(pl.multiple_of((me ^ d) * OWN, OWN), OWN)


def spatial_forward(
    me_ref, x0, x1, x2, x3, mod, gains, wt, wo, q_o, k_o, v_o, st_o, p0, p1, p2, p3, xrow,
    modc, xs, both, lines, square,
):
    me = me_ref[0]
    gain_q, gain_k = gain_columns(gains, 0, square)
    modc[...] = turned_lines(mod, lines)
    for d, x in enumerate((x0, x1, x2, x3)):
        xs[part_of(me, d), :] = x[...]
    stream = xs[...].astype(F32)
    mean = jnp.sum(stream, axis=0, keepdims=True) * (1.0 / WIDE)
    centred = stream - mean
    inverse = lax.rsqrt(jnp.sum(centred * centred, axis=0, keepdims=True) * (1.0 / WIDE) + EPS)
    normed = (centred * inverse * (1.0 + modc[:, 1:2]) + modc[:, 0:1]).astype(BF16)
    weights = wt[...].reshape(3 * PART, WIDE)
    projected = dot(weights, normed, (1, 0))
    query, inv_q = head_norm_t(projected[:PART], gain_q)
    key, inv_k = head_norm_t(projected[PART : 2 * PART], gain_k)
    q_o[...] = query
    k_o[...] = key
    v_o[...] = projected[2 * PART :].astype(BF16)
    st_o[0:4, :] = inv_q.reshape(PER, ROWS)
    st_o[4:8, :] = inv_k.reshape(PER, ROWS)
    st_o[8:9, :] = mean
    st_o[9:10, :] = inverse
    attended = softmax_pieces(query, key, v_o[...])
    branch = dot(attended, wo[...], (0, 0)).astype(BF16)
    both[...] = branch
    for d, partial in enumerate((p0, p1, p2, p3)):
        partial[...] = both[own_of(me, d), :]
    xrow[...] = xs[:, own_of(me, 0)].astype(F32).T.astype(BF16)


def temporal_group(normed, gated, gain_q, gain_k, weights, wo):
    n = normed.shape[0]
    left = lax.broadcasted_iota(jnp.int32, (n, n), 0)
    right = lax.broadcasted_iota(jnp.int32, (n, n), 1)
    mask = ((left & 1) == (right & 1)) & ((left // OWN) == (right // OWN))
    projected = dot(weights, normed, (1, 1))
    query, inv_q = head_norm_t(projected[:PART], gain_q)
    key, inv_k = head_norm_t(projected[PART : 2 * PART], gain_k)
    value = projected[2 * PART :].astype(BF16)
    grad_att = dot(wo, gated, (1, 1)).astype(BF16)
    attended, gq, gk, gv = [], [], [], []

    def start(rows):
        return dot(key[rows], query[rows], (0, 0)), dot(value[rows], grad_att[rows], (0, 0))

    for rows, (scores, grad_probs) in one_ahead(start):
        q, k, v, da = query[rows], key[rows], value[rows], grad_att[rows]
        unnormed = jnp.where(mask, jnp.exp2(scores * (SCALE * LOG2E)), 0.0)
        probs = unnormed * (1.0 / jnp.sum(unnormed, axis=0, keepdims=True))
        rounded = probs.astype(BF16)
        attended.append(dot(v, rounded, (1, 0)))
        inner = jnp.sum(grad_probs * probs, axis=0, keepdims=True)
        grad_scores = (probs * (grad_probs - inner)).astype(BF16)
        gv.append(dot(da, rounded, (1, 1)))
        gq.append(dot(k, grad_scores, (1, 0)) * SCALE)
        gk.append(dot(q, grad_scores, (1, 1)) * SCALE)
    attended = jnp.concatenate(attended, axis=0).astype(BF16)
    gq = jnp.concatenate(gq, axis=0).astype(BF16)
    gk = jnp.concatenate(gk, axis=0).astype(BF16)
    gv = jnp.concatenate(gv, axis=0).astype(BF16)
    dq = head_back_t(gq, query, inv_q, gain_q)
    dk = head_back_t(gk, key, inv_k, gain_k)
    stacked = jnp.concatenate([dq, dk, gv], axis=0)
    return dot(stacked, weights, (0, 0)), dot(attended, wo, (0, 0))


def temporal_own(tc0, tc1, mod, gains, wt, wo, gn_o, br_o, normed_o, gated_o, square):
    both = jnp.concatenate([tc0[...], tc1[...]], axis=0)
    stream, incoming = both[:, :WIDE].astype(F32), both[:, WIDE:].astype(F32)
    mean = jnp.sum(stream, axis=1, keepdims=True) * (1.0 / WIDE)
    centred = stream - mean
    inverse = lax.rsqrt(jnp.sum(centred * centred, axis=1, keepdims=True) * (1.0 / WIDE) + EPS)
    normed = (centred * inverse * (1.0 + mod[1, 1:2, :]) + mod[0, 1:2, :]).astype(BF16)
    gated = (mod[2, 1:2, :] * incoming).astype(BF16)
    normed_o[...] = normed
    gated_o[...] = gated
    term, branch = temporal_group(
        normed, gated, *gain_columns(gains, 1, square), wt[...].reshape(3 * PART, WIDE), wo[...]
    )
    gn_o[...] = term.astype(BF16)
    br_o[...] = branch.astype(BF16)


def temporal_far(
    at_ref, normed, gated, gn_r, br_r, gains, w0, w1, w2, w3, gn0, gn1, op0, op1, ws, square
):
    for d, w in enumerate((w0, w1, w2, w3)):
        ws[pl.ds(pl.multiple_of(((at_ref[0] + d) & 3) * PART, 32), PART), :] = w[...]
    term, branch = temporal_group(
        normed[...],
        gated[...],
        *gain_columns(gains, 1, square),
        ws[: 3 * PART, :],
        ws[3 * PART :, :],
    )
    term = term + gn_r[...].astype(F32)
    branch = branch + br_r[...].astype(F32)
    gn0[...] = term[:OWN]
    gn1[...] = term[OWN:].astype(BF16)
    op0[...] = branch[:OWN]
    op1[...] = branch[OWN:].astype(BF16)


def temporal_finish(tc0, gn0, gn1, op0, op1, mod, gm_o, mixed_o):
    stream = tc0[:, :WIDE].astype(F32)
    mean = jnp.sum(stream, axis=1, keepdims=True) * (1.0 / WIDE)
    shifted = stream - mean
    inverse = lax.rsqrt(jnp.sum(shifted * shifted, axis=1, keepdims=True) * (1.0 / WIDE) + EPS)
    centred = shifted * inverse
    scaled = (gn0[...] + gn1[...].astype(F32)) * (1.0 + mod[1, 1:2, :])
    first = jnp.sum(scaled, axis=1, keepdims=True) * (1.0 / WIDE)
    second = jnp.sum(scaled * centred, axis=1, keepdims=True) * (1.0 / WIDE)
    gm_o[...] = (tc0[:, WIDE:].astype(F32) + inverse * (scaled - first - centred * second)).astype(BF16)
    mixed_o[...] = (stream + mod[2, 1:2, :] * (op0[...] + op1[...].astype(F32))).astype(BF16)


def backward_half(queries, grad_att, k_r, v_r):
    gq, gk, gv = [], [], []

    def start(rows):
        return dot(k_r[rows, :], queries[rows], (0, 0)), dot(v_r[rows, :], grad_att[rows], (0, 0))

    for rows, (scores, grad_probs) in one_ahead(start):
        q, k, da = queries[rows], k_r[rows, :], grad_att[rows]
        unnormed = jnp.exp2(scores * (SCALE * LOG2E))
        probs = unnormed * (1.0 / jnp.sum(unnormed, axis=0, keepdims=True))
        rounded = probs.astype(BF16)
        inner = jnp.sum(grad_probs * probs, axis=0, keepdims=True)
        grad_scores = (probs * (grad_probs - inner)).astype(BF16)
        gv.append(dot(da, rounded, (1, 1)))
        gk.append(dot(q, grad_scores, (1, 1)))
        gq.append(dot(k, grad_scores, (1, 0)) * SCALE)
    return [jnp.concatenate(g, axis=0) for g in (gq, gk, gv)]


def gated_half(me, d, ga, gb, mod, rows):
    rows[core_of(me, d), :] = (mod[2, 0:1, :] * ga[...].astype(F32)).astype(BF16)
    rows[core_of(me, d ^ 1), :] = (mod[2, 0:1, :] * gb[...].astype(F32)).astype(BF16)
    return rows[...]


def spatial_backward_own(
    me_ref, g0, g1, q_r, k_r, v_r, mod, wo, gq_o, gk_o, gv_o, rows
):
    me = me_ref[0]
    gated = gated_half(me, 0, g0, g1, mod, rows)
    grad_att = dot(wo[...], gated, (1, 1)).astype(BF16)
    gq, gk, gv = backward_half(q_r[:, half_of(me, 0)], grad_att, k_r, v_r)
    gq_o[...] = gq.astype(BF16)
    gk_o[...] = gk
    gv_o[...] = gv


def norm_sums(part, normed, inverse, gains, uw, start):
    n = part.shape[1]
    grad = part.astype(F32)
    before = normed.astype(F32)
    if inverse is not None:
        before = (before * (1.0 / gains)).reshape(PER, HEAD, n) * (1.0 / inverse)
        before = before.reshape(PART, n)
    shift, scale = uw[start : start + PART, 0:1], uw[start : start + PART, 3:4]
    first = jnp.sum(grad * scale, axis=0, keepdims=True)
    return first, jnp.sum(grad * (before - shift), axis=0, keepdims=True)


def spatial_backward_far(
    me_ref, g2, g3, q_r, k_r, v_r, st, gq_r, gk_r, gv_r, mod, gains, uw_r, wo, wn,
    p2, p3, stacked_o, rs_o, rows, gq_s, square,
):
    me = me_ref[0]
    gated = gated_half(me, 2, g2, g3, mod, rows)
    grad_att = dot(wo[...], gated, (1, 1)).astype(BF16)
    gq, gk, gv = backward_half(q_r[:, half_of(me, 1)], grad_att, k_r, v_r)
    gain_q, gain_k = gain_columns(gains, 0, square)
    gq_s[:, half_of(me, 0)] = gq_r[...]
    gq_s[:, half_of(me, 1)] = gq.astype(BF16)
    gk = ((gk + gk_r[...]) * SCALE).astype(BF16)
    inv_q = st[0:4, :].reshape(PER, 1, ROWS)
    inv_k = st[4:8, :].reshape(PER, 1, ROWS)
    stacked_o[:PART, :] = head_back_t(gq_s[...], q_r[...], inv_q, gain_q)
    stacked_o[PART : 2 * PART, :] = head_back_t(gk, k_r[...], inv_k, gain_k)
    stacked_o[2 * PART :, :] = (gv + gv_r[...]).astype(BF16)
    stacked = stacked_o[...]
    turned = wn
    for d, partial in ((3, p3), (2, p2)):
        partial[...] = dot(turned[part_of(me, d), :], stacked, (1, 0)).astype(BF16)
    uw = uw_r[...].T
    sums = [
        norm_sums(stacked[:PART], q_r[...], inv_q, gain_q, uw, 0),
        norm_sums(stacked[PART : 2 * PART], k_r[...], inv_k, gain_k, uw, PART),
        norm_sums(stacked[2 * PART :], v_r[...], None, None, uw, 2 * PART),
    ]
    rs_o[...] = jnp.zeros_like(rs_o)
    rs_o[0:1, :] = sums[0][0] + sums[1][0] + sums[2][0]
    rs_o[1:2, :] = sums[0][1] + sums[1][1] + sums[2][1]


def spatial_backward_last(me_ref, stacked_r, g0, g1, g2, g3, wn, p0, p1a, p1b, gown, rows):
    me = me_ref[0]
    stacked = stacked_r[...]
    turned = wn
    part = dot(turned[part_of(me, 1), :], stacked, (1, 0)).astype(BF16)
    p1a[...] = part[: PART // 2]
    p1b[...] = part[PART // 2 :]
    p0[...] = dot(turned[part_of(me, 0), :], stacked, (1, 0)).astype(BF16)
    for d, g in enumerate((g0, g1, g2, g3)):
        rows[...] = g[...].astype(F32).T
        gown[:, own_of(me, d)] = rows[part_of(me, 0), :].astype(BF16)


def chip_sums(p2, m3, sums, other, chip_o, sums_o):
    total = sums[...] + other[...]
    sums_o[...] = total
    chip_o[:PART, :] = (p2[...].astype(F32) + m3[...].astype(F32)).astype(BF16)
    chip_o[PART:, :] = jnp.concatenate([total, jnp.zeros_like(total)], axis=0).astype(BF16)


def middle_rows(p0, m1, far, xrow, cot, mod, rows_o):
    branch = p0[...].astype(F32) + m1[...].astype(F32) + far[...].astype(F32)
    rows_o[:, :WIDE] = (xrow[...].astype(F32) + mod[2, 0:1, :] * branch).astype(BF16)
    rows_o[:, WIDE:] = cot[...]


def spatial_finish(me_ref, p0, m1a, m1b, o2, rs, st, x0, gown, mod, out_o, lines, modc):
    modc[...] = turned_lines(mod, lines)
    m1 = jnp.concatenate([m1a[...], m1b[...]], axis=0)
    grad = p0[...].astype(F32) + m1.astype(F32) + o2[:PART, :].astype(F32)
    inverse = st[9:10, :]
    scaled = grad * (1.0 + modc[part_of(me_ref[0], 0), 1:2])
    centred = (x0[...].astype(F32) - st[8:9, :]) * inverse
    more = o2[PART:, :].astype(F32)
    first = (rs[0:1, :] + more[0:1]) * (1.0 / WIDE)
    second = (rs[1:2, :] + more[1:2]) * (1.0 / WIDE)
    out_o[...] = (gown[...].astype(F32) + inverse * (scaled - first - centred * second)).astype(BF16)


def split_columns(me_ref, columns, c0, c1, c23):
    me = me_ref[0]
    c0[...] = columns[:, own_of(me, 0)]
    c1[...] = columns[:, own_of(me, 1)]
    c23[:PART, :] = columns[:, own_of(me, 2)]
    c23[PART:, :] = columns[:, own_of(me, 3)]


def place_columns(me_ref, c0, c1, c2, c3, out_o):
    me = me_ref[0]
    for d, c in enumerate((c0[...], c1[...], c2[:PART, :], c3[PART:, :])):
        out_o[:, own_of(me, d)] = c


def gather_rows(me_ref, c0, c1, c2, c3, wt, mod, rows_o, wn_o, uw_o, cs, lines):
    me = me_ref[0]
    weights = wt[...].reshape(3 * PART, WIDE)
    wn_o[...] = weights.T
    uw_o[...] = dot(weights, turned_lines(mod, lines).astype(BF16), (1, 0)).T
    for d, c in enumerate((c0[...], c1[...], c2[:PART, :], c3[PART:, :])):
        cs[part_of(me, d), :] = c.astype(F32)
    rows_o[...] = cs[...].T.astype(BF16)


def split_rows(me_ref, rows, c0, c1, c23, cs):
    me = me_ref[0]
    cs[...] = rows[:, WIDE:].astype(F32).T
    c0[...] = cs[part_of(me, 0), :].astype(BF16)
    c1[...] = cs[part_of(me, 1), :].astype(BF16)
    c23[:PART, :] = cs[part_of(me, 2), :].astype(BF16)
    c23[PART:, :] = cs[part_of(me, 3), :].astype(BF16)


def swap(values, d):
    return lax.ppermute(values, "head", [(i, i ^ d) for i in range(4)])


def exchange(parts):
    mine, mate, both = parts
    far = swap(both, 2)
    return [mine, swap(mate, 1), far, swap(far, 1)]


def across_seq(rows):
    rows = rows.reshape(64, 2, 2 * WIDE)
    moved = lax.all_to_all(rows, "seq", split_axis=0, concat_axis=0, tiled=True)
    return moved.reshape(OWN, 2 * WIDE)


def from_neighbour(chunk, d):
    index = [(s, h) for s in range(64) for h in range(4)]
    near = [(s * 4 + h, (s ^ 4) * 4 + (h ^ d)) for s, h in index]
    return lax.ppermute(chunk, ("seq", "head"), near)


def round_x(chunk, d):
    return lax.ppermute(chunk, "seq", [(s // 4 * 4 + (s + d) % 4, s) for s in range(64)])


def on_device(tokens, cotangent, qkv_weight, out_weight, modulation, head_gains):
    me = lax.axis_index("head")
    mine = me.astype(jnp.int32).reshape(1)
    at = (lax.axis_index("seq") & 3).astype(jnp.int32)
    wt = jnp.transpose(qkv_weight, (0, 2, 3, 1))
    mod = jnp.transpose(modulation, (1, 0, 2))
    row = out((OWN, WIDE))
    col = out((PART, ROWS))
    piece = out((PART, OWN))
    square = pltpu.VMEM((8, 128), F32)

    x0 = tokens.T
    x2 = swap(x0, 2)
    x1 = swap(x0, 1)
    pieces = [piece, piece, out((2 * PART, OWN))]
    parts = list(call(split_columns, pieces, [mine, cotangent.T], smem=1))
    weights = [wt[0], wt[1], out_weight[0], out_weight[1]]
    x2, weights, parts[0] = lax.optimization_barrier((x2, weights, parts[0]))
    wt_s, wt_t, wo_s, wo_t = weights
    x3 = swap(x2, 1)
    parts = exchange(parts)
    query, key, value, stats, p0, p1, p2, p3, xrow = call(
        spatial_forward,
        [col] * 3 + [out((16, ROWS), F32)] + [row] * 5,
        [mine, x0, x1, x2, x3, mod, head_gains, wt_s, wo_s],
        [pltpu.VMEM((WIDE, 8), F32), pltpu.VMEM((WIDE, ROWS), BF16),
         pltpu.VMEM((ROWS, WIDE), BF16), pltpu.VMEM((8, WIDE), F32), square],
        smem=1, wide=True,
    )
    m3, parts[2], parts[3] = lax.optimization_barrier((swap(p3, 1), parts[2], parts[3]))
    m1 = swap(p1, 1)
    chip = (p2.astype(F32) + m3.astype(F32)).astype(BF16)
    far = swap(chip, 2)
    cot0, wn, uw = call(
        gather_rows, [row, out((WIDE, 3 * PART)), out((8, 3 * PART), F32)],
        [mine, *parts, wt_s, mod],
        [pltpu.VMEM((WIDE, OWN), F32), pltpu.VMEM((8, WIDE), F32)], smem=1, wide=True, behind=[chip],
    )

    chunks = [lax.select_n(at ^ d, wt_t[0], wt_t[1], wt_t[2], wo_t) for d in (0, 2)]
    chunks, far, cot0 = lax.optimization_barrier((chunks, far, cot0))
    near = swap(from_neighbour(chunks[0], 3), 1)
    others = [near, round_x(near, 1), from_neighbour(chunks[1], 2), round_x(near, 3)]

    (rows,) = call(middle_rows, [out((OWN, 2 * WIDE))], [p0, m1, far, xrow, cot0, mod])
    tc0 = across_seq(rows)
    tc1 = swap(tc0, 1)
    gn, br, normed, gated = call(
        temporal_own, [out((2 * OWN, WIDE))] * 4,
        [tc0, tc1, mod, head_gains, wt_t, wo_t],
        [square],
    )
    gn0, gn1, op0, op1 = call(
        temporal_far,
        [out((OWN, WIDE), F32), row, out((OWN, WIDE), F32), row],
        [at.reshape(1), normed, gated, gn, br, head_gains, *others],
        [pltpu.VMEM((4 * PART, WIDE), BF16), square],
        smem=1,
    )
    gn1, op1 = swap(gn1, 1), swap(op1, 1)
    grad_middle, mixed_rows = call(
        temporal_finish, [row] * 2, [tc0, gn0, gn1, op0, op1, mod]
    )

    moved = across_seq(jnp.concatenate([grad_middle, mixed_rows], axis=1))
    g0 = moved[:, :WIDE]
    g2 = swap(g0, 2)
    g1 = swap(g0, 1)
    gq, gk, gv = call(
        spatial_backward_own,
        [out((PART, 2 * OWN)), out((PART, ROWS), F32), out((PART, ROWS), F32)],
        [mine, g0, g1, query, key, value, mod, wo_s],
        [pltpu.VMEM((2 * OWN, WIDE), BF16)],
        smem=1,
    )
    parts = call(split_rows, pieces, [mine, moved], [pltpu.VMEM((WIDE, OWN), F32)], smem=1)
    parts = list(parts)
    g2, gq, parts[0] = lax.optimization_barrier((g2, gq, parts[0]))
    g3 = swap(g2, 1)
    parts = exchange(parts)
    p2, p3, stacked, sums = call(
        spatial_backward_far,
        [col, col, out((3 * PART, ROWS)), out((8, ROWS), F32)],
        [mine, g2, g3, query, key, value, stats, gq, gk, gv, mod, head_gains, uw, wo_s,
         wn],
        [pltpu.VMEM((2 * OWN, WIDE), BF16), pltpu.VMEM((PART, ROWS), BF16), square],
        smem=1,
    )
    m3, other, parts[2], parts[3] = lax.optimization_barrier(
        (swap(p3, 1), swap(sums, 1), parts[2], parts[3])
    )
    chip, sums = call(
        chip_sums, [out((PART + 16, ROWS)), out((8, ROWS), F32)], [p2, m3, sums, other]
    )
    far = swap(chip, 2)
    p0, p1a, p1b, gown = call(
        spatial_backward_last,
        [col, out((PART // 2, ROWS)), out((PART // 2, ROWS)), col],
        [mine, stacked, g0, g1, g2, g3, wn],
        [pltpu.VMEM((WIDE, OWN), F32)],
        smem=1,
        behind=[chip],
    )
    m1a, m1b = swap(p1a, 1), swap(p1b, 1)

    (mixed,) = call(place_columns, [col], [mine, *parts], smem=1, behind=[p0])

    (grad,) = call(
        spatial_finish, [col], [mine, p0, m1a, m1b, far, sums, stats, x0, gown, mod],
        [pltpu.VMEM((8, WIDE), F32), pltpu.VMEM((WIDE, 8), F32)],
        smem=1,
    )
    return (mixed.T, grad.T)


def solution(mesh):
    in_specs = (
        P("seq", "head"),
        P("seq", "head"),
        P(None, None, None, "head"),
        P(None, "head", None),
        P(),
        P(),
    )
    out_specs = (P("seq", "head"), P("seq", "head"))
    return jax.shard_map(
        on_device, mesh=mesh, in_specs=in_specs, out_specs=out_specs, check_vma=False
    )
```

```python
import jax
import jax.numpy as jnp
from jax import lax
from jax.experimental import pallas as pl
from jax.experimental.pallas import tpu as pltpu
from jax.sharding import PartitionSpec as P

EPS = 1e-06
HEAD = 72
PER = 4
WIDE = 1152
PART = 288
ROWS = 512
OWN = 128
LOG2E = 1.4426950408889634
SCALE = HEAD**-0.5
F32 = jnp.float32
BF16 = jnp.bfloat16
VMEM_MIB = 24
VMEM_WIDE_MIB = 56


def dot(a, b, over):
    return lax.dot_general(a, b, (((over[0],), (over[1],)), ((), ())), preferred_element_type=F32)


def call(body, outs, operands, scratch=(), smem=0, behind=(), wide=False):
    n, skip = len(operands), len(behind)
    specs = [
        pl.BlockSpec(memory_space=pltpu.SMEM if i < smem else pltpu.VMEM) for i in range(n)
    ] + [pl.BlockSpec(memory_space=pl.ANY)] * skip

    def run(*refs):
        body(*refs[:n], *refs[n + skip :])

    return pl.pallas_call(
        run,
        out_shape=list(outs),
        in_specs=specs,
        out_specs=[pl.BlockSpec(memory_space=pltpu.VMEM)] * len(outs),
        scratch_shapes=list(scratch),
        compiler_params=pltpu.CompilerParams(vmem_limit_bytes=(VMEM_WIDE_MIB if wide else VMEM_MIB) * 2**20),
        cost_estimate=pl.CostEstimate(flops=1, bytes_accessed=1, transcendentals=0),
    )(*operands, *behind)


def out(shape, dtype=BF16):
    return jax.ShapeDtypeStruct(shape, dtype)


def head_norm_t(part, gains):
    n = part.shape[1]
    cube = part.reshape(PER, HEAD, n)
    inverse = lax.rsqrt(jnp.sum(cube * cube, axis=1, keepdims=True) * (1.0 / HEAD) + EPS)
    return (cube * inverse * gains.reshape(PER, HEAD, 1)).reshape(PART, n).astype(BF16), inverse


def head_back_t(incoming, normed, inverse, gains):
    n = incoming.shape[1]
    grad = incoming.astype(F32).reshape(PER, HEAD, n)
    norm = normed.astype(F32).reshape(PER, HEAD, n)
    gain = gains.reshape(PER, HEAD, 1)
    inner = jnp.sum(norm * grad, axis=1, keepdims=True) * (1.0 / HEAD)
    return (inverse * (gain * grad - norm * (1.0 / gain) * inner)).reshape(PART, n).astype(BF16)


def turned_lines(mod, lines):
    lines[...] = jnp.zeros_like(lines)
    for i in range(3):
        lines[i : i + 1, :] = mod[i, 0:1, :]
    lines[3:4, :] = 1.0 + mod[1, 0:1, :]
    return lines[...].T


def gain_columns(gains, block, square):
    square[...] = jnp.zeros_like(square)
    square[0:2, 0:HEAD] = gains[block]
    turned = square[...].T
    return [jnp.concatenate([turned[:HEAD, i : i + 1]] * PER, axis=0) for i in range(2)]


def one_ahead(start, depth=2):
    heads = [slice(h * HEAD, (h + 1) * HEAD) for h in range(PER)]
    ahead = [start(rows) for rows in heads[:depth]]
    for h, rows in enumerate(heads):
        if h + depth < PER:
            ahead.append(start(heads[h + depth]))
        yield rows, ahead.pop(0)


def softmax_pieces(query, key, value):
    pieces = []
    for rows, scores in one_ahead(lambda rows: dot(key[rows], query[rows], (0, 0))):
        unnormed = jnp.exp2(scores * (SCALE * LOG2E))
        total = jnp.sum(unnormed, axis=0, keepdims=True)
        pieces.append(dot(value[rows], unnormed.astype(BF16), (1, 0)) * (1.0 / total))
    return jnp.concatenate(pieces, axis=0).astype(BF16)


def half_of(me, other):
    return pl.ds(pl.multiple_of(((me // 2) ^ other) * 2 * OWN, 2 * OWN), 2 * OWN)


def core_of(me, d):
    return pl.ds(pl.multiple_of(((me ^ d) & 1) * OWN, OWN), OWN)


def part_of(me, d):
    return pl.ds(pl.multiple_of((me ^ d) * PART, 32), PART)


def own_of(me, d):
    return pl.ds(pl.multiple_of((me ^ d) * OWN, OWN), OWN)


def spatial_forward(
    me_ref, x0, x1, x2, x3, mod, gains, wt, wo, q_o, k_o, v_o, st_o, p0, p1, p2, p3, xrow,
    modc, xs, both, lines, square,
):
    me = me_ref[0]
    gain_q, gain_k = gain_columns(gains, 0, square)
    modc[...] = turned_lines(mod, lines)
    for d, x in enumerate((x0, x1, x2, x3)):
        xs[part_of(me, d), :] = x[...]
    stream = xs[...].astype(F32)
    mean = jnp.sum(stream, axis=0, keepdims=True) * (1.0 / WIDE)
    centred = stream - mean
    inverse = lax.rsqrt(jnp.sum(centred * centred, axis=0, keepdims=True) * (1.0 / WIDE) + EPS)
    normed = (centred * inverse * (1.0 + modc[:, 1:2]) + modc[:, 0:1]).astype(BF16)
    weights = wt[...].reshape(3 * PART, WIDE)
    projected = dot(weights, normed, (1, 0))
    query, inv_q = head_norm_t(projected[:PART], gain_q)
    key, inv_k = head_norm_t(projected[PART : 2 * PART], gain_k)
    q_o[...] = query
    k_o[...] = key
    v_o[...] = projected[2 * PART :].astype(BF16)
    st_o[0:4, :] = inv_q.reshape(PER, ROWS)
    st_o[4:8, :] = inv_k.reshape(PER, ROWS)
    st_o[8:9, :] = mean
    st_o[9:10, :] = inverse
    attended = softmax_pieces(query, key, v_o[...])
    branch = dot(attended, wo[...], (0, 0)).astype(BF16)
    both[...] = branch
    for d, partial in enumerate((p0, p1, p2, p3)):
        partial[...] = both[own_of(me, d), :]
    xrow[...] = xs[:, own_of(me, 0)].astype(F32).T.astype(BF16)


def temporal_group(normed, gated, gain_q, gain_k, weights, wo):
    n = normed.shape[0]
    left = lax.broadcasted_iota(jnp.int32, (n, n), 0)
    right = lax.broadcasted_iota(jnp.int32, (n, n), 1)
    mask = ((left & 1) == (right & 1)) & ((left // OWN) == (right // OWN))
    projected = dot(weights, normed, (1, 1))
    query, inv_q = head_norm_t(projected[:PART], gain_q)
    key, inv_k = head_norm_t(projected[PART : 2 * PART], gain_k)
    value = projected[2 * PART :].astype(BF16)
    grad_att = dot(wo, gated, (1, 1)).astype(BF16)
    attended, gq, gk, gv = [], [], [], []

    def start(rows):
        return dot(key[rows], query[rows], (0, 0)), dot(value[rows], grad_att[rows], (0, 0))

    for rows, (scores, grad_probs) in one_ahead(start):
        q, k, v, da = query[rows], key[rows], value[rows], grad_att[rows]
        unnormed = jnp.where(mask, jnp.exp2(scores * (SCALE * LOG2E)), 0.0)
        probs = unnormed * (1.0 / jnp.sum(unnormed, axis=0, keepdims=True))
        rounded = probs.astype(BF16)
        attended.append(dot(v, rounded, (1, 0)))
        inner = jnp.sum(grad_probs * probs, axis=0, keepdims=True)
        grad_scores = (probs * (grad_probs - inner)).astype(BF16)
        gv.append(dot(da, rounded, (1, 1)))
        gq.append(dot(k, grad_scores, (1, 0)) * SCALE)
        gk.append(dot(q, grad_scores, (1, 1)) * SCALE)
    attended = jnp.concatenate(attended, axis=0).astype(BF16)
    gq = jnp.concatenate(gq, axis=0).astype(BF16)
    gk = jnp.concatenate(gk, axis=0).astype(BF16)
    gv = jnp.concatenate(gv, axis=0).astype(BF16)
    dq = head_back_t(gq, query, inv_q, gain_q)
    dk = head_back_t(gk, key, inv_k, gain_k)
    stacked = jnp.concatenate([dq, dk, gv], axis=0)
    return dot(stacked, weights, (0, 0)), dot(attended, wo, (0, 0))


def temporal_own(tc0, tc1, mod, gains, wt, wo, gn_o, br_o, normed_o, gated_o, square):
    both = jnp.concatenate([tc0[...], tc1[...]], axis=0)
    stream, incoming = both[:, :WIDE].astype(F32), both[:, WIDE:].astype(F32)
    mean = jnp.sum(stream, axis=1, keepdims=True) * (1.0 / WIDE)
    centred = stream - mean
    inverse = lax.rsqrt(jnp.sum(centred * centred, axis=1, keepdims=True) * (1.0 / WIDE) + EPS)
    normed = (centred * inverse * (1.0 + mod[1, 1:2, :]) + mod[0, 1:2, :]).astype(BF16)
    gated = (mod[2, 1:2, :] * incoming).astype(BF16)
    normed_o[...] = normed
    gated_o[...] = gated
    term, branch = temporal_group(
        normed, gated, *gain_columns(gains, 1, square), wt[...].reshape(3 * PART, WIDE), wo[...]
    )
    gn_o[...] = term.astype(BF16)
    br_o[...] = branch.astype(BF16)


def temporal_far(
    at_ref, normed, gated, gn_r, br_r, gains, w0, w1, w2, w3, gn0, gn1, op0, op1, ws, square
):
    for d, w in enumerate((w0, w1, w2, w3)):
        ws[pl.ds(pl.multiple_of(((at_ref[0] + d) & 3) * PART, 32), PART), :] = w[...]
    term, branch = temporal_group(
        normed[...],
        gated[...],
        *gain_columns(gains, 1, square),
        ws[: 3 * PART, :],
        ws[3 * PART :, :],
    )
    term = term + gn_r[...].astype(F32)
    branch = branch + br_r[...].astype(F32)
    gn0[...] = term[:OWN]
    gn1[...] = term[OWN:].astype(BF16)
    op0[...] = branch[:OWN]
    op1[...] = branch[OWN:].astype(BF16)


def temporal_finish(tc0, gn0, gn1, op0, op1, mod, gm_o, mixed_o):
    stream = tc0[:, :WIDE].astype(F32)
    mean = jnp.sum(stream, axis=1, keepdims=True) * (1.0 / WIDE)
    shifted = stream - mean
    inverse = lax.rsqrt(jnp.sum(shifted * shifted, axis=1, keepdims=True) * (1.0 / WIDE) + EPS)
    centred = shifted * inverse
    scaled = (gn0[...] + gn1[...].astype(F32)) * (1.0 + mod[1, 1:2, :])
    first = jnp.sum(scaled, axis=1, keepdims=True) * (1.0 / WIDE)
    second = jnp.sum(scaled * centred, axis=1, keepdims=True) * (1.0 / WIDE)
    gm_o[...] = (tc0[:, WIDE:].astype(F32) + inverse * (scaled - first - centred * second)).astype(BF16)
    mixed_o[...] = (stream + mod[2, 1:2, :] * (op0[...] + op1[...].astype(F32))).astype(BF16)


def backward_half(queries, grad_att, k_r, v_r):
    gq, gk, gv = [], [], []

    def start(rows):
        return dot(k_r[rows, :], queries[rows], (0, 0)), dot(v_r[rows, :], grad_att[rows], (0, 0))

    for rows, (scores, grad_probs) in one_ahead(start):
        q, k, da = queries[rows], k_r[rows, :], grad_att[rows]
        unnormed = jnp.exp2(scores * (SCALE * LOG2E))
        probs = unnormed * (1.0 / jnp.sum(unnormed, axis=0, keepdims=True))
        rounded = probs.astype(BF16)
        inner = jnp.sum(grad_probs * probs, axis=0, keepdims=True)
        grad_scores = (probs * (grad_probs - inner)).astype(BF16)
        gv.append(dot(da, rounded, (1, 1)))
        gk.append(dot(q, grad_scores, (1, 1)))
        gq.append(dot(k, grad_scores, (1, 0)) * SCALE)
    return [jnp.concatenate(g, axis=0) for g in (gq, gk, gv)]


def gated_half(me, d, ga, gb, mod, rows):
    rows[core_of(me, d), :] = (mod[2, 0:1, :] * ga[...].astype(F32)).astype(BF16)
    rows[core_of(me, d ^ 1), :] = (mod[2, 0:1, :] * gb[...].astype(F32)).astype(BF16)
    return rows[...]


def spatial_backward_own(
    me_ref, g0, g1, q_r, k_r, v_r, mod, wo, gq_o, gk_o, gv_o, rows
):
    me = me_ref[0]
    gated = gated_half(me, 0, g0, g1, mod, rows)
    grad_att = dot(wo[...], gated, (1, 1)).astype(BF16)
    gq, gk, gv = backward_half(q_r[:, half_of(me, 0)], grad_att, k_r, v_r)
    gq_o[...] = gq.astype(BF16)
    gk_o[...] = gk
    gv_o[...] = gv


def norm_sums(part, normed, inverse, gains, uw, start):
    n = part.shape[1]
    grad = part.astype(F32)
    before = normed.astype(F32)
    if inverse is not None:
        before = (before * (1.0 / gains)).reshape(PER, HEAD, n) * (1.0 / inverse)
        before = before.reshape(PART, n)
    shift, scale = uw[start : start + PART, 0:1], uw[start : start + PART, 3:4]
    first = jnp.sum(grad * scale, axis=0, keepdims=True)
    return first, jnp.sum(grad * (before - shift), axis=0, keepdims=True)


def spatial_backward_far(
    me_ref, g2, g3, q_r, k_r, v_r, st, gq_r, gk_r, gv_r, mod, gains, uw_r, wo, wn,
    p2, p3, stacked_o, rs_o, rows, gq_s, square,
):
    me = me_ref[0]
    gated = gated_half(me, 2, g2, g3, mod, rows)
    grad_att = dot(wo[...], gated, (1, 1)).astype(BF16)
    gq, gk, gv = backward_half(q_r[:, half_of(me, 1)], grad_att, k_r, v_r)
    gain_q, gain_k = gain_columns(gains, 0, square)
    gq_s[:, half_of(me, 0)] = gq_r[...]
    gq_s[:, half_of(me, 1)] = gq.astype(BF16)
    gk = ((gk + gk_r[...]) * SCALE).astype(BF16)
    inv_q = st[0:4, :].reshape(PER, 1, ROWS)
    inv_k = st[4:8, :].reshape(PER, 1, ROWS)
    stacked_o[:PART, :] = head_back_t(gq_s[...], q_r[...], inv_q, gain_q)
    stacked_o[PART : 2 * PART, :] = head_back_t(gk, k_r[...], inv_k, gain_k)
    stacked_o[2 * PART :, :] = (gv + gv_r[...]).astype(BF16)
    stacked = stacked_o[...]
    turned = wn
    for d, partial in ((3, p3), (2, p2)):
        partial[...] = dot(turned[part_of(me, d), :], stacked, (1, 0)).astype(BF16)
    uw = uw_r[...].T
    sums = [
        norm_sums(stacked[:PART], q_r[...], inv_q, gain_q, uw, 0),
        norm_sums(stacked[PART : 2 * PART], k_r[...], inv_k, gain_k, uw, PART),
        norm_sums(stacked[2 * PART :], v_r[...], None, None, uw, 2 * PART),
    ]
    rs_o[...] = jnp.zeros_like(rs_o)
    rs_o[0:1, :] = sums[0][0] + sums[1][0] + sums[2][0]
    rs_o[1:2, :] = sums[0][1] + sums[1][1] + sums[2][1]


def spatial_backward_last(me_ref, stacked_r, g0, g1, g2, g3, wn, p0, p1a, p1b, gown, rows):
    me = me_ref[0]
    stacked = stacked_r[...]
    turned = wn
    part = dot(turned[part_of(me, 1), :], stacked, (1, 0)).astype(BF16)
    p1a[...] = part[: PART // 2]
    p1b[...] = part[PART // 2 :]
    p0[...] = dot(turned[part_of(me, 0), :], stacked, (1, 0)).astype(BF16)
    for d, g in enumerate((g0, g1, g2, g3)):
        rows[...] = g[...].astype(F32).T
        gown[:, own_of(me, d)] = rows[part_of(me, 0), :].astype(BF16)


def chip_sums(p2, m3, sums, other, chip_o, sums_o):
    total = sums[...] + other[...]
    sums_o[...] = total
    chip_o[:PART, :] = (p2[...].astype(F32) + m3[...].astype(F32)).astype(BF16)
    chip_o[PART:, :] = jnp.concatenate([total, jnp.zeros_like(total)], axis=0).astype(BF16)


def middle_rows(p0, m1, far, xrow, cot, mod, rows_o):
    branch = p0[...].astype(F32) + m1[...].astype(F32) + far[...].astype(F32)
    rows_o[:, :WIDE] = (xrow[...].astype(F32) + mod[2, 0:1, :] * branch).astype(BF16)
    rows_o[:, WIDE:] = cot[...]


def spatial_finish(me_ref, p0, m1a, m1b, o2, rs, st, x0, gown, mod, out_o, lines, modc):
    modc[...] = turned_lines(mod, lines)
    m1 = jnp.concatenate([m1a[...], m1b[...]], axis=0)
    grad = p0[...].astype(F32) + m1.astype(F32) + o2[:PART, :].astype(F32)
    inverse = st[9:10, :]
    scaled = grad * (1.0 + modc[part_of(me_ref[0], 0), 1:2])
    centred = (x0[...].astype(F32) - st[8:9, :]) * inverse
    more = o2[PART:, :].astype(F32)
    first = (rs[0:1, :] + more[0:1]) * (1.0 / WIDE)
    second = (rs[1:2, :] + more[1:2]) * (1.0 / WIDE)
    out_o[...] = (gown[...].astype(F32) + inverse * (scaled - first - centred * second)).astype(BF16)


def split_columns(me_ref, columns, c0, c1, c23):
    me = me_ref[0]
    c0[...] = columns[:, own_of(me, 0)]
    c1[...] = columns[:, own_of(me, 1)]
    c23[:PART, :] = columns[:, own_of(me, 2)]
    c23[PART:, :] = columns[:, own_of(me, 3)]


def moves(swapped):
    a = lax.broadcasted_iota(jnp.int32, (ROWS, ROWS), 0)
    b = lax.broadcasted_iota(jnp.int32, (ROWS, ROWS), 1)
    if swapped:
        a, b = b, a
    target = ((a >> 1) & 3) * OWN + (a >> 3) * 2 + (a & 1)
    return jnp.where(target == b, 1.0, 0.0).astype(BF16)


def unpack_rows(rows, columns_o):
    columns_o[...] = dot(rows[...], moves(False), (0, 0)).astype(BF16)


def pack_parts(me_ref, c0, c1, c2, c3, rows_o, cs):
    me = me_ref[0]
    for d, c in enumerate((c0[...], c1[...], c2[:PART, :], c3[PART:, :])):
        cs[:, own_of(me, d)] = c
    rows_o[...] = dot(moves(False), cs[...], (1, 1)).astype(BF16)


def gather_rows(me_ref, c0, c1, c2, c3, wt, mod, rows_o, wn_o, uw_o, cs, lines):
    me = me_ref[0]
    weights = wt[...].reshape(3 * PART, WIDE)
    wn_o[...] = weights.T
    uw_o[...] = dot(weights, turned_lines(mod, lines).astype(BF16), (1, 0)).T
    for d, c in enumerate((c0[...], c1[...], c2[:PART, :], c3[PART:, :])):
        cs[part_of(me, d), :] = c.astype(F32)
    rows_o[...] = cs[...].T.astype(BF16)


def split_rows(me_ref, rows, c0, c1, c23, cs):
    me = me_ref[0]
    cs[...] = rows[...].astype(F32).T
    c0[...] = cs[part_of(me, 0), :].astype(BF16)
    c1[...] = cs[part_of(me, 1), :].astype(BF16)
    c23[:PART, :] = cs[part_of(me, 2), :].astype(BF16)
    c23[PART:, :] = cs[part_of(me, 3), :].astype(BF16)


def swap(values, d):
    return lax.ppermute(values, "head", [(i, i ^ d) for i in range(4)])


def exchange(parts):
    mine, mate, both = parts
    far = swap(both, 2)
    return [mine, swap(mate, 1), far, swap(far, 1)]


def across_seq(rows, lines, width):
    moved = lax.all_to_all(
        rows.reshape(64, lines, width), "seq", split_axis=0, concat_axis=0, tiled=True
    )
    return moved.reshape(64 * lines, width)


def from_neighbour(chunk, d):
    index = [(s, h) for s in range(64) for h in range(4)]
    near = [(s * 4 + h, (s ^ 4) * 4 + (h ^ d)) for s, h in index]
    return lax.ppermute(chunk, ("seq", "head"), near)


def round_x(chunk, d):
    return lax.ppermute(chunk, "seq", [(s // 4 * 4 + (s + d) % 4, s) for s in range(64)])


def on_device(tokens, cotangent, qkv_weight, out_weight, modulation, head_gains):
    me = lax.axis_index("head")
    mine = me.astype(jnp.int32).reshape(1)
    at = (lax.axis_index("seq") & 3).astype(jnp.int32)
    wt = jnp.transpose(qkv_weight, (0, 2, 3, 1))
    mod = jnp.transpose(modulation, (1, 0, 2))
    row = out((OWN, WIDE))
    col = out((PART, ROWS))
    piece = out((PART, OWN))
    square = pltpu.VMEM((8, 128), F32)

    x0 = tokens.T
    x2 = swap(x0, 2)
    x1 = swap(x0, 1)
    pieces = [piece, piece, out((2 * PART, OWN))]
    parts = list(call(split_columns, pieces, [mine, cotangent.T], smem=1))
    weights = [wt[0], wt[1], out_weight[0], out_weight[1]]
    x2, weights, parts[0] = lax.optimization_barrier((x2, weights, parts[0]))
    wt_s, wt_t, wo_s, wo_t = weights
    x3 = swap(x2, 1)
    parts = exchange(parts)
    query, key, value, stats, p0, p1, p2, p3, xrow = call(
        spatial_forward,
        [col] * 3 + [out((16, ROWS), F32)] + [row] * 5,
        [mine, x0, x1, x2, x3, mod, head_gains, wt_s, wo_s],
        [pltpu.VMEM((WIDE, 8), F32), pltpu.VMEM((WIDE, ROWS), BF16),
         pltpu.VMEM((ROWS, WIDE), BF16), pltpu.VMEM((8, WIDE), F32), square],
        smem=1, wide=True,
    )
    m3, parts[2], parts[3] = lax.optimization_barrier((swap(p3, 1), parts[2], parts[3]))
    m1 = swap(p1, 1)
    chip = (p2.astype(F32) + m3.astype(F32)).astype(BF16)
    far = swap(chip, 2)
    cot0, wn, uw = call(
        gather_rows, [row, out((WIDE, 3 * PART)), out((8, 3 * PART), F32)],
        [mine, *parts, wt_s, mod],
        [pltpu.VMEM((WIDE, OWN), F32), pltpu.VMEM((8, WIDE), F32)], smem=1, wide=True, behind=[chip],
    )

    chunks = [lax.select_n(at ^ d, wt_t[0], wt_t[1], wt_t[2], wo_t) for d in (0, 2)]
    chunks, far, cot0 = lax.optimization_barrier((chunks, far, cot0))
    near = swap(from_neighbour(chunks[0], 3), 1)
    others = [near, round_x(near, 1), from_neighbour(chunks[1], 2), round_x(near, 3)]

    (rows,) = call(middle_rows, [out((OWN, 2 * WIDE))], [p0, m1, far, xrow, cot0, mod])
    tc0 = across_seq(rows, 2, 2 * WIDE)
    tc1 = swap(tc0, 1)
    gn, br, normed, gated = call(
        temporal_own, [out((2 * OWN, WIDE))] * 4,
        [tc0, tc1, mod, head_gains, wt_t, wo_t],
        [square],
    )
    gn0, gn1, op0, op1 = call(
        temporal_far,
        [out((OWN, WIDE), F32), row, out((OWN, WIDE), F32), row],
        [at.reshape(1), normed, gated, gn, br, head_gains, *others],
        [pltpu.VMEM((4 * PART, WIDE), BF16), square],
        smem=1,
    )
    gn1, op1 = swap(gn1, 1), swap(op1, 1)
    grad_middle, mixed_rows = call(
        temporal_finish, [row] * 2, [tc0, gn0, gn1, op0, op1, mod]
    )

    parts = call(
        split_rows, pieces, [mine, mixed_rows], [pltpu.VMEM((WIDE, OWN), F32)], smem=1
    )
    (mixed_rows,) = call(
        pack_parts, [out((ROWS, PART))], [mine, *exchange(parts)],
        [pltpu.VMEM((PART, ROWS), BF16)], smem=1,
    )
    g0 = across_seq(grad_middle, 2, WIDE)
    g0, mixed_rows = lax.optimization_barrier((g0, mixed_rows))
    g2 = swap(g0, 2)
    g1 = swap(g0, 1)
    g1, mixed_rows = lax.optimization_barrier((g1, mixed_rows))
    mixed_rows = across_seq(mixed_rows, 8, PART)

    gq, gk, gv = call(
        spatial_backward_own,
        [out((PART, 2 * OWN)), out((PART, ROWS), F32), out((PART, ROWS), F32)],
        [mine, g0, g1, query, key, value, mod, wo_s],
        [pltpu.VMEM((2 * OWN, WIDE), BF16)],
        smem=1,
    )
    g2, gq = lax.optimization_barrier((g2, gq))
    g3 = swap(g2, 1)
    p2, p3, stacked, sums = call(
        spatial_backward_far,
        [col, col, out((3 * PART, ROWS)), out((8, ROWS), F32)],
        [mine, g2, g3, query, key, value, stats, gq, gk, gv, mod, head_gains, uw, wo_s,
         wn],
        [pltpu.VMEM((2 * OWN, WIDE), BF16), pltpu.VMEM((PART, ROWS), BF16), square],
        smem=1,
    )
    m3, other = swap(p3, 1), swap(sums, 1)
    chip, sums = call(
        chip_sums, [out((PART + 16, ROWS)), out((8, ROWS), F32)], [p2, m3, sums, other]
    )
    far = swap(chip, 2)
    p0, p1a, p1b, gown = call(
        spatial_backward_last,
        [col, out((PART // 2, ROWS)), out((PART // 2, ROWS)), col],
        [mine, stacked, g0, g1, g2, g3, wn],
        [pltpu.VMEM((WIDE, OWN), F32)],
        smem=1,
        behind=[chip, mixed_rows],
    )
    m1a, m1b = swap(p1a, 1), swap(p1b, 1)

    (mixed,) = call(unpack_rows, [col], [mixed_rows], behind=[p0])

    (grad,) = call(
        spatial_finish, [col], [mine, p0, m1a, m1b, far, sums, stats, x0, gown, mod],
        [pltpu.VMEM((8, WIDE), F32), pltpu.VMEM((WIDE, 8), F32)],
        smem=1,
    )
    return (mixed.T, grad.T)


def solution(mesh):
    in_specs = (
        P("seq", "head"),
        P("seq", "head"),
        P(None, None, None, "head"),
        P(None, "head", None),
        P(),
        P(),
    )
    out_specs = (P("seq", "head"), P("seq", "head"))
    return jax.shard_map(
        on_device, mesh=mesh, in_specs=in_specs, out_specs=out_specs, check_vma=False
    )
```

```python
import jax
import jax.numpy as jnp
from jax import lax
from jax.experimental import pallas as pl
from jax.experimental.pallas import tpu as pltpu
from jax.sharding import PartitionSpec as P

EPS = 1e-06
HEAD = 72
PER = 4
WIDE = 1152
PART = 288
ROWS = 512
OWN = 128
LOG2E = 1.4426950408889634
SCALE = HEAD**-0.5
F32 = jnp.float32
BF16 = jnp.bfloat16
VMEM_MIB = 24
VMEM_WIDE_MIB = 56


def dot(a, b, over):
    return lax.dot_general(a, b, (((over[0],), (over[1],)), ((), ())), preferred_element_type=F32)


def call(body, outs, operands, scratch=(), smem=0, behind=(), wide=False):
    n, skip = len(operands), len(behind)
    specs = [
        pl.BlockSpec(memory_space=pltpu.SMEM if i < smem else pltpu.VMEM) for i in range(n)
    ] + [pl.BlockSpec(memory_space=pl.ANY)] * skip

    def run(*refs):
        body(*refs[:n], *refs[n + skip :])

    return pl.pallas_call(
        run,
        out_shape=list(outs),
        in_specs=specs,
        out_specs=[pl.BlockSpec(memory_space=pltpu.VMEM)] * len(outs),
        scratch_shapes=list(scratch),
        compiler_params=pltpu.CompilerParams(vmem_limit_bytes=(VMEM_WIDE_MIB if wide else VMEM_MIB) * 2**20),
        cost_estimate=pl.CostEstimate(flops=1, bytes_accessed=1, transcendentals=0),
    )(*operands, *behind)


def out(shape, dtype=BF16):
    return jax.ShapeDtypeStruct(shape, dtype)


def head_norm_t(part, gains):
    n = part.shape[1]
    cube = part.reshape(PER, HEAD, n)
    inverse = lax.rsqrt(jnp.sum(cube * cube, axis=1, keepdims=True) * (1.0 / HEAD) + EPS)
    return (cube * inverse * gains.reshape(PER, HEAD, 1)).reshape(PART, n).astype(BF16), inverse


def head_back_t(incoming, normed, inverse, gains):
    n = incoming.shape[1]
    grad = incoming.astype(F32).reshape(PER, HEAD, n)
    norm = normed.astype(F32).reshape(PER, HEAD, n)
    gain = gains.reshape(PER, HEAD, 1)
    inner = jnp.sum(norm * grad, axis=1, keepdims=True) * (1.0 / HEAD)
    return (inverse * (gain * grad - norm * (1.0 / gain) * inner)).reshape(PART, n).astype(BF16)


def turned_lines(mod, lines):
    lines[...] = jnp.zeros_like(lines)
    for i in range(3):
        lines[i : i + 1, :] = mod[i, 0:1, :]
    lines[3:4, :] = 1.0 + mod[1, 0:1, :]
    return lines[...].T


def gain_columns(gains, block, square):
    square[...] = jnp.zeros_like(square)
    square[0:2, 0:HEAD] = gains[block]
    turned = square[...].T
    return [jnp.concatenate([turned[:HEAD, i : i + 1]] * PER, axis=0) for i in range(2)]


def one_ahead(start, depth=2):
    heads = [slice(h * HEAD, (h + 1) * HEAD) for h in range(PER)]
    ahead = [start(rows) for rows in heads[:depth]]
    for h, rows in enumerate(heads):
        if h + depth < PER:
            ahead.append(start(heads[h + depth]))
        yield rows, ahead.pop(0)


def softmax_pieces(query, key, value):
    pieces = []
    for rows, scores in one_ahead(lambda rows: dot(key[rows], query[rows], (0, 0))):
        unnormed = jnp.exp2(scores * (SCALE * LOG2E))
        total = jnp.sum(unnormed, axis=0, keepdims=True)
        pieces.append(dot(value[rows], unnormed.astype(BF16), (1, 0)) * (1.0 / total))
    return jnp.concatenate(pieces, axis=0).astype(BF16)


def half_of(me, other):
    return pl.ds(pl.multiple_of(((me // 2) ^ other) * 2 * OWN, 2 * OWN), 2 * OWN)


def core_of(me, d):
    return pl.ds(pl.multiple_of(((me ^ d) & 1) * OWN, OWN), OWN)


def part_of(me, d):
    return pl.ds(pl.multiple_of((me ^ d) * PART, 32), PART)


def own_of(me, d):
    return pl.ds(pl.multiple_of((me ^ d) * OWN, OWN), OWN)


def spatial_forward(
    me_ref, x0, x1, x2, x3, mod, gains, wt, wo, q_o, k_o, v_o, st_o, p0, p1, p2, p3, xrow,
    modc, xs, both, lines, square,
):
    me = me_ref[0]
    gain_q, gain_k = gain_columns(gains, 0, square)
    modc[...] = turned_lines(mod, lines)
    for d, x in enumerate((x0, x1, x2, x3)):
        xs[part_of(me, d), :] = x[...]
    stream = xs[...].astype(F32)
    mean = jnp.sum(stream, axis=0, keepdims=True) * (1.0 / WIDE)
    centred = stream - mean
    inverse = lax.rsqrt(jnp.sum(centred * centred, axis=0, keepdims=True) * (1.0 / WIDE) + EPS)
    normed = (centred * inverse * (1.0 + modc[:, 1:2]) + modc[:, 0:1]).astype(BF16)
    weights = wt[...].reshape(3 * PART, WIDE)
    projected = dot(weights, normed, (1, 0))
    query, inv_q = head_norm_t(projected[:PART], gain_q)
    key, inv_k = head_norm_t(projected[PART : 2 * PART], gain_k)
    q_o[...] = query
    k_o[...] = key
    v_o[...] = projected[2 * PART :].astype(BF16)
    st_o[0:4, :] = inv_q.reshape(PER, ROWS)
    st_o[4:8, :] = inv_k.reshape(PER, ROWS)
    st_o[8:9, :] = mean
    st_o[9:10, :] = inverse
    attended = softmax_pieces(query, key, v_o[...])
    branch = dot(attended, wo[...], (0, 0)).astype(BF16)
    both[...] = branch
    for d, partial in enumerate((p0, p1, p2, p3)):
        partial[...] = both[own_of(me, d), :]
    xrow[...] = xs[:, own_of(me, 0)].astype(F32).T.astype(BF16)


def temporal_group(normed, gated, gain_q, gain_k, weights, wo):
    n = normed.shape[0]
    left = lax.broadcasted_iota(jnp.int32, (n, n), 0)
    right = lax.broadcasted_iota(jnp.int32, (n, n), 1)
    mask = ((left & 1) == (right & 1)) & ((left // OWN) == (right // OWN))
    projected = dot(weights, normed, (1, 1))
    query, inv_q = head_norm_t(projected[:PART], gain_q)
    key, inv_k = head_norm_t(projected[PART : 2 * PART], gain_k)
    value = projected[2 * PART :].astype(BF16)
    grad_att = dot(wo, gated, (1, 1)).astype(BF16)
    attended, gq, gk, gv = [], [], [], []

    def start(rows):
        return dot(key[rows], query[rows], (0, 0)), dot(value[rows], grad_att[rows], (0, 0))

    for rows, (scores, grad_probs) in one_ahead(start):
        q, k, v, da = query[rows], key[rows], value[rows], grad_att[rows]
        unnormed = jnp.where(mask, jnp.exp2(scores * (SCALE * LOG2E)), 0.0)
        probs = unnormed * (1.0 / jnp.sum(unnormed, axis=0, keepdims=True))
        rounded = probs.astype(BF16)
        attended.append(dot(v, rounded, (1, 0)))
        inner = jnp.sum(grad_probs * probs, axis=0, keepdims=True)
        grad_scores = (probs * (grad_probs - inner)).astype(BF16)
        gv.append(dot(da, rounded, (1, 1)))
        gq.append(dot(k, grad_scores, (1, 0)) * SCALE)
        gk.append(dot(q, grad_scores, (1, 1)) * SCALE)
    attended = jnp.concatenate(attended, axis=0).astype(BF16)
    gq = jnp.concatenate(gq, axis=0).astype(BF16)
    gk = jnp.concatenate(gk, axis=0).astype(BF16)
    gv = jnp.concatenate(gv, axis=0).astype(BF16)
    dq = head_back_t(gq, query, inv_q, gain_q)
    dk = head_back_t(gk, key, inv_k, gain_k)
    stacked = jnp.concatenate([dq, dk, gv], axis=0)
    return dot(stacked, weights, (0, 0)), dot(attended, wo, (0, 0))


def temporal_own(tc0, tc1, mod, gains, wt, wo, gn_o, br_o, normed_o, gated_o, square):
    both = jnp.concatenate([tc0[...], tc1[...]], axis=0)
    stream, incoming = both[:, :WIDE].astype(F32), both[:, WIDE:].astype(F32)
    mean = jnp.sum(stream, axis=1, keepdims=True) * (1.0 / WIDE)
    centred = stream - mean
    inverse = lax.rsqrt(jnp.sum(centred * centred, axis=1, keepdims=True) * (1.0 / WIDE) + EPS)
    normed = (centred * inverse * (1.0 + mod[1, 1:2, :]) + mod[0, 1:2, :]).astype(BF16)
    gated = (mod[2, 1:2, :] * incoming).astype(BF16)
    normed_o[...] = normed
    gated_o[...] = gated
    term, branch = temporal_group(
        normed, gated, *gain_columns(gains, 1, square), wt[...].reshape(3 * PART, WIDE), wo[...]
    )
    gn_o[...] = term.astype(BF16)
    br_o[...] = branch.astype(BF16)


def temporal_far(
    at_ref, normed, gated, gn_r, br_r, gains, w0, w1, w2, w3, gn0, gn1, op0, op1, ws, square
):
    for d, w in enumerate((w0, w1, w2, w3)):
        ws[pl.ds(pl.multiple_of(((at_ref[0] + d) & 3) * PART, 32), PART), :] = w[...]
    term, branch = temporal_group(
        normed[...],
        gated[...],
        *gain_columns(gains, 1, square),
        ws[: 3 * PART, :],
        ws[3 * PART :, :],
    )
    term = term + gn_r[...].astype(F32)
    branch = branch + br_r[...].astype(F32)
    gn0[...] = term[:OWN]
    gn1[...] = term[OWN:].astype(BF16)
    op0[...] = branch[:OWN]
    op1[...] = branch[OWN:].astype(BF16)


def temporal_finish(tc0, gn0, gn1, op0, op1, mod, gm_o, mixed_o):
    stream = tc0[:, :WIDE].astype(F32)
    mean = jnp.sum(stream, axis=1, keepdims=True) * (1.0 / WIDE)
    shifted = stream - mean
    inverse = lax.rsqrt(jnp.sum(shifted * shifted, axis=1, keepdims=True) * (1.0 / WIDE) + EPS)
    centred = shifted * inverse
    scaled = (gn0[...] + gn1[...].astype(F32)) * (1.0 + mod[1, 1:2, :])
    first = jnp.sum(scaled, axis=1, keepdims=True) * (1.0 / WIDE)
    second = jnp.sum(scaled * centred, axis=1, keepdims=True) * (1.0 / WIDE)
    gm_o[...] = (tc0[:, WIDE:].astype(F32) + inverse * (scaled - first - centred * second)).astype(BF16)
    mixed_o[...] = (stream + mod[2, 1:2, :] * (op0[...] + op1[...].astype(F32))).astype(BF16)


def backward_half(queries, grad_att, k_r, v_r):
    gq, gk, gv = [], [], []

    def start(rows):
        return dot(k_r[rows, :], queries[rows], (0, 0)), dot(v_r[rows, :], grad_att[rows], (0, 0))

    for rows, (scores, grad_probs) in one_ahead(start):
        q, k, da = queries[rows], k_r[rows, :], grad_att[rows]
        unnormed = jnp.exp2(scores * (SCALE * LOG2E))
        probs = unnormed * (1.0 / jnp.sum(unnormed, axis=0, keepdims=True))
        rounded = probs.astype(BF16)
        inner = jnp.sum(grad_probs * probs, axis=0, keepdims=True)
        grad_scores = (probs * (grad_probs - inner)).astype(BF16)
        gv.append(dot(da, rounded, (1, 1)))
        gk.append(dot(q, grad_scores, (1, 1)))
        gq.append(dot(k, grad_scores, (1, 0)) * SCALE)
    return [jnp.concatenate(g, axis=0) for g in (gq, gk, gv)]


def gated_half(me, d, ga, gb, mod, rows):
    rows[core_of(me, d), :] = (mod[2, 0:1, :] * ga[...].astype(F32)).astype(BF16)
    rows[core_of(me, d ^ 1), :] = (mod[2, 0:1, :] * gb[...].astype(F32)).astype(BF16)
    return rows[...]


def spatial_backward_own(
    me_ref, g0, g1, q_r, k_r, v_r, mod, wo, gq_o, gk_o, gv_o, rows
):
    me = me_ref[0]
    gated = gated_half(me, 0, g0, g1, mod, rows)
    grad_att = dot(wo[...], gated, (1, 1)).astype(BF16)
    gq, gk, gv = backward_half(q_r[:, half_of(me, 0)], grad_att, k_r, v_r)
    gq_o[...] = gq.astype(BF16)
    gk_o[...] = gk
    gv_o[...] = gv


def norm_sums(part, normed, inverse, gains, uw, start):
    n = part.shape[1]
    grad = part.astype(F32)
    before = normed.astype(F32)
    if inverse is not None:
        before = (before * (1.0 / gains)).reshape(PER, HEAD, n) * (1.0 / inverse)
        before = before.reshape(PART, n)
    shift, scale = uw[start : start + PART, 0:1], uw[start : start + PART, 3:4]
    first = jnp.sum(grad * scale, axis=0, keepdims=True)
    return first, jnp.sum(grad * (before - shift), axis=0, keepdims=True)


def spatial_backward_far(
    me_ref, g2, g3, q_r, k_r, v_r, st, gq_r, gk_r, gv_r, mod, gains, uw_r, wo, wn,
    p2, p3, stacked_o, rs_o, rows, gq_s, square,
):
    me = me_ref[0]
    gated = gated_half(me, 2, g2, g3, mod, rows)
    grad_att = dot(wo[...], gated, (1, 1)).astype(BF16)
    gq, gk, gv = backward_half(q_r[:, half_of(me, 1)], grad_att, k_r, v_r)
    gain_q, gain_k = gain_columns(gains, 0, square)
    gq_s[:, half_of(me, 0)] = gq_r[...]
    gq_s[:, half_of(me, 1)] = gq.astype(BF16)
    gk = ((gk + gk_r[...]) * SCALE).astype(BF16)
    inv_q = st[0:4, :].reshape(PER, 1, ROWS)
    inv_k = st[4:8, :].reshape(PER, 1, ROWS)
    stacked_o[:PART, :] = head_back_t(gq_s[...], q_r[...], inv_q, gain_q)
    stacked_o[PART : 2 * PART, :] = head_back_t(gk, k_r[...], inv_k, gain_k)
    stacked_o[2 * PART :, :] = (gv + gv_r[...]).astype(BF16)
    stacked = stacked_o[...]
    turned = wn
    for d, partial in ((3, p3), (2, p2)):
        partial[...] = dot(turned[part_of(me, d), :], stacked, (1, 0)).astype(BF16)
    uw = uw_r[...].T
    sums = [
        norm_sums(stacked[:PART], q_r[...], inv_q, gain_q, uw, 0),
        norm_sums(stacked[PART : 2 * PART], k_r[...], inv_k, gain_k, uw, PART),
        norm_sums(stacked[2 * PART :], v_r[...], None, None, uw, 2 * PART),
    ]
    rs_o[...] = jnp.zeros_like(rs_o)
    rs_o[0:1, :] = sums[0][0] + sums[1][0] + sums[2][0]
    rs_o[1:2, :] = sums[0][1] + sums[1][1] + sums[2][1]


def spatial_backward_last(me_ref, stacked_r, g0, g1, g2, g3, wn, p0, p1a, p1b, gown, rows):
    me = me_ref[0]
    stacked = stacked_r[...]
    turned = wn
    part = dot(turned[part_of(me, 1), :], stacked, (1, 0)).astype(BF16)
    p1a[...] = part[: PART // 2]
    p1b[...] = part[PART // 2 :]
    p0[...] = dot(turned[part_of(me, 0), :], stacked, (1, 0)).astype(BF16)
    for d, g in enumerate((g0, g1, g2, g3)):
        rows[...] = g[...].astype(F32).T
        gown[:, own_of(me, d)] = rows[part_of(me, 0), :].astype(BF16)


def spatial_finish(me_ref, p0, m1a, m1b, o2, rs, more, st, x0, gown, mod, out_o, lines, modc):
    modc[...] = turned_lines(mod, lines)
    m1 = jnp.concatenate([m1a[...], m1b[...]], axis=0)
    grad = p0[...].astype(F32) + m1.astype(F32) + o2[...].astype(F32)
    inverse = st[9:10, :]
    scaled = grad * (1.0 + modc[part_of(me_ref[0], 0), 1:2])
    centred = (x0[...].astype(F32) - st[8:9, :]) * inverse
    first = (rs[0:1, :] + more[0:1, :]) * (1.0 / WIDE)
    second = (rs[1:2, :] + more[1:2, :]) * (1.0 / WIDE)
    out_o[...] = (gown[...].astype(F32) + inverse * (scaled - first - centred * second)).astype(BF16)


def split_columns(me_ref, columns, c0, c1, c23):
    me = me_ref[0]
    c0[...] = columns[:, own_of(me, 0)]
    c1[...] = columns[:, own_of(me, 1)]
    c23[:PART, :] = columns[:, own_of(me, 2)]
    c23[PART:, :] = columns[:, own_of(me, 3)]


def place_columns(me_ref, c0, c1, c2, c3, out_o):
    me = me_ref[0]
    for d, c in enumerate((c0[...], c1[...], c2[:PART, :], c3[PART:, :])):
        out_o[:, own_of(me, d)] = c


def gather_rows(me_ref, c0, c1, c2, c3, wt, mod, rows_o, wn_o, uw_o, cs, lines):
    me = me_ref[0]
    weights = wt[...].reshape(3 * PART, WIDE)
    wn_o[...] = weights.T
    uw_o[...] = dot(weights, turned_lines(mod, lines).astype(BF16), (1, 0)).T
    for d, c in enumerate((c0[...], c1[...], c2[:PART, :], c3[PART:, :])):
        cs[part_of(me, d), :] = c.astype(F32)
    rows_o[...] = cs[...].T.astype(BF16)


def split_rows(me_ref, rows, c0, c1, c23, cs):
    me = me_ref[0]
    cs[...] = rows[...].astype(F32).T
    c0[...] = cs[part_of(me, 0), :].astype(BF16)
    c1[...] = cs[part_of(me, 1), :].astype(BF16)
    c23[:PART, :] = cs[part_of(me, 2), :].astype(BF16)
    c23[PART:, :] = cs[part_of(me, 3), :].astype(BF16)


def swap(values, d):
    return lax.ppermute(values, "head", [(i, i ^ d) for i in range(4)])


def exchange(parts):
    mine, mate, both = parts
    far = swap(both, 2)
    return [mine, swap(mate, 1), far, swap(far, 1)]


def across_seq(one, two):
    rows = jnp.concatenate([one, two], axis=1).reshape(64, 2, 2 * WIDE)
    moved = lax.all_to_all(rows, "seq", split_axis=0, concat_axis=0, tiled=True)
    return moved


def from_neighbour(chunk, d):
    index = [(s, h) for s in range(64) for h in range(4)]
    near = [(s * 4 + h, (s ^ 4) * 4 + (h ^ d)) for s, h in index]
    return lax.ppermute(chunk, ("seq", "head"), near)


def round_x(chunk, d):
    return lax.ppermute(chunk, "seq", [(s // 4 * 4 + (s + d) % 4, s) for s in range(64)])


def on_device(tokens, cotangent, qkv_weight, out_weight, modulation, head_gains):
    me = lax.axis_index("head")
    mine = me.astype(jnp.int32).reshape(1)
    at = (lax.axis_index("seq") & 3).astype(jnp.int32)
    wt = jnp.transpose(qkv_weight, (0, 2, 3, 1))
    mod = jnp.transpose(modulation, (1, 0, 2))
    row = out((OWN, WIDE))
    col = out((PART, ROWS))
    piece = out((PART, OWN))
    square = pltpu.VMEM((8, 128), F32)

    x0 = tokens.T
    x2 = swap(x0, 2)
    x1 = swap(x0, 1)
    pieces = [piece, piece, out((2 * PART, OWN))]
    parts = list(call(split_columns, pieces, [mine, cotangent.T], smem=1))
    weights = [wt[0], wt[1], out_weight[0], out_weight[1]]
    x2, weights, parts[0] = lax.optimization_barrier((x2, weights, parts[0]))
    wt_s, wt_t, wo_s, wo_t = weights
    x3 = swap(x2, 1)
    parts = exchange(parts)
    query, key, value, stats, p0, p1, p2, p3, xrow = call(
        spatial_forward,
        [col] * 3 + [out((16, ROWS), F32)] + [row] * 5,
        [mine, x0, x1, x2, x3, mod, head_gains, wt_s, wo_s],
        [pltpu.VMEM((WIDE, 8), F32), pltpu.VMEM((WIDE, ROWS), BF16),
         pltpu.VMEM((ROWS, WIDE), BF16), pltpu.VMEM((8, WIDE), F32), square],
        smem=1, wide=True,
    )
    m3, parts[2], parts[3] = lax.optimization_barrier((swap(p3, 1), parts[2], parts[3]))
    m1 = swap(p1, 1)
    chip = (p2.astype(F32) + m3.astype(F32)).astype(BF16)
    far = swap(chip, 2)
    cot0, wn, uw = call(
        gather_rows, [row, out((WIDE, 3 * PART)), out((8, 3 * PART), F32)],
        [mine, *parts, wt_s, mod],
        [pltpu.VMEM((WIDE, OWN), F32), pltpu.VMEM((8, WIDE), F32)], smem=1, wide=True, behind=[chip],
    )

    chunks = [lax.select_n(at ^ d, wt_t[0], wt_t[1], wt_t[2], wo_t) for d in (0, 2)]
    chunks, far = lax.optimization_barrier((chunks, far))
    near = swap(from_neighbour(chunks[0], 3), 1)
    others = [near, round_x(near, 1), from_neighbour(chunks[1], 2), round_x(near, 3)]

    branch = p0.astype(F32) + m1.astype(F32) + far.astype(F32)
    middle = (xrow.astype(F32) + modulation[0, 2][None] * branch).astype(BF16)

    tc0 = across_seq(middle, cot0).reshape(OWN, 2 * WIDE)
    tc1 = swap(tc0, 1)
    gn, br, normed, gated = call(
        temporal_own, [out((2 * OWN, WIDE))] * 4,
        [tc0, tc1, mod, head_gains, wt_t, wo_t],
        [square],
    )
    gn0, gn1, op0, op1 = call(
        temporal_far,
        [out((OWN, WIDE), F32), row, out((OWN, WIDE), F32), row],
        [at.reshape(1), normed, gated, gn, br, head_gains, *others],
        [pltpu.VMEM((4 * PART, WIDE), BF16), square],
        smem=1,
    )
    gn1, op1 = swap(gn1, 1), swap(op1, 1)
    grad_middle, mixed_rows = call(
        temporal_finish, [row] * 2, [tc0, gn0, gn1, op0, op1, mod]
    )

    moved = across_seq(grad_middle, mixed_rows)
    g0 = moved[:, :, :WIDE].reshape(OWN, WIDE)
    mixed_rows = moved[:, :, WIDE:].reshape(OWN, WIDE)
    g2 = swap(g0, 2)
    g1 = swap(g0, 1)
    gq, gk, gv = call(
        spatial_backward_own,
        [out((PART, 2 * OWN)), out((PART, ROWS), F32), out((PART, ROWS), F32)],
        [mine, g0, g1, query, key, value, mod, wo_s],
        [pltpu.VMEM((2 * OWN, WIDE), BF16)],
        smem=1,
    )
    parts = call(split_rows, pieces, [mine, mixed_rows], [pltpu.VMEM((WIDE, OWN), F32)], smem=1)
    g2, gq, *parts = lax.optimization_barrier((g2, gq, *parts))
    g3 = swap(g2, 1)
    parts = exchange(parts)
    p2, p3, stacked, sums = call(
        spatial_backward_far,
        [col, col, out((3 * PART, ROWS)), out((8, ROWS), F32)],
        [mine, g2, g3, query, key, value, stats, gq, gk, gv, mod, head_gains, uw, wo_s,
         wn],
        [pltpu.VMEM((2 * OWN, WIDE), BF16), pltpu.VMEM((PART, ROWS), BF16), square],
        smem=1,
    )
    m3, other, parts[2], parts[3] = lax.optimization_barrier(
        (swap(p3, 1), swap(sums, 1), parts[2], parts[3])
    )
    chip = (p2.astype(F32) + m3.astype(F32)).astype(BF16)
    far = swap(chip, 2)
    sums = sums + other
    more = swap(sums, 2)
    p0, p1a, p1b, gown = call(
        spatial_backward_last,
        [col, out((PART // 2, ROWS)), out((PART // 2, ROWS)), col],
        [mine, stacked, g0, g1, g2, g3, wn],
        [pltpu.VMEM((WIDE, OWN), F32)],
        smem=1,
        behind=[chip],
    )
    m1a, m1b = swap(p1a, 1), swap(p1b, 1)

    (mixed,) = call(place_columns, [col], [mine, *parts], smem=1, behind=[p0])

    (grad,) = call(
        spatial_finish, [col], [mine, p0, m1a, m1b, far, sums, more, stats, x0, gown, mod],
        [pltpu.VMEM((8, WIDE), F32), pltpu.VMEM((WIDE, 8), F32)],
        smem=1,
    )
    return (mixed.T, grad.T)


def solution(mesh):
    in_specs = (
        P("seq", "head"),
        P("seq", "head"),
        P(None, None, None, "head"),
        P(None, "head", None),
        P(),
        P(),
    )
    out_specs = (P("seq", "head"), P("seq", "head"))
    return jax.shard_map(
        on_device, mesh=mesh, in_specs=in_specs, out_specs=out_specs, check_vma=False
    )
```
